32 devices in a mesh: dp: 8 (over y, x, core), tensor: 4 (over z).
Axes of the slice: x: 2, y: 2, z: 4, core: 2. Of those that a mesh axis runs over, the one named last changes fastest.
Arguments:
- inputs: bfloat16 [16384, 384], P(('dp', 'tensor')), may hold values from -6 to 6
- lengths: int32 [16], P('dp'), may hold values from 256 to 1024, as said below
- expert_ids: int32 [16384, 2], P('dp'), may hold values from 0 to 7, all different within a row; in each aligned block of 2048 rows (0 to 2047, 2048 to 4095, ...) at most 1024 rows name the same one
- gain_attn: bfloat16 [384], replicated, may hold values from 0.5 to 1.5
- w_query: bfloat16 [384, 384], P(None, 'tensor'), may hold values from -0.3125 to 0.3125
- w_key: bfloat16 [384, 384], P(None, 'tensor'), may hold values from -0.3125 to 0.3125
- w_value: bfloat16 [384, 384], P(None, 'tensor'), may hold values from -0.3125 to 0.3125
- w_out: bfloat16 [384, 384], P('tensor'), may hold values from -1.5 to 1.5
- gain_ffn: bfloat16 [384], replicated, may hold values from 0.5 to 1.5
- router: bfloat16 [384, 8], replicated, may hold values from -0.21875 to 0.21875
- shared_gate_vec: bfloat16 [384], replicated, may hold values from -0.3125 to 0.3125
- exp_gate: bfloat16 [8, 384, 768], P(None, None, 'tensor'), may hold values from -0.3125 to 0.3125
- exp_up: bfloat16 [8, 384, 768], P(None, None, 'tensor'), may hold values from -0.3125 to 0.3125
- exp_down: bfloat16 [8, 768, 384], P(None, 'tensor'), may hold values from -0.875 to 0.875
- sh_gate: bfloat16 [384, 1536], P(None, 'tensor'), may hold values from -0.3125 to 0.3125
- sh_up: bfloat16 [384, 1536], P(None, 'tensor'), may hold values from -0.3125 to 0.3125
- sh_down: bfloat16 [1536, 384], P('tensor'), may hold values from -0.3125 to 0.3125
- cotangent: bfloat16 [16384, 384], P(('dp', 'tensor')), may hold values from -6 to 6
Outputs:
- output: bfloat16 [16384, 384], P(('dp', 'tensor'))
- d_inputs: float32 [16384, 384], P(('dp', 'tensor'))
- d_gain_attn: float32 [384], replicated
- d_w_query: float32 [384, 384], P(None, 'tensor')
- d_w_key: float32 [384, 384], P(None, 'tensor')
- d_w_value: float32 [384, 384], P(None, 'tensor')
- d_w_out: float32 [384, 384], P('tensor')
- d_gain_ffn: float32 [384], replicated
- d_router: float32 [384, 8], replicated
- d_shared_gate_vec: float32 [384], replicated
- d_exp_gate: float32 [8, 384, 768], P(None, None, 'tensor')
- d_exp_up: float32 [8, 384, 768], P(None, None, 'tensor')
- d_exp_down: float32 [8, 768, 384], P(None, 'tensor')
- d_sh_gate: float32 [384, 1536], P(None, 'tensor')
- d_sh_up: float32 [384, 1536], P(None, 'tensor')
- d_sh_down: float32 [1536, 384], P('tensor')
The draws below stay inside these ranges and needn't reach their ends.
Inputs may be any that keep to these rules, and one draw needn't show every extreme that they name: `lengths`: in every draw some series has all 1024 points valid. `expert_ids`: each row names two different experts; within the 2048 rows of one dp group (aligned blocks) no expert is named by more than 1024 rows.
All inputs are finite; a program needn't handle non-finite values.
Results may differ from the reference program's by a relative error of at most 0.022.
Values may be sent and summed in bfloat16 or wider, within the bound.
A program may use at most 192 MiB of HBM per device.

```python
import math
import jax
import jax.numpy as jnp
import numpy as np
from jax import lax

D = 384
HEADS = 12
HEAD_DIM = 32
FF = 1536
EFF = 768
EXPERTS = 8
SEQS = 2
LEN = 1024
TOK_GROUP = 2048
TOKENS = 16384
SEQUENCES = 16
CAP = 1024
N_DP = 8


def draw_lengths(key, part):
    key = jax.random.fold_in(key, 3)
    first_key, second_key = jax.random.split(key)
    values = jax.random.randint(first_key, (SEQUENCES,), LEN // 4, LEN + 1)
    full_one = jax.random.randint(second_key, (), 0, SEQUENCES)
    return jnp.where(jnp.arange(SEQUENCES) == full_one, LEN, values).astype(jnp.int32)


def block_levels(key, dims, cuts, smallest, largest):
    def one(dim, blocks):
        steps = jax.random.uniform(jax.random.fold_in(jax.random.fold_in(key, 6), dim), (blocks,), jnp.float32, smallest / len(cuts), largest / len(cuts))
        return jnp.repeat(jnp.exp(steps), dims[dim] // blocks).reshape((-1,) + (1,) * (len(dims) - dim - 1))

    level = one(*cuts[0])
    for cut in cuts[1:]:
        level = level * one(*cut)
    return level


def routed_block(stream_key, own, number, rows, number_of, top, most, skew):
    order = jax.random.permutation(stream_key, number_of)
    packed, common = shares(number_of, rows * top, most, skew, True), shares(number_of, rows * top, most, skew, False)
    places = jnp.arange(number_of)

    def named(tallies, turn):
        used = int((tallies > 0).sum())
        fixed = max(1, used // 4)
        passed = fixed + (places - fixed + turn * (used - fixed)) % max(1, number_of - fixed)
        return jnp.zeros((number_of,), jnp.int32).at[order[jnp.where(places < fixed, places, passed)]].set(jnp.asarray(tallies, jnp.int32))

    tallies = jnp.where(number % 4 == 0, named(packed, number // 4), named(common, number - number // 4 - 1))
    mixed = jax.random.permutation(jax.random.fold_in(own, 3), number_of)
    donor, sink = mixed[0:number_of // 2 * 2:2], mixed[1:number_of // 2 * 2:2]
    slack = jnp.minimum(tallies[donor] - 1, most - tallies[sink]) // 2
    slack = jnp.where((donor == order[0]) | (sink == order[0]) | (tallies[sink] == 0), 0, jnp.maximum(slack, 0))
    passed = jax.random.randint(jax.random.fold_in(own, 4), (number_of // 2,), 0, 1 << 20) % (slack + 1)
    tallies = tallies.at[donor].add(-passed).at[sink].add(passed)
    items = jnp.searchsorted(jnp.cumsum(tallies), jnp.arange(rows * top), side="right").astype(jnp.int32)
    grid = items.reshape(top, rows).T
    grid = grid[jax.random.permutation(jax.random.fold_in(own, 1), rows)]
    turn = jax.random.randint(jax.random.fold_in(own, 2), (rows, 1), 0, top)
    return jnp.take_along_axis(grid, (jnp.arange(top)[None, :] + turn) % top, axis=1)


def shares(number_of, total, reach, slope, full):
    loads = [(1 << 20) // math.isqrt(rank ** slope) + 1 for rank in range(1, number_of + 1)]
    largest = reach if full else min(reach, max(-(-total // number_of), total * loads[0] // sum(loads)))
    least = 1 if total - largest >= number_of - 1 else 0
    counts, surplus = [largest] + [least] * (number_of - 1), total - largest - least * (number_of - 1)
    while surplus > 0:
        candidates = [i for i in range(1, number_of) if counts[i] < largest] or [i for i in range(1, number_of) if counts[i] < reach]
        mass, remaining = sum([loads[i] for i in candidates]), surplus
        for i in candidates:
            addition = min(reach - counts[i], max(1, remaining * loads[i] // mass), surplus)
            counts[i] = counts[i] + addition
            surplus = surplus - addition
    return np.array(counts)


def centred(stream_key, extent, spread, most, cuts=(), kind=jnp.bfloat16):
    values = spread * jax.random.normal(stream_key, extent, jnp.float32)
    if cuts:
        values = values * block_levels(stream_key, extent, cuts, -0.22, 0.18)
    return jnp.clip(values, -most, most).astype(kind)


def setup_inputs(seed: int = 0) -> dict:
    key_list = jax.random.split(jax.random.key(seed), 19)
    inputs = centred(key_list[0], (TOKENS, D), 1.0, 6.0, ((0, 32),))
    lengths = draw_lengths(jax.random.fold_in(key_list[18], 71), 0)
    expert_ids_keys = jax.random.split(jax.random.fold_in(key_list[2], 1), TOKENS // TOK_GROUP)
    expert_ids_turns = jax.random.permutation(jax.random.fold_in(key_list[2], 3), TOKENS // TOK_GROUP)
    expert_ids = jax.vmap(lambda own, number: routed_block(jax.random.fold_in(key_list[2], 2), own, number, TOK_GROUP, EXPERTS, 2, CAP, 1))(expert_ids_keys, expert_ids_turns).reshape((TOKENS, 2))
    gain_attn = jnp.clip(1.0 + 0.1 * jax.random.normal(key_list[3], (D,), jnp.float32), 0.5, 1.5).astype(jnp.bfloat16)
    w_query = centred(key_list[4], (D, D), D ** -0.5, 0.3125, ((1, 4),))
    w_key = centred(key_list[5], (D, D), D ** -0.5, 0.3125, ((1, 4),))
    w_value = centred(key_list[6], (D, D), D ** -0.5, 0.3125, ((1, 4),))
    w_out = centred(key_list[7], (D, D), (HEAD_DIM // 2) ** -0.5, 1.5, ((0, 4),))
    gain_ffn = jnp.clip(1.0 + 0.1 * jax.random.normal(key_list[8], (D,), jnp.float32), 0.5, 1.5).astype(jnp.bfloat16)
    router = centred(key_list[9], (D, EXPERTS), (2 * D) ** -0.5, 0.21875)
    shared_gate_vec = centred(key_list[10], (D,), D ** -0.5, 0.3125)
    exp_gate = centred(key_list[11], (EXPERTS, D, EFF), D ** -0.5, 0.3125, ((2, 4),))
    exp_up = centred(key_list[12], (EXPERTS, D, EFF), D ** -0.5, 0.3125, ((2, 4),))
    exp_down = centred(key_list[13], (EXPERTS, EFF, D), (EFF // 16) ** -0.5, 0.875, ((1, 4),))
    sh_gate = centred(key_list[14], (D, FF), D ** -0.5, 0.3125, ((1, 4),))
    sh_up = centred(key_list[15], (D, FF), D ** -0.5, 0.3125, ((1, 4),))
    sh_down = centred(key_list[16], (FF, D), (FF // 4) ** -0.5, 0.3125, ((0, 4),))
    cotangent = centred(key_list[17], (TOKENS, D), 1.0, 6.0, ((0, 32),))
    return dict(inputs=inputs, lengths=lengths, expert_ids=expert_ids, gain_attn=gain_attn, w_query=w_query, w_key=w_key, w_value=w_value, w_out=w_out, gain_ffn=gain_ffn, router=router, shared_gate_vec=shared_gate_vec, exp_gate=exp_gate, exp_up=exp_up, exp_down=exp_down, sh_gate=sh_gate, sh_up=sh_up, sh_down=sh_down, cotangent=cotangent)


HIGH = lax.Precision.HIGHEST

@jax.custom_vjp
def low(v):
    return lax.optimization_barrier(v.astype(jnp.bfloat16)).astype(jnp.float32)

@jax.custom_vjp
def low_back(v):
    return v

def low_keep(v):
    return (low(v), None)

def low_pass(kept, grad):
    return (grad,)

def back_keep(v):
    return (v, None)

def back_low(kept, grad):
    return (low(grad),)
low.defvjp(low_keep, low_pass)
low_back.defvjp(back_keep, back_low)

def mix(left, right):
    return jnp.dot(left, right, precision=HIGH, preferred_element_type=jnp.float32)

def norm_rows(values, gain):
    factor = lax.rsqrt(lax.optimization_barrier(jnp.mean(values * values, axis=-1, keepdims=True)) + 1e-06)
    return values * factor * gain

def silu(values):
    return values * lax.logistic(values)

def rotary_tables(length, head_dim):
    half = head_dim // 2
    freqs = 10000.0 ** (-jnp.arange(half, dtype=jnp.float32) / half)
    angles = jnp.arange(length, dtype=jnp.float32)[:, None] * freqs[None, :]
    return (jnp.cos(angles), jnp.sin(angles))

def rotate(values, cosine, sine):
    half = values.shape[-1] // 2
    first = values[..., :half]
    second = values[..., half:]
    cos_wide = cosine[:, None, :]
    sin_wide = sine[:, None, :]
    return jnp.concatenate([first * cos_wide - second * sin_wide, first * sin_wide + second * cos_wide], axis=-1)

def allowed_keys(length, count):
    position = jnp.arange(count, dtype=jnp.int32)
    return (position[None, :] <= position[:, None]) & (position[None, :] < length)

def route_slots(expert_ids, experts, capacity):
    flat_ids = expert_ids.reshape(-1).astype(jnp.int32)
    onehot = (flat_ids[:, None] == jnp.arange(experts, dtype=jnp.int32)[None, :]).astype(jnp.int32)
    ranks = (lax.optimization_barrier(jnp.sum(jnp.cumsum(onehot, axis=0) * onehot, axis=1)) - 1).astype(jnp.int32)
    slots = (flat_ids * capacity + ranks).astype(jnp.int32)
    owners = (jnp.arange(flat_ids.shape[0], dtype=jnp.int32) // expert_ids.shape[1]).astype(jnp.int32)
    slot_tokens = jnp.zeros((experts * capacity,), jnp.int32).at[slots].set(owners)
    return (slot_tokens, slots.reshape(expert_ids.shape))

def forward_group(x_rows, seq_lengths, expert_choice, params):
    gain_attn, w_query, w_key, w_value, w_out, gain_ffn, router, shared_vec, exp_gate, exp_up, exp_down, sh_gate, sh_up, sh_down = params
    cosine, sine = rotary_tables(LEN, HEAD_DIM)
    norm_attn = low(norm_rows(x_rows, gain_attn))
    sequences = norm_attn.reshape(SEQS, LEN, D)

    def attend(items):
        rows_seq, length = items
        query_pre = low_back(mix(rows_seq, w_query)).reshape(LEN, HEADS, HEAD_DIM)
        key_pre = low_back(mix(rows_seq, w_key)).reshape(LEN, HEADS, HEAD_DIM)
        value_all = low(low_back(mix(rows_seq, w_value))).reshape(LEN, HEADS, HEAD_DIM)
        queries = low(rotate(query_pre, cosine, sine))
        keys = low(rotate(key_pre, cosine, sine))
        scores = low_back(jnp.einsum('qhd,khd->hqk', queries, keys, precision=HIGH) * HEAD_DIM ** (-0.5))
        scores = jnp.where(allowed_keys(length, LEN)[None], scores, -1e+30)
        row_max = lax.optimization_barrier(jnp.max(scores, axis=-1, keepdims=True))
        weights = jnp.exp(scores - row_max)
        probs = weights / lax.optimization_barrier(jnp.sum(weights, axis=-1, keepdims=True))
        mixed = jnp.einsum('hqk,khd->qhd', low(probs), value_all, precision=HIGH)
        return low(low_back(mixed)).reshape(LEN, D)
    heads_out = lax.map(jax.checkpoint(attend), (sequences, seq_lengths)).reshape(TOK_GROUP, D)
    middle = x_rows + low_back(mix(heads_out, w_out))
    norm_ffn = low(norm_rows(middle, gain_ffn))
    logits = mix(norm_ffn, router)
    expo = jnp.exp(logits - lax.optimization_barrier(jnp.max(logits, axis=-1, keepdims=True)))
    route = expo / lax.optimization_barrier(jnp.sum(expo, axis=-1, keepdims=True))
    chosen = (expert_choice[:, :, None] == jnp.arange(EXPERTS, dtype=jnp.int32)[None, None, :]).astype(jnp.float32)
    gates = lax.optimization_barrier(jnp.sum(route[:, None, :] * chosen, axis=-1))
    shared_scale = lax.logistic(mix(norm_ffn, shared_vec[:, None]))
    slot_tokens, slots = route_slots(expert_choice, EXPERTS, CAP)
    expert_in = norm_ffn[slot_tokens].reshape(EXPERTS, CAP, D)
    gate_pre = low_back(jnp.einsum('ecd,edf->ecf', expert_in, exp_gate, precision=HIGH))
    up_pre = low_back(jnp.einsum('ecd,edf->ecf', expert_in, exp_up, precision=HIGH))
    hidden = low(silu(gate_pre) * up_pre)
    expert_out = low_back(jnp.einsum('ecf,efd->ecd', hidden, exp_down, precision=HIGH)).reshape(EXPERTS * CAP, D)
    routed = lax.optimization_barrier(jnp.sum(gates[:, :, None] * expert_out[slots], axis=1))
    sh_gate_pre = low_back(mix(norm_ffn, sh_gate))
    sh_up_pre = low_back(mix(norm_ffn, sh_up))
    sh_hidden = low(silu(sh_gate_pre) * sh_up_pre)
    sh_result = low_back(mix(sh_hidden, sh_down))
    return middle + low_back(routed + shared_scale * sh_result)

def reference(inputs, lengths, expert_ids, gain_attn, w_query, w_key, w_value, w_out, gain_ffn, router, shared_gate_vec, exp_gate, exp_up, exp_down, sh_gate, sh_up, sh_down, cotangent):
    params = tuple((item_one.astype(jnp.float32) for item_one in (gain_attn, w_query, w_key, w_value, w_out, gain_ffn, router, shared_gate_vec, exp_gate, exp_up, exp_down, sh_gate, sh_up, sh_down)))

    def forward(x_all, *weights):

        def one_group(items):
            return forward_group(items[0], items[1], items[2], weights)
        grouped = (x_all.reshape(N_DP, TOK_GROUP, D), lengths.reshape(N_DP, SEQS), expert_ids.reshape(N_DP, TOK_GROUP, 2))
        return lax.map(jax.checkpoint(one_group), grouped).reshape(TOKENS, D)
    result, pull_back = jax.vjp(forward, inputs.astype(jnp.float32), *params)
    grads = pull_back(cotangent.astype(jnp.float32))
    return (result.astype(jnp.bfloat16), grads[0], grads[1], grads[2], grads[3], grads[4], grads[5], grads[6], grads[7], grads[8], grads[9], grads[10], grads[11], grads[12], grads[13], grads[14])
```

```python
import functools

import jax
import jax.numpy as jnp
import numpy as np
from jax import lax
from jax.experimental import pallas as pl
from jax.experimental.pallas import tpu as pltpu
from jax.sharding import PartitionSpec as P

HD = 32
LEN = 1024
NT = 4
LANES = 128
QB = 256
BF = jnp.bfloat16
F32 = jnp.float32
MESH = pl.DeviceIdType.MESH
NEG = -1e30
SCALE = HD**-0.5
LOG2E = 1.4426950408889634
LN2 = 0.6931471805599453


def nn(a, b):
    return lax.dot_general(a, b, (((1,), (0,)), ((), ())), preferred_element_type=F32)


def nt(a, b):
    return lax.dot_general(a, b, (((1,), (1,)), ((), ())), preferred_element_type=F32)


def inv_rms(v):
    return lax.rsqrt(jnp.mean(v * v, axis=-1, keepdims=True) + 1e-06)


def rms_back(v, grad, gain):
    r = inv_rms(v)
    u = v * r
    g = grad * gain
    return r * (g - u * jnp.mean(g * u, axis=-1, keepdims=True)), grad * u


def up16(n):
    return -(-n // 16) * 16


class Plan:
    def __init__(self, nd, rows, width, experts, eff, ff):
        self.nd, self.R, self.W = nd, rows, width
        self.G = NT * rows
        self.NG = width // LANES
        self.HC = width // NT
        self.B = 2 * eff
        self.EB = experts // 2
        self.NB = self.EB + 1
        assert ff == self.B == width and LEN == 2 * rows
        self.E, self.eff, self.ff = experts, eff, ff
        self.share = min(4, nd)
        self.nc = nd // 2
        total = 3 * self.NB * width
        self.piece = up16(-(-total // nd))
        self.half = self.nc * self.piece
        self.total = total
        self.flat = 2 * self.half
        self.hp = 2 * self.HC
        self.pr = max(16, self.hp // self.nc)
        self.owners = self.hp // self.pr
        assert self.owners * self.pr == self.hp and self.pr % 16 == 0 and self.owners <= self.nc


class Sems:
    def __init__(self):
        self.n = 0

    def take(self, n):
        base = self.n
        self.n += n
        return base


def sem_plan(p):
    s, names = Sems(), {}
    names["w"] = s.take(3 * (4 // p.share))
    names["f"] = s.take(3 * (4 // p.share) * max(p.share - 1, 1))
    names["x"] = s.take(1)
    names["c"] = s.take(3)
    names["n"] = s.take(6)
    names["dx"] = s.take(3)
    names["o"] = s.take(3)
    names["h1"] = s.take(1)
    names["h2"] = s.take(max(p.nc - 1, 1))
    names["h3"] = s.take(max(p.nc - 1, 1))
    names["h4"] = s.take(p.nc)
    names["px"] = s.take(1)
    names["f1"] = s.take(1)
    names["f2"] = s.take(max(p.nc - 1, 1))
    names["f3"] = s.take(3)
    names["f4"] = s.take(p.nd - 1)
    names["s1"] = s.take(p.nd - 1)
    names["s2"] = s.take(3)
    return s.n, names


def kernel(
    p,
    names,
    len_ref,
    ids_ref,
    gains,
    watt,
    rext,
    x_hbm,
    cot_hbm,
    eg_hbm,
    eu_hbm,
    ed_hbm,
    sg_hbm,
    su_hbm,
    sd_hbm,
    cosk,
    sink,
    cost,
    sint,
    out_ref,
    din_ref,
    res_hbm,
    att_ref,
    sm_ref,
    send,
    recv,
    lsem,
    wfull,
    xs,
    xn,
    cotg,
    normg,
    wg,
    wu,
    wd,
    qT,
    qN,
    kN,
    kT,
    vN,
    vT,
    oT,
    lse,
    bias,
    mid,
    dx_own,
    out_own,
    dxr,
    outr,
    acc,
    drext,
    stage,
    h1,
    h2,
    res,
    agrad,
    dON,
    dOT,
    delta,
    pxs,
    pxr,
    A,
    f1,
    f2,
    fD,
    f3,
    att,
    smr,
    smz,
):
    R, W, NG = p.R, p.W, p.NG
    dp, z = lax.axis_index("dp"), lax.axis_index("tensor")
    zlo = lax.rem(z, 2)
    zk = [z, z + 1 - 2 * zlo, lax.rem(z + 2, NT), NT - 1 - z]
    core = lax.rem(dp, 2)
    chip = lax.div(dp, 2)
    mate = dp + 1 - 2 * core
    half_own = zlo

    def remote(src, dst, kind, i, dev):
        j = names[kind] + i
        return pltpu.make_async_remote_copy(
            src_ref=src, dst_ref=dst, send_sem=send.at[j], recv_sem=recv.at[j], device_id=dev, device_id_type=MESH
        )

    def to_z(k):
        return (dp, zk[k])

    def chip_at(j):
        return lax.rem(chip + j, p.nc)

    def on_chip(j):
        return (2 * chip_at(j) + core, z)

    V = pltpu.VMEM
    x_in, cot_in = xs.at[half_own], cotg.at[z]
    loads = [
        pltpu.make_async_copy(src, dst, lsem.at[i])
        for i, (src, dst) in enumerate(
            [
                (x_hbm, x_in),
                (cot_hbm, cot_in),
                (eg_hbm, wg.at[: p.EB]),
                (eu_hbm, wu.at[: p.EB]),
                (ed_hbm, wd.at[: p.EB]),
                (sg_hbm, agrad.at[:W]),
                (su_hbm, pxs.at[:W]),
                (sd_hbm, wd.at[p.EB]),
            ]
        )
    ]
    for c in loads:
        c.start()
    barrier = pltpu.get_barrier_semaphore()
    for k in (1, 2, 3):
        pl.semaphore_signal(barrier, inc=1, device_id=to_z(k), device_id_type=MESH)

    def greet(j, carry):
        pl.semaphore_signal(barrier, inc=1, device_id=(lax.rem(dp + j, p.nd), z), device_id_type=MESH)
        return carry

    lax.fori_loop(1, p.nd, greet, 0)
    pl.semaphore_wait(barrier, 3 + p.nd - 1)

    S = p.share
    member = lax.rem(dp, S)
    base = dp - member
    own_cols = pl.ds(pl.multiple_of(z * p.HC, 32), p.HC)

    def cols_of(k):
        return pl.ds(pl.multiple_of(zk[k] * p.HC, 32), p.HC)

    def w_send(k, i):
        m = member + S * i
        return remote(watt.at[m], wfull.at[m, own_cols], "w", (k - 1) * (4 // S) + i, to_z(k))

    def w_recv(k, i):
        m = member + S * i
        return remote(watt.at[m], wfull.at[m, cols_of(k)], "w", (k - 1) * (4 // S) + i, to_z(k))

    def w_forward(k, i, j):
        m = member + S * i
        there = base + lax.rem(member + j, S)
        return remote(
            wfull.at[m, cols_of(k)],
            wfull.at[m, cols_of(k)],
            "f",
            ((k - 1) * (4 // S) + i) * (S - 1) + j - 1,
            (there, z),
        )

    x_copy = remote(x_in, x_in, "x", 0, to_z(1))
    for k in (1, 2, 3):
        for i in range(4 // S):
            w_send(k, i).start()
    loads[0].wait()
    x_copy.start()
    for m in range(4):
        wfull[m, own_cols] = watt[m]
    gain_attn, gain_ffn = gains[0:1], gains[1:2]

    def mask_rows(i, carry):
        key = lax.broadcasted_iota(jnp.int32, (QB, R), 0) + i * QB
        query = lax.broadcasted_iota(jnp.int32, (QB, R), 1) + half_own * R
        length = len_ref[lax.div(z, 2)]
        bias[pl.ds(pl.multiple_of(i * QB, QB), QB)] = jnp.where((key <= query) & (key < length), 0.0, NEG)
        return carry

    lax.fori_loop(0, LEN // QB, mask_rows, 0)
    for k in (1, 2, 3):
        for i in range(4 // S):
            w_recv(k, i).wait_recv()
            for j in range(1, S):
                w_forward(k, i, j).start()

    for c in loads[1:]:
        c.wait()
    wg[p.EB] = agrad[:W].T
    wu[p.EB] = pxs[:W].T
    x_copy.wait_recv()
    for k in (1, 2, 3):
        remote(cot_in, cot_in, "c", k - 1, to_z(k)).start()

    def norm_half(i, carry):
        v = xs[i].astype(F32)
        xn[pl.ds(pl.multiple_of(i * R, R), R)] = (v * inv_rms(v) * gain_attn).astype(BF)
        return carry

    lax.fori_loop(0, 2, norm_half, 0)
    for k in (1, 2, 3):
        for i in range(4 // S):
            for j in range(1, S):
                w_forward(k, i, j).wait_recv()

    own_pos = pl.ds(pl.multiple_of(half_own * R, R), R)
    lane = lax.broadcasted_iota(jnp.int32, (1, LANES), 1)
    low_half = lax.rem(lane, HD) < HD // 2

    def swap_halves(v):
        return jnp.where(low_half, pltpu.roll(v, LANES - HD // 2, 1), pltpu.roll(v, HD // 2, 1))

    q_pre = nt(wfull[0], xn[own_pos])
    cos_own, sin_own = cost[:, own_pos], sint[:, own_pos]
    for h in range(W // HD):
        a = q_pre[h * HD : h * HD + HD // 2]
        b = q_pre[h * HD + HD // 2 : (h + 1) * HD]
        qT[h * HD : h * HD + HD // 2] = ((a * cos_own - b * sin_own) * (SCALE * LOG2E)).astype(BF)
        qT[h * HD + HD // 2 : (h + 1) * HD] = ((a * sin_own + b * cos_own) * (SCALE * LOG2E)).astype(BF)

    def project(i, carry):
        rows = pl.ds(pl.multiple_of(i * QB, QB), QB)
        xb = xn[rows]
        k_pre = nt(xb, wfull[1])
        v_pre = nt(xb, wfull[2])
        c, s = cosk[rows], sink[rows]
        for g in range(NG):
            kg = k_pre[:, g * LANES : (g + 1) * LANES]
            kN[g, rows] = (kg * c + swap_halves(kg) * s).astype(BF)
            vN[g, rows] = v_pre[:, g * LANES : (g + 1) * LANES].astype(BF)
        return carry

    lax.fori_loop(0, LEN // QB, project, 0)
    for g in range(NG):
        rows = slice(g * LANES, (g + 1) * LANES)
        kT[rows] = kN[g].T
        vT[rows] = vN[g].T
        qN[g] = qT[rows].T

    head_row = lax.div(lax.broadcasted_iota(jnp.int32, (LANES, 1), 0), HD)
    head_lane = lax.div(lane, HD)
    HPG = LANES // HD

    def scores(g, h, qb):
        qg = qT[pl.ds(pl.multiple_of(g * LANES, LANES), LANES), qb * QB : (qb + 1) * QB]
        masked = jnp.where(head_row == h, qg, jnp.zeros_like(qg))
        return nn(kN[g], masked) + bias[:, qb * QB : (qb + 1) * QB]

    for qb in range(R // QB):
        cols = slice(qb * QB, (qb + 1) * QB)

        def heads(g, carry):
            for h in range(HPG):
                s = scores(g, h, qb)
                top = jnp.max(s, axis=0, keepdims=True)
                e = jnp.exp2(s - top)
                total = jnp.sum(e, axis=0, keepdims=True)
                at = pl.ds(pl.multiple_of(g * LANES + h * HD, HD), HD)
                o = nn(vT[at], e.astype(BF)) * (1.0 / total)
                oT[at, cols] = o.astype(BF)
                lse[pl.ds(g * HPG + h, 1), cols] = top + jnp.log(total) * LOG2E
            return carry

        lax.fori_loop(0, NG, heads, 0)
        rows = slice(qb * QB, (qb + 1) * QB)
        m = x_in[rows].astype(F32) + nn(oT[:, cols].T, wfull[3])
        mid[rows] = m
        normg[z, rows] = (m * inv_rms(m) * gain_ffn).astype(BF)
        for k in (1, 2, 3):
            remote(normg.at[z, rows], normg.at[z, rows], "n", (k - 1) * 2 + qb, to_z(k)).start()

    for k in (1, 2, 3):
        remote(cot_in, cot_in, "c", k - 1, to_z(k)).wait_recv()

    def zero_acc(i, carry):
        acc[pl.ds(pl.multiple_of(i * 16, 16), 16)] = jnp.zeros((16, W), F32)
        return carry

    lax.fori_loop(0, p.total // 16, zero_acc, 0)
    drext[...] = jnp.zeros_like(drext)
    zhi = lax.div(z, 2)

    def chunk_of(k):
        return 2 * lax.rem(zhi + lax.div(k, 2), 2) + lax.rem(zlo + lax.rem(k, 2), 2)

    def unit(C_s, G_s, RG_s, xT, gT, out_acc, dx_acc, k, carry):
        c = chunk_of(k)

        @pl.when(k > 0)
        def _():
            for b in range(R // QB):
                part = normg.at[c, b * QB : (b + 1) * QB]
                remote(part, part, "n", (k - 1) * 2 + b, (dp, c)).wait_recv()

        x = normg[c]
        xT[...] = x.T
        gT[...] = cotg[c].T
        logits = nn(x, rext[...])
        is_expert = lane < p.E
        lg = jnp.where(is_expert, logits, NEG)
        ex = jnp.exp(lg - jnp.max(lg, axis=-1, keepdims=True))
        route = ex / jnp.sum(ex, axis=-1, keepdims=True)
        at = pl.ds(pl.multiple_of(c * R, R), R)
        down = lax.broadcasted_iota(jnp.int32, (LANES, R), 0)
        named = (down == ids_ref[0:1, at]) | (down == ids_ref[1:2, at]) | ((down >= p.E) & (down < p.E + 2))
        chosen = jnp.where(named, 1.0, 0.0).T
        C_s[...] = chosen
        gate = jnp.where(is_expert, route, lax.logistic(logits)) * chosen
        G_s[...] = gate
        RG_s[...] = jnp.zeros_like(RG_s)
        out_acc[...] = jnp.zeros_like(out_acc)
        dx_acc[...] = jnp.zeros_like(dx_acc)

        def block(b, carry):
            xb, gb = normg[c], cotg[c]
            a = nt(xb, wg[b])
            u = nt(xb, wu[b])
            hg = nt(gb, wd[b])
            gates = G_s[...]
            first = jnp.sum(jnp.where(lane == 2 * b, gates, 0.0), axis=-1, keepdims=True)
            second = jnp.sum(jnp.where(lane == 2 * b + 1, gates, 0.0), axis=-1, keepdims=True)
            wide = lax.broadcasted_iota(jnp.int32, (1, p.B), 1) < p.eff
            gc = jnp.where(wide, first, second)
            sig = 0.5 * jnp.tanh(0.5 * a) + 0.5
            act = a * sig
            slope = sig + act - act * sig
            h = act * u
            prod = h * hg
            s0 = jnp.sum(jnp.where(wide, prod, 0.0), axis=-1, keepdims=True)
            s1 = jnp.sum(jnp.where(wide, 0.0, prod), axis=-1, keepdims=True)
            RG_s[...] += jnp.where(lane == 2 * b, s0, 0.0) + jnp.where(lane == 2 * b + 1, s1, 0.0)
            hs = (h * gc).astype(BF)
            hgs = hg * gc
            da = (hgs * u * slope).astype(BF)
            du = (hgs * act).astype(BF)
            out_acc[...] += nn(hs, wd[b])
            dx_acc[...] += nn(da, wg[b]) + nn(du, wu[b])
            xt = xT[...]

            def add(kind, value):
                at = pl.ds(pl.multiple_of((kind * p.NB + b) * W, W), W)
                acc[at] += value

            add(0, nn(xt, da))
            add(1, nn(xt, du))
            add(2, nn(gT[...], hs))
            return carry

        lax.fori_loop(0, p.NB, block, 0)
        rg = RG_s[...] * C_s[...]
        gate = G_s[...]
        dot = jnp.sum(jnp.where(is_expert, gate * rg, 0.0), axis=-1, keepdims=True)
        logits = nn(normg[c], rext[...])
        lg = jnp.where(is_expert, logits, NEG)
        ex = jnp.exp(lg - jnp.max(lg, axis=-1, keepdims=True))
        route = ex / jnp.sum(ex, axis=-1, keepdims=True)
        lgrad = jnp.where(is_expert, route * (rg - dot), rg * gate * (1.0 - gate)).astype(BF)
        drext[...] += nn(xT[...], lgrad)
        dx = dx_acc[...] + nt(lgrad, rext[...])

        @pl.when(k == 0)
        def _():
            dx_own[...] = dx
            out_own[...] = out_acc[...]

        @pl.when(k > 0)
        def _():
            normg[c] = dx.astype(BF)
            cotg[c] = out_acc[...].astype(BF)
            remote(normg.at[c], dxr.at[k - 1], "dx", k - 1, (dp, c)).start()

        return carry

    def chunks(C_s, G_s, RG_s, xT, gT, out_acc, dx_acc):
        lax.fori_loop(0, NT, functools.partial(unit, C_s, G_s, RG_s, xT, gT, out_acc, dx_acc), 0)

    pl.run_scoped(
        chunks, V((R, LANES), F32), V((R, LANES), F32), V((R, LANES), F32), V((W, R), BF), V((W, R), BF), V((R, W), F32), V((R, W), F32)
    )

    def to_stage(i, carry):
        at = pl.ds(pl.multiple_of(i * W, W), W)
        turned = (lax.rem(i, p.NB) < p.EB) | (i >= 2 * p.NB)

        @pl.when(turned)
        def _():
            stage[at] = acc[at].astype(BF).T

        @pl.when(jnp.logical_not(turned))
        def _():
            stage[at] = acc[at].astype(BF)

        return carry

    own_half = pl.multiple_of(core * p.half, 16)
    mate_half = pl.multiple_of((1 - core) * p.half, 16)
    lax.fori_loop(0, 3 * p.NB, to_stage, 0)
    if p.flat > p.total:
        stage[p.total :] = jnp.zeros((p.flat - p.total, W), BF)
    h1_copy = remote(stage.at[pl.ds(mate_half, p.half)], h1, "h1", 0, (mate, z))
    h1_copy.start()

    for k in (1, 2, 3):
        remote(normg.at[zk[k]], dxr.at[k - 1], "dx", k - 1, to_z(k)).wait_recv()
    for k in (1, 2, 3):
        remote(cotg.at[zk[k]], outr.at[k - 1], "o", k - 1, to_z(k)).start()
    dn = dx_own[...] + dxr[0].astype(F32) + dxr[1].astype(F32) + dxr[2].astype(F32)
    mid_back, dgain = rms_back(mid[...], dn, gain_ffn)
    sm_own = jnp.sum(dgain, axis=0, keepdims=True)
    mg = cot_in[...].astype(F32) + mid_back
    dx_own[...] = mg
    ag = mg.astype(BF)
    agrad[...] = ag
    dO = nt(ag, wfull[3])
    for g in range(NG):
        dON[g] = dO[:, g * LANES : (g + 1) * LANES].astype(BF)
    dOt = nt(wfull[3], ag).astype(BF)
    dOT[...] = dOt
    both = dOt.astype(F32) * oT[...].astype(F32)
    for h in range(W // HD):
        delta[h : h + 1] = jnp.sum(both[h * HD : (h + 1) * HD], axis=0, keepdims=True)

    def piece_at(j):
        return pl.ds(pl.multiple_of(core * p.half + chip_at(j) * p.piece, 16), p.piece)

    h1_copy.wait_recv()

    def add_mate(i, carry):
        near = pl.ds(pl.multiple_of(i * 16, 16), 16)
        at = pl.ds(pl.multiple_of(own_half + i * 16, 16), 16)
        stage[at] = (stage[at].astype(F32) + h1[near].astype(F32)).astype(BF)
        return carry

    lax.fori_loop(0, p.half // 16, add_mate, 0)

    def h2_copy(j):
        return remote(stage.at[piece_at(j)], h2.at[j - 1], "h2", j - 1, on_chip(j))

    for j in range(1, p.nc):
        h2_copy(j).start()

    dw = [acc.at[m * W : (m + 1) * W] for m in range(4)]
    dxn = acc.at[4 * W : 4 * W + LEN]
    dw[3][...] = nn(oT[...], agrad[...])
    dxn[...] = jnp.zeros_like(dxn)

    def back_group(pT, dsT, dk_acc, dv_acc, dqT, g, carry):
        at_g = pl.ds(pl.multiple_of(g * LANES, LANES), LANES)
        for qb in range(R // QB):
            cols = slice(qb * QB, (qb + 1) * QB)
            for h in range(HPG):
                s = scores(g, h, qb)
                prob = jnp.exp2(s - lse[pl.ds(g * HPG + h, 1), cols])
                og = dOT[at_g, cols]
                d_prob = nn(vN[g], jnp.where(head_row == h, og, jnp.zeros_like(og)))
                ds = (prob * (d_prob - delta[pl.ds(g * HPG + h, 1), cols])).astype(BF)
                pT[:, h * QB : (h + 1) * QB] = prob.astype(BF)
                dsT[:, h * QB : (h + 1) * QB] = ds
                at = pl.ds(pl.multiple_of(g * LANES + h * HD, HD), HD)
                dqT[h * HD : (h + 1) * HD, cols] = nn(kT[at], ds) * SCALE
            og, qg = dON[g, cols], qN[g, cols]
            o_heads = jnp.concatenate([jnp.where(head_lane == h, og, jnp.zeros_like(og)) for h in range(HPG)], axis=0)
            q_heads = jnp.concatenate([jnp.where(head_lane == h, qg, jnp.zeros_like(qg)) for h in range(HPG)], axis=0)
            dv = nn(pT[...], o_heads)
            dk = nn(dsT[...], q_heads) * LN2
            if qb == 0:
                dv_acc[...] = dv
                dk_acc[...] = dk
            else:
                dv_acc[...] += dv
                dk_acc[...] += dk
        dv = dv_acc[...].astype(BF)
        dk = dk_acc[...]
        dk = (dk * cosk[...] - swap_halves(dk) * sink[...]).astype(BF)
        parts = []
        for h in range(HPG):
            a = dqT[h * HD : h * HD + HD // 2]
            b = dqT[h * HD + HD // 2 : (h + 1) * HD]
            parts += [a * cos_own + b * sin_own, b * cos_own - a * sin_own]
        dq = jnp.concatenate(parts, axis=0).astype(BF)
        dw[0][at_g] = nn(dq, xn[own_pos])
        dw[1][at_g] = nn(dk.T, xn[...])
        dw[2][at_g] = nn(dv.T, xn[...])
        dxn[...] += nn(dk, wfull[1, at_g]) + nn(dv, wfull[2, at_g])
        dxn[own_pos] += nn(dq.T, wfull[0, at_g])
        return carry

    def back(pT, dsT, dk_acc, dv_acc, dqT):
        lax.fori_loop(0, NG, functools.partial(back_group, pT, dsT, dk_acc, dv_acc, dqT), 0)

    wide = V((LEN, HPG * QB), BF)
    pl.run_scoped(back, wide, wide, V((LEN, LANES), F32), V((LEN, LANES), F32), V((LANES, R), F32))

    pxs[...] = dxn[pl.ds(pl.multiple_of((1 - half_own) * R, R), R)].astype(BF)
    px_copy = remote(pxs, pxr, "px", 0, to_z(1))
    px_copy.start()

    for t in range(NT):
        for m in range(4):
            row = m * p.HC
            A[t, row // p.hp, row % p.hp : row % p.hp + p.HC] = dw[m][t * p.HC : (t + 1) * p.HC].astype(BF)
    f1_copy = remote(A.at[:, 1 - core], f1, "f1", 0, (mate, z))
    f1_copy.start()

    dg = jnp.zeros((1, W), F32)
    for half in range(2):
        v = xs[half].astype(F32)
        dg += jnp.sum(dxn[half * R : (half + 1) * R] * (v * inv_rms(v)), axis=0, keepdims=True)
    smr[dp, 0:1] = dg
    smr[dp, 1:2] = sm_own
    smr[dp, 2:16] = drext[...].T[0:14]

    def small(j):
        there = lax.rem(dp + j, p.nd)
        return remote(smr.at[dp], smr.at[dp], "s1", j - 1, (there, z))

    for j in range(1, p.nd):
        small(j).start()

    for j in range(1, p.nc):
        h2_copy(j).wait_recv()

    def add_chips(i, carry):
        near = pl.ds(pl.multiple_of(i * 16, 16), 16)
        at = pl.ds(pl.multiple_of(own_half + chip * p.piece + i * 16, 16), 16)
        v = stage[at].astype(F32)
        for j in range(1, p.nc):
            v += h2[j - 1, near].astype(F32)
        res[at] = v.astype(BF)
        return carry

    lax.fori_loop(0, p.piece // 16, add_chips, 0)

    def h3_copy(j):
        return remote(res.at[piece_at(0)], res.at[piece_at(0)], "h3", j - 1, on_chip(j))

    def h4_copy(j):
        return remote(res.at[piece_at(j)], res.at[piece_at(j)], "h4", j, (mate, z))

    for j in range(1, p.nc):
        h3_copy(j).start()
    h4_copy(0).start()

    f1_copy.wait_recv()
    for t in range(NT):
        A[t, core] = (A[t, core].astype(F32) + f1[t].astype(F32)).astype(BF)

    def chip_rows(j):
        return pl.ds(pl.multiple_of(chip_at(j) * p.pr, 16), p.pr)

    def f2_copy(j):
        return remote(A.at[:, core, chip_rows(j)], f2.at[j - 1], "f2", j - 1, on_chip(j))

    def owner(c):
        return (lambda f: f()) if p.owners == p.nc else pl.when(c < p.owners)

    owns = owner(chip)
    for j in range(1, p.nc):
        owner(chip_at(j))(lambda j=j: f2_copy(j).start())

    def f3_copy(k):
        return remote(fD.at[zk[k]], f3.at[k - 1], "f3", k - 1, to_z(k))

    @owns
    def _():
        for j in range(1, p.nc):
            f2_copy(j).wait_recv()
        for t in range(NT):
            v = A[t, core, chip_rows(0)].astype(F32)
            for j in range(1, p.nc):
                v += f2[j - 1, t].astype(F32)
            fD[t] = v.astype(BF)
        for k in (1, 2, 3):
            f3_copy(k).start()

    for j in range(1, p.nd):
        small(j).wait_recv()
    total = smr[0]
    for j in range(1, p.nd):
        total += smr[j]
    smz[z] = total

    def small_z(k):
        return remote(smz.at[z], smz.at[z], "s2", k - 1, to_z(k))

    for k in (1, 2, 3):
        small_z(k).start()
    def f4_copy(j):
        there = lax.rem(dp + j, p.nd)
        part = att.at[core, chip_rows(0)]
        return remote(part, part, "f4", j - 1, (there, z))

    @owns
    def _():
        for k in (1, 2, 3):
            f3_copy(k).wait_recv()
        v = fD[z].astype(F32)
        for k in (1, 2, 3):
            v += f3[k - 1].astype(F32)
        att[core, chip_rows(0)] = v.astype(BF)
        for j in range(1, p.nd):
            f4_copy(j).start()

    px_copy.wait_recv()
    dn = dxn[own_pos] + pxr[...].astype(F32)
    x_back, _ = rms_back(x_in[...].astype(F32), dn, gain_attn)
    din_ref[...] = dx_own[...] + x_back
    for k in (1, 2, 3):
        remote(cotg.at[zk[k]], outr.at[k - 1], "o", k - 1, to_z(k)).wait_recv()
    whole = mid[...] + (out_own[...] + outr[0].astype(F32) + outr[1].astype(F32) + outr[2].astype(F32))
    out_ref[...] = whole.astype(BF)

    for k in (1, 2, 3):
        small_z(k).wait_recv()
    sm_ref[...] = smz[0] + smz[1] + smz[2] + smz[3]
    for j in range(1, p.nc):
        h3_copy(j).wait_recv()
        h4_copy(p.nc - j).start()
    for j in range(p.nc):
        h4_copy(j).wait_recv()
    write = pltpu.make_async_copy(res, res_hbm, lsem.at[0])
    write.start()
    for j in range(1, p.nd):
        sender = lax.rem(dp + p.nd - j, p.nd)
        owner(lax.div(sender, 2))(lambda j=j: f4_copy(j).wait_recv())
    for c in range(2):
        att_ref[c * p.hp : (c + 1) * p.hp] = att[c]

    for k in (1, 2, 3):
        for i in range(4 // S):
            w_send(k, i).wait_send()
            for j in range(1, S):
                w_forward(k, i, j).wait_send()
        remote(cot_in, cot_in, "c", k - 1, to_z(k)).wait_send()
        for b in range(R // QB):
            part = normg.at[z, b * QB : (b + 1) * QB]
            remote(part, part, "n", (k - 1) * 2 + b, to_z(k)).wait_send()
        remote(normg.at[zk[k]], dxr.at[k - 1], "dx", k - 1, to_z(k)).wait_send()
        remote(cotg.at[zk[k]], outr.at[k - 1], "o", k - 1, to_z(k)).wait_send()
        small_z(k).wait_send()
    x_copy.wait_send()
    h1_copy.wait_send()
    px_copy.wait_send()
    f1_copy.wait_send()
    for j in range(1, p.nc):
        h2_copy(j).wait_send()
        h3_copy(j).wait_send()
        owner(chip_at(j))(lambda j=j: f2_copy(j).wait_send())
    for j in range(p.nc):
        h4_copy(j).wait_send()
    for j in range(1, p.nd):
        small(j).wait_send()

    @owns
    def _():
        for k in (1, 2, 3):
            f3_copy(k).wait_send()
        for j in range(1, p.nd):
            f4_copy(j).wait_send()

    write.wait()


def tables():
    half = HD // 2
    freqs = 10000.0 ** (-np.arange(half, dtype=np.float32) / np.float32(half))
    angles = np.arange(LEN, dtype=np.float32)[:, None] * freqs.astype(np.float32)[None, :]
    cosine, sine = np.cos(angles).astype(np.float32), np.sin(angles).astype(np.float32)
    reps = LANES // HD
    cos_wide = np.tile(np.concatenate([cosine, cosine], axis=1), (1, reps))
    sin_wide = np.tile(np.concatenate([-sine, sine], axis=1), (1, reps))
    return cos_wide, sin_wide, np.ascontiguousarray(cosine.T), np.ascontiguousarray(sine.T)


def per_device(
    nd,
    inputs,
    lengths,
    expert_ids,
    gain_attn,
    w_query,
    w_key,
    w_value,
    w_out,
    gain_ffn,
    router,
    shared_gate_vec,
    exp_gate,
    exp_up,
    exp_down,
    sh_gate,
    sh_up,
    sh_down,
    cotangent,
):
    R, W = inputs.shape
    experts, _, eff = exp_gate.shape
    ff = sh_gate.shape[1]
    p = Plan(nd, R, W, experts, eff, ff)
    number, names = sem_plan(p)
    gains = jnp.stack([gain_attn, gain_ffn]).astype(F32)
    watt = jnp.stack([w_query.T, w_key.T, w_value.T, w_out])
    vec = shared_gate_vec[:, None]
    rext = jnp.concatenate([router, vec, vec, jnp.zeros((W, LANES - experts - 2), BF)], axis=1)
    eg = exp_gate.swapaxes(1, 2).reshape(p.EB, p.B, W)
    eu = exp_up.swapaxes(1, 2).reshape(p.EB, p.B, W)
    ed = exp_down.reshape(p.EB, p.B, W)
    cosk, sink, cost, sint = tables()
    vm = pl.BlockSpec(memory_space=pltpu.VMEM)
    hbm = pl.BlockSpec(memory_space=pl.ANY)
    V = pltpu.VMEM
    hc = W // HD
    scratch = [
        pltpu.SemaphoreType.DMA((number,)),
        pltpu.SemaphoreType.DMA((number,)),
        pltpu.SemaphoreType.DMA((8,)),
        V((4, W, W), BF),
        V((2, R, W), BF),
        V((LEN, W), BF),
        V((NT, R, W), BF),
        V((NT, R, W), BF),
        V((p.NB, W, p.B), BF),
        V((p.NB, W, p.B), BF),
        V((p.NB, p.B, W), BF),
        V((W, R), BF),
        V((p.NG, R, LANES), BF),
        V((p.NG, LEN, LANES), BF),
        V((W, LEN), BF),
        V((p.NG, LEN, LANES), BF),
        V((W, LEN), BF),
        V((W, R), BF),
        V((up16(hc), R), F32),
        V((LEN, R), F32),
        V((R, W), F32),
        V((R, W), F32),
        V((R, W), F32),
        V((3, R, W), BF),
        V((3, R, W), BF),
        V((p.total, W), F32),
        V((W, LANES), F32),
        V((p.flat, W), BF),
        V((p.half, W), BF),
        V((max(p.nc - 1, 1), p.piece, W), BF),
        V((p.flat, W), BF),
        V((R, W), BF),
        V((p.NG, R, LANES), BF),
        V((W, R), BF),
        V((up16(hc), R), F32),
        V((R, W), BF),
        V((R, W), BF),
        V((NT, 2, p.hp, W), BF),
        V((NT, p.hp, W), BF),
        V((max(p.nc - 1, 1), NT, p.pr, W), BF),
        V((NT, p.pr, W), BF),
        V((3, p.pr, W), BF),
        V((2, p.hp, W), BF),
        V((nd, 16, W), F32),
        V((NT, 16, W), F32),
    ]
    output, d_inputs, res, att, small = pl.pallas_call(
        functools.partial(kernel, p, names),
        out_shape=[
            jax.ShapeDtypeStruct((R, W), BF),
            jax.ShapeDtypeStruct((R, W), F32),
            jax.ShapeDtypeStruct((p.flat, W), BF),
            jax.ShapeDtypeStruct((2 * p.hp, W), BF),
            jax.ShapeDtypeStruct((16, W), F32),
        ],
        in_specs=[pl.BlockSpec(memory_space=pltpu.SMEM)] + [vm] * 4 + [hbm] * 8 + [vm] * 4,
        out_specs=[vm, vm, hbm, vm, vm],
        scratch_shapes=scratch,
        compiler_params=pltpu.CompilerParams(collective_id=0, has_side_effects=True, vmem_limit_bytes=63 << 20),
        name="block",
    )(
        lengths,
        expert_ids.T,
        gains,
        watt,
        rext,
        inputs,
        cotangent,
        eg,
        eu,
        ed,
        sh_gate,
        sh_up,
        sh_down,
        jnp.asarray(cosk),
        jnp.asarray(sink),
        jnp.asarray(cost),
        jnp.asarray(sint),
    )
    kinds = res[: p.total].reshape(3, p.NB * p.B, W).astype(F32)

    def routed(kind):
        return kinds[kind, : experts * eff].reshape(experts, eff, W)

    d_exp_gate, d_exp_up = routed(0).swapaxes(1, 2), routed(1).swapaxes(1, 2)
    d_exp_down = routed(2)
    d_sh_gate, d_sh_up = kinds[0, experts * eff :], kinds[1, experts * eff :]
    d_sh_down = kinds[2, experts * eff :]
    att = att[: 4 * p.HC].reshape(4, p.HC, W).astype(F32)
    return (
        output,
        d_inputs,
        small[0],
        att[0].T,
        att[1].T,
        att[2].T,
        att[3],
        small[1],
        small[2 : 2 + experts].T,
        small[2 + experts] + small[3 + experts],
        d_exp_gate,
        d_exp_up,
        d_exp_down,
        d_sh_gate,
        d_sh_up,
        d_sh_down,
    )


def solution(mesh):
    rows = P(("dp", "tensor"), None)
    cols = P(None, "tensor")
    deep = P(None, None, "tensor")
    weights = (cols, cols, cols, P("tensor", None))
    experts = (deep, deep, P(None, "tensor", None), cols, cols, P("tensor", None))
    in_specs = (rows, P("dp"), P("dp", None), P()) + weights + (P(), P(), P()) + experts + (rows,)
    out_specs = (rows, rows, P()) + weights + (P(), P(), P()) + experts
    return jax.shard_map(
        functools.partial(per_device, mesh.shape["dp"]),
        mesh=mesh,
        in_specs=in_specs,
        out_specs=out_specs,
        check_vma=False,
    )
```

```python
import functools

import jax
import jax.numpy as jnp
import numpy as np
from jax import lax
from jax.experimental import pallas as pl
from jax.experimental.pallas import tpu as pltpu
from jax.sharding import PartitionSpec as P

HD = 32
LEN = 1024
NT = 4
LANES = 128
QB = 256
BF = jnp.bfloat16
F32 = jnp.float32
MESH = pl.DeviceIdType.MESH
NEG = -1e30
SCALE = HD**-0.5
LOG2E = 1.4426950408889634
LN2 = 0.6931471805599453


def nn(a, b):
    return lax.dot_general(a, b, (((1,), (0,)), ((), ())), preferred_element_type=F32)


def nt(a, b):
    return lax.dot_general(a, b, (((1,), (1,)), ((), ())), preferred_element_type=F32)


def inv_rms(v):
    return lax.rsqrt(jnp.mean(v * v, axis=-1, keepdims=True) + 1e-06)


def rms_back(v, grad, gain):
    r = inv_rms(v)
    u = v * r
    g = grad * gain
    return r * (g - u * jnp.mean(g * u, axis=-1, keepdims=True)), grad * u


def up16(n):
    return -(-n // 16) * 16


class Plan:
    def __init__(self, nd, rows, width, experts, eff, ff):
        self.nd, self.R, self.W = nd, rows, width
        self.G = NT * rows
        self.NG = width // LANES
        self.HC = width // NT
        self.B = 2 * eff
        self.EB = experts // 2
        self.NB = self.EB + 1
        assert ff == self.B == width and LEN == 2 * rows
        self.E, self.eff, self.ff = experts, eff, ff
        self.share = min(4, nd)
        self.nc = nd // 2
        self.hp = 2 * self.HC
        assert 2 * self.hp == width == self.B
        self.pr = max(16, self.hp // self.nc)
        self.owners = self.hp // self.pr
        assert self.owners * self.pr == self.hp and self.pr % 16 == 0 and self.owners <= self.nc


class Sems:
    def __init__(self):
        self.n = 0

    def take(self, n):
        base = self.n
        self.n += n
        return base


def sem_plan(p):
    s, names = Sems(), {}
    names["w"] = s.take(3 * (4 // p.share))
    names["f"] = s.take(3 * (4 // p.share) * max(p.share - 1, 1))
    names["x"] = s.take(1)
    for way in "rl":
        names["c" + way] = s.take(4)
        names["n" + way] = s.take(8)
    names["dx"] = s.take(3)
    names["o"] = s.take(3)
    names["h1"] = s.take(p.NB)
    names["h2"] = s.take(p.NB * max(p.nc - 1, 1))
    names["h3"] = s.take(p.NB * max(p.nc - 1, 1))
    names["h4"] = s.take(p.NB * p.nc)
    names["px"] = s.take(1)
    names["f1"] = s.take(1)
    names["f2"] = s.take(max(p.nc - 1, 1))
    names["f3"] = s.take(3)
    names["f4"] = s.take(p.nd - 1)
    names["s1"] = s.take(p.nd - 1)
    names["s2"] = s.take(3)
    return s.n, names


def kernel(
    p,
    names,
    len_ref,
    ids_ref,
    gain_attn_ref,
    gain_ffn_ref,
    router_ref,
    vec_ref,
    wq_ref,
    wk_ref,
    wv_ref,
    wo_ref,
    x_hbm,
    cot_hbm,
    eg_hbm,
    eu_hbm,
    ed_hbm,
    sg_hbm,
    su_hbm,
    sd_hbm,
    cosk,
    sink,
    cost,
    sint,
    out_ref,
    din_ref,
    eg_out,
    eu_out,
    ed_out,
    sg_out,
    su_out,
    sd_out,
    att_ref,
    sm_ref,
    send,
    recv,
    lsem,
    wfull,
    rext32,
    rext,
    xs,
    xn,
    cotg,
    normg,
    wg,
    wu,
    wd,
    qT,
    qN,
    kN,
    kvT,
    vN,
    oT,
    lse,
    bias,
    mid,
    dx_own,
    out_own,
    dxr,
    outr,
    acc,
    drext,
    stage,
    h1,
    h2,
    res,
    agrad,
    dON,
    dOT,
    delta,
    pxr,
    A,
    f1,
    f2,
    fD,
    f3,
    att,
    smr,
    smz,
):
    R, W, NG = p.R, p.W, p.NG
    dp, z = lax.axis_index("dp"), lax.axis_index("tensor")
    zlo = lax.rem(z, 2)
    zk = [z, z + 1 - 2 * zlo, lax.rem(z + 2, NT), NT - 1 - z]
    core = lax.rem(dp, 2)
    chip = lax.div(dp, 2)
    mate = dp + 1 - 2 * core
    half_own = zlo

    def remote(src, dst, kind, i, dev):
        j = names[kind] + i
        return pltpu.make_async_remote_copy(
            src_ref=src, dst_ref=dst, send_sem=send.at[j], recv_sem=recv.at[j], device_id=dev, device_id_type=MESH
        )

    def to_z(k):
        return (dp, zk[k])

    def chip_at(j):
        return lax.rem(chip + j, p.nc)

    def on_chip(j):
        return (2 * chip_at(j) + core, z)

    def hop(kind, buf, way, i, part, rows, at):
        there = (dp, z + 1) if way == "r" else (dp, z - 1)
        ref = buf.at[at, rows]
        parts = 1 if kind == "c" else R // QB
        return remote(ref, ref, kind + way, i * parts + part, there)

    def send_own(kind, buf, part, rows):
        @pl.when(z < NT - 1)
        def _():
            hop(kind, buf, "r", 0, part, rows, z).start()

        @pl.when(z > 0)
        def _():
            hop(kind, buf, "l", 0, part, rows, z).start()

    def own_sent(kind, buf, part, rows):
        @pl.when(z < NT - 1)
        def _():
            hop(kind, buf, "r", 0, part, rows, z).wait_send()

        @pl.when(z > 0)
        def _():
            hop(kind, buf, "l", 0, part, rows, z).wait_send()

    def arrive(kind, buf, i, part, rows):
        @pl.when(z - 1 - i >= 0)
        def _():
            hop(kind, buf, "r", i, part, rows, z - 1 - i).wait_recv()

            @pl.when(z < NT - 1)
            def _():
                hop(kind, buf, "r", i + 1, part, rows, z - 1 - i).start()

        @pl.when(z + 1 + i < NT)
        def _():
            hop(kind, buf, "l", i, part, rows, z + 1 + i).wait_recv()

            @pl.when(z > 0)
            def _():
                hop(kind, buf, "l", i + 1, part, rows, z + 1 + i).start()

    def handed_on(kind, buf, c, part, rows):
        @pl.when((c < z) & (z < NT - 1))
        def _():
            hop(kind, buf, "r", z - c, part, rows, c).wait_send()

        @pl.when((c > z) & (z > 0))
        def _():
            hop(kind, buf, "l", c - z, part, rows, c).wait_send()

    halves = [slice(i * QB, (i + 1) * QB) for i in range(R // QB)]

    V = pltpu.VMEM
    x_in, cot_in = xs.at[half_own], cotg.at[z]
    loads = [
        pltpu.make_async_copy(src, dst, lsem.at[i])
        for i, (src, dst) in enumerate(
            [
                (x_hbm, x_in),
                (cot_hbm, cot_in),
                (eg_hbm, wg.at[: p.EB]),
                (eu_hbm, wu.at[: p.EB]),
                (ed_hbm, wd.at[: p.EB]),
                (sg_hbm, agrad.at[:W]),
                (su_hbm, dOT.at[:, :W]),
                (sd_hbm, wd.at[p.EB]),
            ]
        )
    ]
    for c in loads:
        c.start()
    barrier = pltpu.get_barrier_semaphore()
    for k in (1, 2, 3):
        pl.semaphore_signal(barrier, inc=1, device_id=to_z(k), device_id_type=MESH)

    def greet(j, carry):
        pl.semaphore_signal(barrier, inc=1, device_id=(lax.rem(dp + j, p.nd), z), device_id_type=MESH)
        return carry

    lax.fori_loop(1, p.nd, greet, 0)
    pl.semaphore_wait(barrier, 3 + p.nd - 1)

    S = p.share
    member = lax.rem(dp, S)
    base = dp - member
    own_cols = pl.ds(pl.multiple_of(z * p.HC, 32), p.HC)

    def cols_of(k):
        return pl.ds(pl.multiple_of(zk[k] * p.HC, 32), p.HC)

    def w_send(k, i):
        m = member + S * i
        return remote(wfull.at[m, own_cols], wfull.at[m, own_cols], "w", (k - 1) * (4 // S) + i, to_z(k))

    def w_recv(k, i):
        m = member + S * i
        return remote(wfull.at[m, cols_of(k)], wfull.at[m, cols_of(k)], "w", (k - 1) * (4 // S) + i, to_z(k))

    def w_forward(k, i, j):
        m = member + S * i
        there = base + lax.rem(member + j, S)
        return remote(
            wfull.at[m, cols_of(k)],
            wfull.at[m, cols_of(k)],
            "f",
            ((k - 1) * (4 // S) + i) * (S - 1) + j - 1,
            (there, z),
        )

    for m, ref in enumerate((wq_ref, wk_ref, wv_ref, wo_ref)):
        wfull[m, own_cols] = ref[...]
    x_copy = remote(x_in, x_in, "x", 0, to_z(1))
    for k in (1, 2, 3):
        for i in range(4 // S):
            w_send(k, i).start()
    loads[0].wait()
    x_copy.start()
    gain_attn = gain_attn_ref[...].astype(F32)
    gain_ffn = gain_ffn_ref[...].astype(F32)
    rext32[0 : p.E] = router_ref[...].astype(F32)
    rext32[p.E : p.E + 1] = vec_ref[...].astype(F32)
    rext32[p.E + 1 : p.E + 2] = vec_ref[...].astype(F32)
    rext32[p.E + 2 :] = jnp.zeros((14 - p.E, W), F32)
    rext[0:16] = rext32[...].astype(BF)
    rext[16:] = jnp.zeros((LANES - 16, W), BF)

    def mask_rows(i, carry):
        key = lax.broadcasted_iota(jnp.int32, (QB, R), 0) + i * QB
        query = lax.broadcasted_iota(jnp.int32, (QB, R), 1) + half_own * R
        length = len_ref[lax.div(z, 2)]
        bias[pl.ds(pl.multiple_of(i * QB, QB), QB)] = jnp.where((key <= query) & (key < length), 0.0, NEG)
        return carry

    lax.fori_loop(0, LEN // QB, mask_rows, 0)
    for k in (1, 2, 3):
        for i in range(4 // S):
            w_recv(k, i).wait_recv()
            for j in range(1, S):
                w_forward(k, i, j).start()

    for c in loads[1:]:
        c.wait()
    wg[p.EB] = agrad[:W].T
    wu[p.EB] = dOT[:, :W].T
    x_copy.wait_recv()
    send_own("c", cotg, 0, slice(None))

    def norm_half(i, carry):
        v = xs[i].astype(F32)
        xn[pl.ds(pl.multiple_of(i * R, R), R)] = (v * inv_rms(v) * gain_attn).astype(BF)
        return carry

    lax.fori_loop(0, 2, norm_half, 0)
    for k in (1, 2, 3):
        for i in range(4 // S):
            for j in range(1, S):
                w_forward(k, i, j).wait_recv()

    own_pos = pl.ds(pl.multiple_of(half_own * R, R), R)
    lane = lax.broadcasted_iota(jnp.int32, (1, LANES), 1)
    low_half = lax.rem(lane, HD) < HD // 2

    def swap_halves(v):
        return jnp.where(low_half, pltpu.roll(v, LANES - HD // 2, 1), pltpu.roll(v, HD // 2, 1))

    q_pre = nt(wfull[0], xn[own_pos])
    cos_own, sin_own = cost[:, own_pos], sint[:, own_pos]
    for h in range(W // HD):
        a = q_pre[h * HD : h * HD + HD // 2]
        b = q_pre[h * HD + HD // 2 : (h + 1) * HD]
        qT[h * HD : h * HD + HD // 2] = ((a * cos_own - b * sin_own) * (SCALE * LOG2E)).astype(BF)
        qT[h * HD + HD // 2 : (h + 1) * HD] = ((a * sin_own + b * cos_own) * (SCALE * LOG2E)).astype(BF)

    def project(i, carry):
        rows = pl.ds(pl.multiple_of(i * QB, QB), QB)
        xb = xn[rows]
        k_pre = nt(xb, wfull[1])
        v_pre = nt(xb, wfull[2])
        c, s = cosk[rows], sink[rows]
        for g in range(NG):
            kg = k_pre[:, g * LANES : (g + 1) * LANES]
            kN[g, rows] = (kg * c + swap_halves(kg) * s).astype(BF)
            vN[g, rows] = v_pre[:, g * LANES : (g + 1) * LANES].astype(BF)
        return carry

    lax.fori_loop(0, LEN // QB, project, 0)
    for g in range(NG):
        rows = slice(g * LANES, (g + 1) * LANES)
        kvT[rows] = vN[g].T
        qN[g] = qT[rows].T

    head_row = lax.div(lax.broadcasted_iota(jnp.int32, (LANES, 1), 0), HD)
    head_lane = lax.div(lane, HD)
    HPG = LANES // HD

    def scores(g, h, qb):
        qg = qT[pl.ds(pl.multiple_of(g * LANES, LANES), LANES), qb * QB : (qb + 1) * QB]
        masked = jnp.where(head_row == h, qg, jnp.zeros_like(qg))
        return nn(kN[g], masked) + bias[:, qb * QB : (qb + 1) * QB]

    for qb in range(R // QB):
        cols = slice(qb * QB, (qb + 1) * QB)

        def heads(g, carry):
            for h in range(HPG):
                s = scores(g, h, qb)
                top = jnp.max(s, axis=0, keepdims=True)
                e = jnp.exp2(s - top)
                total = jnp.sum(e, axis=0, keepdims=True)
                at = pl.ds(pl.multiple_of(g * LANES + h * HD, HD), HD)
                o = nn(kvT[at], e.astype(BF)) * (1.0 / total)
                oT[at, cols] = o.astype(BF)
                lse[pl.ds(g * HPG + h, 1), cols] = top + jnp.log(total) * LOG2E
            return carry

        lax.fori_loop(0, NG, heads, 0)
        rows = slice(qb * QB, (qb + 1) * QB)
        m = x_in[rows].astype(F32) + nn(oT[:, cols].T, wfull[3])
        mid[rows] = m
        normg[z, rows] = (m * inv_rms(m) * gain_ffn).astype(BF)
        if qb == 0:
            arrive("c", cotg, 0, 0, slice(None))
        send_own("n", normg, qb, rows)
    arrive("c", cotg, 1, 0, slice(None))
    for g in range(NG):
        kvT[g * LANES : (g + 1) * LANES] = kN[g].T

    def zero_acc(i, carry):
        acc[pl.ds(pl.multiple_of(i * 16, 16), 16)] = jnp.zeros((16, W), F32)
        return carry

    lax.fori_loop(0, 3 * p.NB * W // 16, zero_acc, 0)
    drext[...] = jnp.zeros_like(drext)
    zhi = lax.div(z, 2)

    def chunk_of(k):
        return 2 * lax.rem(zhi + lax.div(k, 2), 2) + lax.rem(zlo + lax.rem(k, 2), 2)

    def chip_rows(j):
        return pl.ds(pl.multiple_of(chip_at(j) * p.pr, 16), p.pr)

    def owner(c):
        return (lambda f: f()) if p.owners == p.nc else pl.when(c < p.owners)

    owns = owner(chip)

    def h1_copy(b):
        return remote(stage.at[b, :, 1 - core], h1.at[b], "h1", b, (mate, z))

    def h2_copy(b, j):
        i = b * (p.nc - 1) + j - 1
        return remote(stage.at[b, :, core, chip_rows(j)], h2.at[j - 1, b], "h2", i, on_chip(j))

    def h3_copy(b, j):
        part = res.at[b, :, core, chip_rows(0)]
        return remote(part, part, "h3", b * (p.nc - 1) + j - 1, on_chip(j))

    def h4_copy(b, j):
        part = res.at[b, :, core, chip_rows(j)]
        return remote(part, part, "h4", b * p.nc + j, (mate, z))

    def mate_half(b):
        for kind in range(3):
            v = acc[pl.ds(pl.multiple_of((3 * b + kind) * W, W), W)].astype(BF)
            if kind == 2:
                v = v.T
                stage[b, kind, 0] = v[: p.hp]
                stage[b, kind, 1] = v[p.hp :]
            else:

                @pl.when(b < p.EB)
                def _(v=v, kind=kind):
                    w = v.T
                    stage[b, kind, 0] = w[: p.hp]
                    stage[b, kind, 1] = w[p.hp :]

                @pl.when(b >= p.EB)
                def _(v=v, kind=kind):
                    stage[b, kind, 0] = v[: p.hp]
                    stage[b, kind, 1] = v[p.hp :]

        h1_copy(b).start()

    def to_chips(b):
        h1_copy(b).wait_recv()
        for kind in range(3):
            stage[b, kind, core] = (stage[b, kind, core].astype(F32) + h1[b, kind].astype(F32)).astype(BF)
        for j in range(1, p.nc):
            owner(chip_at(j))(lambda j=j: h2_copy(b, j).start())

    def from_chips(b):
        @owns
        def _():
            for j in range(1, p.nc):
                h2_copy(b, j).wait_recv()
            for kind in range(3):
                v = stage[b, kind, core, chip_rows(0)].astype(F32)
                for j in range(1, p.nc):
                    v += h2[j - 1, b, kind].astype(F32)
                res[b, kind, core, chip_rows(0)] = v.astype(BF)
            for j in range(1, p.nc):
                h3_copy(b, j).start()
            h4_copy(b, 0).start()

    def hand_over(b):
        for j in range(1, p.nc):
            sender = lax.rem(chip + p.nc - j, p.nc)

            @owner(sender)
            def _(j=j):
                h3_copy(b, j).wait_recv()
                h4_copy(b, p.nc - j).start()

    def unit(C_s, G_s, RG_s, xT, gT, out_acc, dx_acc, k, carry):
        c = chunk_of(k)

        x = normg[c]
        xT[...] = x.T
        gT[...] = cotg[c].T
        logits = nt(x, rext[...])
        is_expert = lane < p.E
        lg = jnp.where(is_expert, logits, NEG)
        ex = jnp.exp(lg - jnp.max(lg, axis=-1, keepdims=True))
        route = ex / jnp.sum(ex, axis=-1, keepdims=True)
        at = pl.ds(pl.multiple_of(c * R, R), R)
        down = lax.broadcasted_iota(jnp.int32, (LANES, R), 0)
        named = (down == ids_ref[0:1, at]) | (down == ids_ref[1:2, at]) | ((down >= p.E) & (down < p.E + 2))
        chosen = jnp.where(named, 1.0, 0.0).T
        C_s[...] = chosen
        gate = jnp.where(is_expert, route, lax.logistic(logits)) * chosen
        G_s[...] = gate
        RG_s[...] = jnp.zeros_like(RG_s)
        out_acc[...] = jnp.zeros_like(out_acc)
        dx_acc[...] = jnp.zeros_like(dx_acc)

        def block(b, carry):
            @pl.when((b == 0) & (k < NT - 1))
            def _():
                arrive("n", normg, k, 0, halves[0])

            @pl.when((b == 3) & (k < NT - 1))
            def _():
                arrive("n", normg, k, 1, halves[1])

            @pl.when((b == 1) & (k == 1))
            def _():
                arrive("c", cotg, 2, 0, slice(None))

            xb, gb = normg[c], cotg[c]
            a = nt(xb, wg[b])
            u = nt(xb, wu[b])
            hg = nt(gb, wd[b])
            gates = G_s[...]
            first = jnp.sum(jnp.where(lane == 2 * b, gates, 0.0), axis=-1, keepdims=True)
            second = jnp.sum(jnp.where(lane == 2 * b + 1, gates, 0.0), axis=-1, keepdims=True)
            wide = lax.broadcasted_iota(jnp.int32, (1, p.B), 1) < p.eff
            gc = jnp.where(wide, first, second)
            sig = 0.5 * jnp.tanh(0.5 * a) + 0.5
            act = a * sig
            slope = sig + act - act * sig
            h = act * u
            prod = h * hg
            s0 = jnp.sum(jnp.where(wide, prod, 0.0), axis=-1, keepdims=True)
            s1 = jnp.sum(jnp.where(wide, 0.0, prod), axis=-1, keepdims=True)
            RG_s[...] += jnp.where(lane == 2 * b, s0, 0.0) + jnp.where(lane == 2 * b + 1, s1, 0.0)
            hs = (h * gc).astype(BF)
            hgs = hg * gc
            da = (hgs * u * slope).astype(BF)
            du = (hgs * act).astype(BF)
            out_acc[...] += nn(hs, wd[b])
            dx_acc[...] += nn(da, wg[b]) + nn(du, wu[b])
            xt = xT[...]

            def add(kind, value):
                at = pl.ds(pl.multiple_of((3 * b + kind) * W, W), W)
                acc[at] += value

            add(0, nn(xt, da))
            add(1, nn(xt, du))
            add(2, nn(gT[...], hs))

            @pl.when(k == NT - 1)
            def _():
                mate_half(b)

                @pl.when(b > 0)
                def _():
                    to_chips(b - 1)

            return carry

        lax.fori_loop(0, p.NB, block, 0)
        rg = RG_s[...] * C_s[...]
        gate = G_s[...]
        dot = jnp.sum(jnp.where(is_expert, gate * rg, 0.0), axis=-1, keepdims=True)
        logits = nt(normg[c], rext[...])
        lg = jnp.where(is_expert, logits, NEG)
        ex = jnp.exp(lg - jnp.max(lg, axis=-1, keepdims=True))
        route = ex / jnp.sum(ex, axis=-1, keepdims=True)
        lgrad = jnp.where(is_expert, route * (rg - dot), rg * gate * (1.0 - gate)).astype(BF)
        drext[...] += nn(xT[...], lgrad)
        dx = dx_acc[...] + nn(lgrad, rext[...])

        for b in range(R // QB):
            handed_on("n", normg, c, b, halves[b])
        handed_on("c", cotg, c, 0, slice(None))

        @pl.when(k == 0)
        def _():
            dx_own[...] = dx
            out_own[...] = out_acc[...]

        @pl.when(k > 0)
        def _():
            normg[c] = dx.astype(BF)
            cotg[c] = out_acc[...].astype(BF)
            remote(normg.at[c], dxr.at[k - 1], "dx", k - 1, (dp, c)).start()

        return carry

    def chunks(C_s, G_s, RG_s, xT, gT, out_acc, dx_acc):
        lax.fori_loop(0, NT, functools.partial(unit, C_s, G_s, RG_s, xT, gT, out_acc, dx_acc), 0)

    pl.run_scoped(
        chunks, V((R, LANES), F32), V((R, LANES), F32), V((R, LANES), F32), V((W, R), BF), V((W, R), BF), V((R, W), F32), V((R, W), F32)
    )

    to_chips(p.NB - 1)

    for k in (1, 2, 3):
        remote(normg.at[zk[k]], dxr.at[k - 1], "dx", k - 1, to_z(k)).wait_recv()
    for k in (1, 2, 3):
        remote(cotg.at[zk[k]], outr.at[k - 1], "o", k - 1, to_z(k)).start()
    dn = dx_own[...] + dxr[0].astype(F32) + dxr[1].astype(F32) + dxr[2].astype(F32)
    mid_back, dgain = rms_back(mid[...], dn, gain_ffn)
    sm_own = jnp.sum(dgain, axis=0, keepdims=True)
    mg = cot_in[...].astype(F32) + mid_back
    dx_own[...] = mg
    ag = mg.astype(BF)
    agrad[...] = ag
    dO = nt(ag, wfull[3])
    for g in range(NG):
        dON[g] = dO[:, g * LANES : (g + 1) * LANES].astype(BF)
    dOt = nt(wfull[3], ag).astype(BF)
    dOT[...] = dOt
    both = dOt.astype(F32) * oT[...].astype(F32)
    for h in range(W // HD):
        delta[h : h + 1] = jnp.sum(both[h * HD : (h + 1) * HD], axis=0, keepdims=True)

    dw = [acc.at[m * W : (m + 1) * W] for m in range(4)]
    dxn = acc.at[4 * W : 4 * W + LEN]
    dw[3][...] = nn(oT[...], agrad[...])
    dxn[...] = jnp.zeros_like(dxn)

    def back_group(pT, dsT, dk_acc, dv_acc, dqT, g, carry):
        def chips(b, carry):
            from_chips(b)
            return carry

        lax.fori_loop(2 * g, jnp.minimum(2 * g + 2, p.NB), chips, 0)
        at_g = pl.ds(pl.multiple_of(g * LANES, LANES), LANES)
        for qb in range(R // QB):
            cols = slice(qb * QB, (qb + 1) * QB)
            for h in range(HPG):
                s = scores(g, h, qb)
                prob = jnp.exp2(s - lse[pl.ds(g * HPG + h, 1), cols])
                og = dOT[at_g, cols]
                d_prob = nn(vN[g], jnp.where(head_row == h, og, jnp.zeros_like(og)))
                ds = (prob * (d_prob - delta[pl.ds(g * HPG + h, 1), cols])).astype(BF)
                pT[:, h * QB : (h + 1) * QB] = prob.astype(BF)
                dsT[:, h * QB : (h + 1) * QB] = ds
                at = pl.ds(pl.multiple_of(g * LANES + h * HD, HD), HD)
                dqT[h * HD : (h + 1) * HD, cols] = nn(kvT[at], ds) * SCALE
            og, qg = dON[g, cols], qN[g, cols]
            o_heads = jnp.concatenate([jnp.where(head_lane == h, og, jnp.zeros_like(og)) for h in range(HPG)], axis=0)
            q_heads = jnp.concatenate([jnp.where(head_lane == h, qg, jnp.zeros_like(qg)) for h in range(HPG)], axis=0)
            dv = nn(pT[...], o_heads)
            dk = nn(dsT[...], q_heads) * LN2
            if qb == 0:
                dv_acc[...] = dv
                dk_acc[...] = dk
            else:
                dv_acc[...] += dv
                dk_acc[...] += dk
        dv = dv_acc[...].astype(BF)
        dk = dk_acc[...]
        dk = (dk * cosk[...] - swap_halves(dk) * sink[...]).astype(BF)
        parts = []
        for h in range(HPG):
            a = dqT[h * HD : h * HD + HD // 2]
            b = dqT[h * HD + HD // 2 : (h + 1) * HD]
            parts += [a * cos_own + b * sin_own, b * cos_own - a * sin_own]
        dq = jnp.concatenate(parts, axis=0).astype(BF)
        dw[0][at_g] = nn(dq, xn[own_pos])
        dw[1][at_g] = nn(dk.T, xn[...])
        dw[2][at_g] = nn(dv.T, xn[...])
        dxn[...] += nn(dk, wfull[1, at_g]) + nn(dv, wfull[2, at_g])
        dxn[own_pos] += nn(dq.T, wfull[0, at_g])
        return carry

    def back(pT, dsT, dk_acc, dv_acc, dqT):
        lax.fori_loop(0, NG, functools.partial(back_group, pT, dsT, dk_acc, dv_acc, dqT), 0)

    wide = V((LEN, HPG * QB), BF)
    pl.run_scoped(back, wide, wide, V((LEN, LANES), F32), V((LEN, LANES), F32), V((LANES, R), F32))

    pxs = agrad
    pxs[...] = dxn[pl.ds(pl.multiple_of((1 - half_own) * R, R), R)].astype(BF)
    px_copy = remote(pxs, pxr, "px", 0, to_z(1))
    px_copy.start()

    for t in range(NT):
        for m in range(4):
            row = m * p.HC
            A[t, row // p.hp, row % p.hp : row % p.hp + p.HC] = dw[m][t * p.HC : (t + 1) * p.HC].astype(BF)
    f1_copy = remote(A.at[:, 1 - core], f1, "f1", 0, (mate, z))
    f1_copy.start()

    dg = jnp.zeros((1, W), F32)
    for half in range(2):
        v = xs[half].astype(F32)
        dg += jnp.sum(dxn[half * R : (half + 1) * R] * (v * inv_rms(v)), axis=0, keepdims=True)
    rext32[0:1] = dg
    rext32[1:2] = sm_own
    rext32[2:16] = drext[...].T[0:14]
    smr[dp] = rext32[...].astype(BF)

    def small(j):
        there = lax.rem(dp + j, p.nd)
        return remote(smr.at[dp], smr.at[dp], "s1", j - 1, (there, z))

    for j in range(1, p.nd):
        small(j).start()

    f1_copy.wait_recv()
    for t in range(NT):
        A[t, core] = (A[t, core].astype(F32) + f1[t].astype(F32)).astype(BF)

    def f2_copy(j):
        return remote(A.at[:, core, chip_rows(j)], f2.at[j - 1], "f2", j - 1, on_chip(j))

    for j in range(1, p.nc):
        owner(chip_at(j))(lambda j=j: f2_copy(j).start())

    def f3_copy(k):
        return remote(fD.at[zk[k]], f3.at[k - 1], "f3", k - 1, to_z(k))

    @owns
    def _():
        for j in range(1, p.nc):
            f2_copy(j).wait_recv()
        for t in range(NT):
            v = A[t, core, chip_rows(0)].astype(F32)
            for j in range(1, p.nc):
                v += f2[j - 1, t].astype(F32)
            fD[t] = v.astype(BF)
        for k in (1, 2, 3):
            f3_copy(k).start()

    for j in range(1, p.nd):
        small(j).wait_recv()
    total = smr[0].astype(F32)
    for j in range(1, p.nd):
        total += smr[j].astype(F32)
    smz[z] = total

    def small_z(k):
        return remote(smz.at[z], smz.at[z], "s2", k - 1, to_z(k))

    for k in (1, 2, 3):
        small_z(k).start()
    def f4_copy(j):
        there = lax.rem(dp + j, p.nd)
        part = att.at[core, chip_rows(0)]
        return remote(part, part, "f4", j - 1, (there, z))

    @owns
    def _():
        for k in (1, 2, 3):
            f3_copy(k).wait_recv()
        v = fD[z].astype(F32)
        for k in (1, 2, 3):
            v += f3[k - 1].astype(F32)
        att[core, chip_rows(0)] = v.astype(BF)
        for j in range(1, p.nd):
            f4_copy(j).start()

    px_copy.wait_recv()
    dn = dxn[own_pos] + pxr[...].astype(F32)
    x_back, _ = rms_back(x_in[...].astype(F32), dn, gain_attn)
    din_ref[...] = dx_own[...] + x_back
    for k in (1, 2, 3):
        remote(cotg.at[zk[k]], outr.at[k - 1], "o", k - 1, to_z(k)).wait_recv()
    whole = mid[...] + (out_own[...] + outr[0].astype(F32) + outr[1].astype(F32) + outr[2].astype(F32))
    out_ref[...] = whole.astype(BF)

    for k in (1, 2, 3):
        small_z(k).wait_recv()
    sm_ref[...] = smz[0] + smz[1] + smz[2] + smz[3]

    def hand_all(b, carry):
        hand_over(b)
        return carry

    lax.fori_loop(0, p.NB, hand_all, 0)

    def mate_done(b, carry):
        for j in range(p.nc):
            owner(chip_at(j))(lambda j=j: h4_copy(b, j).wait_recv())
        return carry

    lax.fori_loop(0, p.NB, mate_done, 0)
    writes = [
        pltpu.make_async_copy(res.at[part, kind], out, lsem.at[i])
        for i, (part, kind, out) in enumerate(
            [
                (slice(0, p.EB), 0, eg_out),
                (slice(0, p.EB), 1, eu_out),
                (slice(0, p.EB), 2, ed_out),
                (slice(p.EB, p.NB), 0, sg_out),
                (slice(p.EB, p.NB), 1, su_out),
                (slice(p.EB, p.NB), 2, sd_out),
            ]
        )
    ]
    for c in writes:
        c.start()
    for j in range(1, p.nd):
        sender = lax.rem(dp + p.nd - j, p.nd)
        owner(lax.div(sender, 2))(lambda j=j: f4_copy(j).wait_recv())
    for c in range(2):
        att_ref[c * p.hp : (c + 1) * p.hp] = att[c]

    for k in (1, 2, 3):
        for i in range(4 // S):
            w_send(k, i).wait_send()
            for j in range(1, S):
                w_forward(k, i, j).wait_send()
        remote(normg.at[zk[k]], dxr.at[k - 1], "dx", k - 1, to_z(k)).wait_send()
        remote(cotg.at[zk[k]], outr.at[k - 1], "o", k - 1, to_z(k)).wait_send()
        small_z(k).wait_send()
    own_sent("c", cotg, 0, slice(None))
    for b in range(R // QB):
        own_sent("n", normg, b, halves[b])
    x_copy.wait_send()
    px_copy.wait_send()
    f1_copy.wait_send()
    for j in range(1, p.nc):
        owner(chip_at(j))(lambda j=j: f2_copy(j).wait_send())

    def sums_sent(b, carry):
        h1_copy(b).wait_send()
        for j in range(1, p.nc):
            owner(chip_at(j))(lambda j=j: h2_copy(b, j).wait_send())
            owns(lambda j=j: h3_copy(b, j).wait_send())
        for j in range(p.nc):
            owner(chip_at(j))(lambda j=j: h4_copy(b, j).wait_send())
        return carry

    lax.fori_loop(0, p.NB, sums_sent, 0)
    for j in range(1, p.nd):
        small(j).wait_send()

    @owns
    def _():
        for k in (1, 2, 3):
            f3_copy(k).wait_send()
        for j in range(1, p.nd):
            f4_copy(j).wait_send()

    for c in writes:
        c.wait()


def tables():
    half = HD // 2
    freqs = 10000.0 ** (-np.arange(half, dtype=np.float32) / np.float32(half))
    angles = np.arange(LEN, dtype=np.float32)[:, None] * freqs.astype(np.float32)[None, :]
    cosine, sine = np.cos(angles).astype(np.float32), np.sin(angles).astype(np.float32)
    reps = LANES // HD
    cos_wide = np.tile(np.concatenate([cosine, cosine], axis=1), (1, reps))
    sin_wide = np.tile(np.concatenate([-sine, sine], axis=1), (1, reps))
    return cos_wide, sin_wide, np.ascontiguousarray(cosine.T), np.ascontiguousarray(sine.T)


def per_device(
    nd,
    inputs,
    lengths,
    expert_ids,
    gain_attn,
    w_query,
    w_key,
    w_value,
    w_out,
    gain_ffn,
    router,
    shared_gate_vec,
    exp_gate,
    exp_up,
    exp_down,
    sh_gate,
    sh_up,
    sh_down,
    cotangent,
):
    R, W = inputs.shape
    experts, _, eff = exp_gate.shape
    ff = sh_gate.shape[1]
    p = Plan(nd, R, W, experts, eff, ff)
    number, names = sem_plan(p)
    eg = exp_gate.swapaxes(1, 2).reshape(p.EB, p.B, W)
    eu = exp_up.swapaxes(1, 2).reshape(p.EB, p.B, W)
    ed = exp_down.reshape(p.EB, p.B, W)
    cosk, sink, cost, sint = tables()
    vm = pl.BlockSpec(memory_space=pltpu.VMEM)
    hbm = pl.BlockSpec(memory_space=pl.ANY)
    V = pltpu.VMEM
    hc = W // HD
    scratch = [
        pltpu.SemaphoreType.DMA((number,)),
        pltpu.SemaphoreType.DMA((number,)),
        pltpu.SemaphoreType.DMA((8,)),
        V((4, W, W), BF),
        V((16, W), F32),
        V((LANES, W), BF),
        V((2, R, W), BF),
        V((LEN, W), BF),
        V((NT, R, W), BF),
        V((NT, R, W), BF),
        V((p.NB, W, p.B), BF),
        V((p.NB, W, p.B), BF),
        V((p.NB, p.B, W), BF),
        V((W, R), BF),
        V((p.NG, R, LANES), BF),
        V((p.NG, LEN, LANES), BF),
        V((W, LEN), BF),
        V((p.NG, LEN, LANES), BF),
        V((W, R), BF),
        V((up16(hc), R), F32),
        V((LEN, R), F32),
        V((R, W), F32),
        V((R, W), F32),
        V((R, W), F32),
        V((3, R, W), BF),
        V((3, R, W), BF),
        V((3 * p.NB * W, W), F32),
        V((W, LANES), F32),
        V((p.NB, 3, 2, p.hp, W), BF),
        V((p.NB, 3, p.hp, W), BF),
        V((max(p.nc - 1, 1), p.NB, 3, p.pr, W), BF),
        V((p.NB, 3, 2, p.hp, W), BF),
        V((R, W), BF),
        V((p.NG, R, LANES), BF),
        V((W, R), BF),
        V((up16(hc), R), F32),
        V((R, W), BF),
        V((NT, 2, p.hp, W), BF),
        V((NT, p.hp, W), BF),
        V((max(p.nc - 1, 1), NT, p.pr, W), BF),
        V((NT, p.pr, W), BF),
        V((3, p.pr, W), BF),
        V((2, p.hp, W), BF),
        V((nd, 16, W), BF),
        V((NT, 16, W), F32),
    ]
    routed = jax.ShapeDtypeStruct((p.EB, 2, p.hp, W), BF)
    shared = jax.ShapeDtypeStruct((1, 2, p.hp, W), BF)
    results = pl.pallas_call(
        functools.partial(kernel, p, names),
        out_shape=[
            jax.ShapeDtypeStruct((R, W), BF),
            jax.ShapeDtypeStruct((R, W), F32),
            routed,
            routed,
            routed,
            shared,
            shared,
            shared,
            jax.ShapeDtypeStruct((2 * p.hp, W), BF),
            jax.ShapeDtypeStruct((16, W), F32),
        ],
        in_specs=[pl.BlockSpec(memory_space=pltpu.SMEM)] + [vm] * 9 + [hbm] * 8 + [vm] * 4,
        out_specs=[vm, vm] + [hbm] * 6 + [vm, vm],
        scratch_shapes=scratch,
        compiler_params=pltpu.CompilerParams(collective_id=0, has_side_effects=True, vmem_limit_bytes=63 << 20),
        name="block",
    )(
        lengths,
        expert_ids.T,
        gain_attn[None],
        gain_ffn[None],
        router.T,
        shared_gate_vec[None],
        w_query.T,
        w_key.T,
        w_value.T,
        w_out,
        inputs,
        cotangent,
        eg,
        eu,
        ed,
        sh_gate,
        sh_up,
        sh_down,
        jnp.asarray(cosk),
        jnp.asarray(sink),
        jnp.asarray(cost),
        jnp.asarray(sint),
    )
    return widen(p, *results)


def widen_kernel(p, out_b, din, eg, eu, ed, sg, su, sd, att, small, *outs):
    (out_o, din_o, ga_o, wq_o, wk_o, wv_o, wo_o, gf_o, ro_o, ve_o, eg_o, eu_o, ed_o, sg_o, su_o, sd_o) = outs
    step = pl.program_id(0)
    for c in range(2):
        rows = slice(c * p.hp, (c + 1) * p.hp)
        for src, dst in ((eg, eg_o), (eu, eu_o), (ed, ed_o)):
            dst[0, rows] = src[0, c].astype(F32)

    @pl.when(step == 0)
    def _():
        out_o[...] = out_b[...]
        din_o[...] = din[...]
        for m, dst in enumerate((wq_o, wk_o, wv_o, wo_o)):
            dst[...] = att[m * p.HC : (m + 1) * p.HC].astype(F32)
        ga_o[...] = small[0:1]
        gf_o[...] = small[1:2]
        ro_o[...] = small[2 : 2 + p.E]
        ve_o[...] = small[2 + p.E : 3 + p.E] + small[3 + p.E : 4 + p.E]
        for c in range(2):
            rows = slice(c * p.hp, (c + 1) * p.hp)
            for src, dst in ((sg, sg_o), (su, su_o), (sd, sd_o)):
                dst[rows] = src[0, c].astype(F32)


def widen(p, *results):
    R, W = p.R, p.W

    def whole(shape):
        return pl.BlockSpec(shape, lambda i: (0,) * len(shape))

    def split(shape):
        return pl.BlockSpec((1,) + shape[1:], lambda i: (i,) + (0,) * (len(shape) - 1))

    blocks = (p.EB, 2, p.hp, W)
    routed = (p.EB, p.B, W)
    row, head, sh = (1, W), (p.HC, W), (W, W)
    shapes = [(R, W), (R, W), row, head, head, head, head, row, (p.E, W), row, routed, routed, routed, sh, sh, sh]
    out = pl.pallas_call(
        functools.partial(widen_kernel, p),
        grid=(p.EB,),
        out_shape=[jax.ShapeDtypeStruct(s, BF if i == 0 else F32) for i, s in enumerate(shapes)],
        in_specs=[whole((R, W))] * 2
        + [split(blocks)] * 3
        + [whole((1,) + blocks[1:])] * 3
        + [whole((2 * p.hp, W)), whole((16, W))],
        out_specs=[split(s) if s == routed else whole(s) for s in shapes],
        compiler_params=pltpu.CompilerParams(vmem_limit_bytes=48 << 20),
        name="widen",
    )(*results)
    out = list(out)
    for i in (2, 7, 9):
        out[i] = out[i][0]
    for i in (3, 4, 5, 8):
        out[i] = out[i].T
    for i in (10, 11, 12):
        out[i] = out[i].reshape(p.E, p.eff, W)
    for i in (10, 11):
        out[i] = out[i].swapaxes(1, 2)
    return tuple(out)


def solution(mesh):
    rows = P(("dp", "tensor"), None)
    cols = P(None, "tensor")
    deep = P(None, None, "tensor")
    weights = (cols, cols, cols, P("tensor", None))
    experts = (deep, deep, P(None, "tensor", None), cols, cols, P("tensor", None))
    in_specs = (rows, P("dp"), P("dp", None), P()) + weights + (P(), P(), P()) + experts + (rows,)
    out_specs = (rows, rows, P()) + weights + (P(), P(), P()) + experts
    return jax.shard_map(
        functools.partial(per_device, mesh.shape["dp"]),
        mesh=mesh,
        in_specs=in_specs,
        out_specs=out_specs,
        check_vma=False,
    )
```

```python
import functools

import jax
import jax.numpy as jnp
import numpy as np
from jax import lax
from jax.experimental import pallas as pl
from jax.experimental.pallas import tpu as pltpu
from jax.sharding import PartitionSpec as P

HD = 32
LEN = 1024
NT = 4
LANES = 128
QB = 256
TILE = 32
BF = jnp.bfloat16
F32 = jnp.float32
MESH = pl.DeviceIdType.MESH
NEG = -1e30
SCALE = HD**-0.5
LOG2E = 1.4426950408889634
LN2 = 0.6931471805599453


def nn(a, b):
    return lax.dot_general(a, b, (((1,), (0,)), ((), ())), preferred_element_type=F32)


def nt(a, b):
    return lax.dot_general(a, b, (((1,), (1,)), ((), ())), preferred_element_type=F32)


def inv_rms(v):
    return lax.rsqrt(jnp.mean(v * v, axis=-1, keepdims=True) + 1e-06)


def rms_back(v, grad, gain):
    r = inv_rms(v)
    u = v * r
    g = grad * gain
    return r * (g - u * jnp.mean(g * u, axis=-1, keepdims=True)), grad * u


def up16(n):
    return -(-n // 16) * 16


class Plan:
    def __init__(self, nd, rows, width, experts, eff, ff):
        self.nd, self.R, self.W = nd, rows, width
        self.G = NT * rows
        self.NG = width // LANES
        self.HC = width // NT
        self.B = 2 * eff
        self.EB = experts // 2
        self.NB = self.EB + 1
        assert ff == self.B == width and LEN == 2 * rows
        self.E, self.eff, self.ff = experts, eff, ff
        self.share = min(4, nd)
        self.nc = nd // 2
        self.hp = 2 * self.HC
        assert 2 * self.hp == width == self.B
        self.pr = max(16, self.hp // self.nc)
        self.owners = self.hp // self.pr
        assert self.owners * self.pr == self.hp and self.pr % 16 == 0 and self.owners <= self.nc


class Sems:
    def __init__(self):
        self.n = 0

    def take(self, n):
        base = self.n
        self.n += n
        return base


def sem_plan(p):
    s, names = Sems(), {}
    names["w"] = s.take(3 * (4 // p.share))
    names["f"] = s.take(3 * (4 // p.share) * max(p.share - 1, 1))
    names["x"] = s.take(1)
    for way in "rl":
        names["c" + way] = s.take(4)
        names["n" + way] = s.take(8)
    names["dx"] = s.take(3)
    names["o"] = s.take(3)
    names["h1"] = s.take(p.NB)
    names["h2"] = s.take(p.NB * max(p.nc - 1, 1))
    names["h3"] = s.take(p.NB * max(p.nc - 1, 1))
    names["h4"] = s.take(p.NB * p.nc)
    names["px"] = s.take(1)
    names["f1"] = s.take(1)
    names["f2"] = s.take(max(p.nc - 1, 1))
    names["f3"] = s.take(3)
    names["f4"] = s.take(p.nd - 1)
    names["s1"] = s.take(p.nd - 1)
    names["s2"] = s.take(3)
    return s.n, names


def kernel(
    p,
    names,
    len_ref,
    ids_ref,
    gain_attn_ref,
    gain_ffn_ref,
    router_ref,
    vec_ref,
    wq_ref,
    wk_ref,
    wv_ref,
    wo_ref,
    x_hbm,
    cot_hbm,
    eg_hbm,
    eu_hbm,
    ed_hbm,
    sg_hbm,
    su_hbm,
    sd_hbm,
    cosk,
    sink,
    cost,
    sint,
    out_ref,
    din_ref,
    att_ref,
    sm_ref,
    res,
    send,
    recv,
    lsem,
    wfull,
    rext32,
    rext,
    rextT,
    xs,
    xn,
    cotg,
    normg,
    wgu,
    wguT,
    wd,
    wdT,
    qT,
    qN,
    kN,
    kvT,
    vN,
    oT,
    lse,
    bias,
    mid,
    dx_own,
    out_own,
    dxr,
    outr,
    acc,
    drext,
    stage,
    h1,
    h2,
    fin,
    agrad,
    dON,
    dOT,
    delta,
    pxr,
    A,
    f1,
    f2,
    fD,
    f3,
    att,
    smr,
    smz,
):
    R, W, NG = p.R, p.W, p.NG
    dp, z = lax.axis_index("dp"), lax.axis_index("tensor")
    zlo = lax.rem(z, 2)
    zk = [z, z + 1 - 2 * zlo, lax.rem(z + 2, NT), NT - 1 - z]
    core = lax.rem(dp, 2)
    chip = lax.div(dp, 2)
    mate = dp + 1 - 2 * core
    half_own = zlo

    def remote(src, dst, kind, i, dev):
        j = names[kind] + i
        return pltpu.make_async_remote_copy(
            src_ref=src, dst_ref=dst, send_sem=send.at[j], recv_sem=recv.at[j], device_id=dev, device_id_type=MESH
        )

    def to_z(k):
        return (dp, zk[k])

    def chip_at(j):
        return lax.rem(chip + j, p.nc)

    def on_chip(j):
        return (2 * chip_at(j) + core, z)

    def hop(kind, buf, way, i, part, rows, at):
        there = (dp, z + 1) if way == "r" else (dp, z - 1)
        ref = buf.at[at, rows]
        parts = 1 if kind == "c" else R // QB
        return remote(ref, ref, kind + way, i * parts + part, there)

    def send_own(kind, buf, part, rows):
        @pl.when(z < NT - 1)
        def _():
            hop(kind, buf, "r", 0, part, rows, z).start()

        @pl.when(z > 0)
        def _():
            hop(kind, buf, "l", 0, part, rows, z).start()

    def own_sent(kind, buf, part, rows):
        @pl.when(z < NT - 1)
        def _():
            hop(kind, buf, "r", 0, part, rows, z).wait_send()

        @pl.when(z > 0)
        def _():
            hop(kind, buf, "l", 0, part, rows, z).wait_send()

    def arrive(kind, buf, i, part, rows):
        @pl.when(z - 1 - i >= 0)
        def _():
            hop(kind, buf, "r", i, part, rows, z - 1 - i).wait_recv()

            @pl.when(z < NT - 1)
            def _():
                hop(kind, buf, "r", i + 1, part, rows, z - 1 - i).start()

        @pl.when(z + 1 + i < NT)
        def _():
            hop(kind, buf, "l", i, part, rows, z + 1 + i).wait_recv()

            @pl.when(z > 0)
            def _():
                hop(kind, buf, "l", i + 1, part, rows, z + 1 + i).start()

    def handed_on(kind, buf, c, part, rows):
        @pl.when((c < z) & (z < NT - 1))
        def _():
            hop(kind, buf, "r", z - c, part, rows, c).wait_send()

        @pl.when((c > z) & (z > 0))
        def _():
            hop(kind, buf, "l", c - z, part, rows, c).wait_send()

    halves = [slice(i * QB, (i + 1) * QB) for i in range(R // QB)]

    V = pltpu.VMEM
    x_in, cot_in = xs.at[half_own], cotg.at[z]
    loads = [
        pltpu.make_async_copy(src, dst, lsem.at[i])
        for i, (src, dst) in enumerate(
            [
                (x_hbm, x_in),
                (cot_hbm, cot_in),
                (eg_hbm, wgu.at[: p.EB, : p.B]),
                (eu_hbm, wgu.at[: p.EB, p.B :]),
                (ed_hbm, wd.at[: p.EB]),
                (sg_hbm, wguT.at[p.EB, :, : p.B]),
                (su_hbm, wguT.at[p.EB, :, p.B :]),
                (sd_hbm, wd.at[p.EB]),
            ]
        )
    ]
    for c in loads:
        c.start()
    barrier = pltpu.get_barrier_semaphore()
    for k in (1, 2, 3):
        pl.semaphore_signal(barrier, inc=1, device_id=to_z(k), device_id_type=MESH)

    def greet(j, carry):
        pl.semaphore_signal(barrier, inc=1, device_id=(lax.rem(dp + j, p.nd), z), device_id_type=MESH)
        return carry

    lax.fori_loop(1, p.nd, greet, 0)
    pl.semaphore_wait(barrier, 3 + p.nd - 1)

    S = p.share
    member = lax.rem(dp, S)
    base = dp - member
    own_cols = pl.ds(pl.multiple_of(z * p.HC, 32), p.HC)

    def cols_of(k):
        return pl.ds(pl.multiple_of(zk[k] * p.HC, 32), p.HC)

    def w_send(k, i):
        m = member + S * i
        return remote(wfull.at[m, own_cols], wfull.at[m, own_cols], "w", (k - 1) * (4 // S) + i, to_z(k))

    def w_recv(k, i):
        m = member + S * i
        return remote(wfull.at[m, cols_of(k)], wfull.at[m, cols_of(k)], "w", (k - 1) * (4 // S) + i, to_z(k))

    def w_forward(k, i, j):
        m = member + S * i
        there = base + lax.rem(member + j, S)
        return remote(
            wfull.at[m, cols_of(k)],
            wfull.at[m, cols_of(k)],
            "f",
            ((k - 1) * (4 // S) + i) * (S - 1) + j - 1,
            (there, z),
        )

    for m, ref in enumerate((wq_ref, wk_ref, wv_ref, wo_ref)):
        wfull[m, own_cols] = ref[...]
    x_copy = remote(x_in, x_in, "x", 0, to_z(1))
    for k in (1, 2, 3):
        for i in range(4 // S):
            w_send(k, i).start()
    loads[0].wait()
    x_copy.start()
    gain_attn = gain_attn_ref[...].astype(F32)[None]
    gain_ffn = gain_ffn_ref[...].astype(F32)[None]
    rext32[0 : p.E] = router_ref[...].astype(F32)
    vec = vec_ref[...].astype(F32)[None]
    rext32[p.E : p.E + 1] = vec
    rext32[p.E + 1 : p.E + 2] = vec
    rext32[p.E + 2 :] = jnp.zeros((14 - p.E, W), F32)
    rext[...] = rext32[...].astype(BF)
    rextT[...] = jnp.concatenate([rext32[...], jnp.zeros((LANES - 16, W), F32)], axis=0).T.astype(BF)

    def mask_rows(i, carry):
        key = lax.broadcasted_iota(jnp.int32, (QB, R), 0) + i * QB
        query = lax.broadcasted_iota(jnp.int32, (QB, R), 1) + half_own * R
        length = len_ref[lax.div(z, 2)]
        bias[pl.ds(pl.multiple_of(i * QB, QB), QB)] = jnp.where((key <= query) & (key < length), 0.0, NEG)
        return carry

    lax.fori_loop(0, LEN // QB, mask_rows, 0)
    for k in (1, 2, 3):
        for i in range(4 // S):
            w_recv(k, i).wait_recv()
            for j in range(1, S):
                w_forward(k, i, j).start()

    for c in loads[1:]:
        c.wait()
    for i in range(2):
        at = slice(i * p.B, (i + 1) * p.B)
        wgu[p.EB, at] = wguT[p.EB, :, at].T

    def turn(b, carry):
        for i in range(2):
            at = slice(i * p.B, (i + 1) * p.B)
            wguT[b, :, at] = wgu[b, at].T
        wdT[b] = wd[b].T
        return carry

    lax.fori_loop(0, p.EB, turn, 0)
    wdT[p.EB] = wd[p.EB].T
    x_copy.wait_recv()
    send_own("c", cotg, 0, slice(None))

    def norm_half(i, carry):
        v = xs[i].astype(F32)
        xn[pl.ds(pl.multiple_of(i * R, R), R)] = (v * inv_rms(v) * gain_attn).astype(BF)
        return carry

    lax.fori_loop(0, 2, norm_half, 0)
    for k in (1, 2, 3):
        for i in range(4 // S):
            for j in range(1, S):
                w_forward(k, i, j).wait_recv()

    own_pos = pl.ds(pl.multiple_of(half_own * R, R), R)
    lane = lax.broadcasted_iota(jnp.int32, (1, LANES), 1)
    low_half = lax.rem(lane, HD) < HD // 2

    def swap_halves(v):
        return jnp.where(low_half, pltpu.roll(v, LANES - HD // 2, 1), pltpu.roll(v, HD // 2, 1))

    q_pre = nt(wfull[0], xn[own_pos])
    cos_own, sin_own = cost[:, own_pos], sint[:, own_pos]
    for h in range(W // HD):
        a = q_pre[h * HD : h * HD + HD // 2]
        b = q_pre[h * HD + HD // 2 : (h + 1) * HD]
        qT[h * HD : h * HD + HD // 2] = ((a * cos_own - b * sin_own) * (SCALE * LOG2E)).astype(BF)
        qT[h * HD + HD // 2 : (h + 1) * HD] = ((a * sin_own + b * cos_own) * (SCALE * LOG2E)).astype(BF)

    def project(i, carry):
        rows = pl.ds(pl.multiple_of(i * QB, QB), QB)
        xb = xn[rows]
        k_pre = nt(xb, wfull[1])
        v_pre = nt(xb, wfull[2])
        c, s = cosk[rows], sink[rows]
        for g in range(NG):
            kg = k_pre[:, g * LANES : (g + 1) * LANES]
            kN[g, rows] = (kg * c + swap_halves(kg) * s).astype(BF)
            vN[g, rows] = v_pre[:, g * LANES : (g + 1) * LANES].astype(BF)
        return carry

    lax.fori_loop(0, LEN // QB, project, 0)
    for g in range(NG):
        rows = slice(g * LANES, (g + 1) * LANES)
        kvT[rows] = vN[g].T
        qN[g] = qT[rows].T

    head_row = lax.div(lax.broadcasted_iota(jnp.int32, (LANES, 1), 0), HD)
    head_lane = lax.div(lane, HD)
    HPG = LANES // HD

    def scores(g, h, qb):
        qg = qT[pl.ds(pl.multiple_of(g * LANES, LANES), LANES), qb * QB : (qb + 1) * QB]
        masked = jnp.where(head_row == h, qg, jnp.zeros_like(qg))
        return nn(kN[g], masked) + bias[:, qb * QB : (qb + 1) * QB]

    for qb in range(R // QB):
        cols = slice(qb * QB, (qb + 1) * QB)

        def heads(g, carry):
            for h in range(HPG):
                s = scores(g, h, qb)
                top = jnp.max(s, axis=0, keepdims=True)
                e = jnp.exp2(s - top)
                total = jnp.sum(e, axis=0, keepdims=True)
                at = pl.ds(pl.multiple_of(g * LANES + h * HD, HD), HD)
                o = nn(kvT[at], e.astype(BF)) * (1.0 / total)
                oT[at, cols] = o.astype(BF)
                lse[pl.ds(g * HPG + h, 1), cols] = top + jnp.log(total) * LOG2E
            return carry

        lax.fori_loop(0, NG, heads, 0)
        rows = slice(qb * QB, (qb + 1) * QB)
        m = x_in[rows].astype(F32) + nn(oT[:, cols].T, wfull[3])
        mid[rows] = m
        normg[z, rows] = (m * inv_rms(m) * gain_ffn).astype(BF)
        if qb == 0:
            arrive("c", cotg, 0, 0, slice(None))
        send_own("n", normg, qb, rows)
    arrive("c", cotg, 1, 0, slice(None))
    for g in range(NG):
        kvT[g * LANES : (g + 1) * LANES] = kN[g].T

    def zero_acc(i, carry):
        acc[pl.ds(pl.multiple_of(i * 16, 16), 16)] = jnp.zeros((16, W), F32)
        return carry

    lax.fori_loop(0, 3 * p.NB * W // 16, zero_acc, 0)
    drext[...] = jnp.zeros_like(drext)
    zhi = lax.div(z, 2)

    def chunk_of(k):
        return 2 * lax.rem(zhi + lax.div(k, 2), 2) + lax.rem(zlo + lax.rem(k, 2), 2)

    def chip_rows(j):
        return pl.ds(pl.multiple_of(chip_at(j) * p.pr, 16), p.pr)

    def owner(c):
        return (lambda f: f()) if p.owners == p.nc else pl.when(c < p.owners)

    owns = owner(chip)

    def h1_copy(b):
        return remote(stage.at[b, :, 1 - core], h1.at[b], "h1", b, (mate, z))

    def h2_copy(b, j):
        i = b * (p.nc - 1) + j - 1
        return remote(stage.at[b, :, core, chip_rows(j)], h2.at[j - 1, b], "h2", i, on_chip(j))

    def h3_copy(b, j):
        i = b * (p.nc - 1) + j - 1
        return remote(fin.at[b], res.at[b, :, core, chip_rows(0)], "h3", i, on_chip(j))

    def h4_copy(b, j):
        part = res.at[b, :, core, chip_rows(j)]
        return remote(fin.at[b] if j == 0 else part, part, "h4", b * p.nc + j, (mate, z))

    def keep(b):
        return pltpu.make_async_copy(fin.at[b], res.at[b, :, core, chip_rows(0)], lsem.at[b])

    def mate_half(b):
        for kind in range(3):
            v = acc[pl.ds(pl.multiple_of((3 * b + kind) * W, W), W)].astype(BF)
            stage[b, kind, 0] = v[: p.hp]
            stage[b, kind, 1] = v[p.hp :]

        @pl.when(b == p.EB)
        def _():
            for kind in range(2):
                v = acc[(3 * p.EB + kind) * W : (3 * p.EB + kind + 1) * W].astype(BF).T
                stage[b, kind, 0] = v[: p.hp]
                stage[b, kind, 1] = v[p.hp :]

        h1_copy(b).start()

    def to_chips(b):
        h1_copy(b).wait_recv()
        for kind in range(3):
            stage[b, kind, core] = (stage[b, kind, core].astype(F32) + h1[b, kind].astype(F32)).astype(BF)
        for j in range(1, p.nc):
            owner(chip_at(j))(lambda j=j: h2_copy(b, j).start())

    def from_chips(b):
        @owns
        def _():
            for j in range(1, p.nc):
                h2_copy(b, j).wait_recv()
            for kind in range(3):
                v = stage[b, kind, core, chip_rows(0)].astype(F32)
                for j in range(1, p.nc):
                    v += h2[j - 1, b, kind].astype(F32)
                fin[b, kind] = v.astype(BF)
            for j in range(1, p.nc):
                h3_copy(b, j).start()
            h4_copy(b, 0).start()
            keep(b).start()

    def hand_over(b):
        for j in range(1, p.nc):
            sender = lax.rem(chip + p.nc - j, p.nc)

            @owner(sender)
            def _(j=j):
                h3_copy(b, j).wait_recv()
                h4_copy(b, p.nc - j).start()

    def unit(gates, xT, gT, out_acc, dx_acc, k, carry):
        c = chunk_of(k)

        xT[...] = normg[c].T
        gT[...] = cotg[c].T
        logits = nn(rext[...], xT[...])
        down = lax.broadcasted_iota(jnp.int32, (16, R), 0)
        is_expert = down < p.E
        lg = jnp.where(is_expert, logits, NEG)
        ex = jnp.exp(lg - jnp.max(lg, axis=0, keepdims=True))
        route = ex / jnp.sum(ex, axis=0, keepdims=True)
        at = pl.ds(pl.multiple_of(c * R, R), R)
        named = (down == ids_ref[0:1, at]) | (down == ids_ref[1:2, at]) | ((down >= p.E) & (down < p.E + 2))
        chosen = jnp.where(named, 1.0, 0.0)
        gate = jnp.where(is_expert, route, lax.logistic(logits)) * chosen
        gates[0] = chosen
        gates[1] = route
        gates[2] = gate
        gates[3] = jnp.zeros_like(gate)
        out_acc[...] = jnp.zeros_like(out_acc)
        dx_acc[...] = jnp.zeros_like(dx_acc)

        def block(b, carry):
            @pl.when((b == 0) & (k < NT - 1))
            def _():
                arrive("n", normg, k, 0, halves[0])

            @pl.when((b == 3) & (k < NT - 1))
            def _():
                arrive("n", normg, k, 1, halves[1])

            @pl.when((b == 1) & (k == 1))
            def _():
                arrive("c", cotg, 2, 0, slice(None))

            au = nn(wgu[b], xT[...])
            hg = nn(wd[b], gT[...])
            h_parts, a_parts, u_parts = [], [], []
            for e in range(2):
                expert = pl.ds(2 * b + e, 1)
                gc = gates[2, expert]
                sums = 0.0
                for first in range(e * p.eff, (e + 1) * p.eff, TILE):
                    rows = slice(first, first + TILE)
                    a, u, back = au[rows], au[p.B + first : p.B + first + TILE], hg[rows]
                    sig = 0.5 * jnp.tanh(0.5 * a) + 0.5
                    act = a * sig
                    slope = sig + act * (1.0 - sig)
                    h = act * u
                    sums += jnp.sum((h * back).reshape(TILE // 8, 8, R), axis=0)
                    scaled = back * gc
                    h_parts.append((h * gc).astype(BF))
                    a_parts.append((scaled * u * slope).astype(BF))
                    u_parts.append((scaled * act).astype(BF))
                gates[3, expert] = jnp.sum(sums, axis=0, keepdims=True)
            hs = jnp.concatenate(h_parts, axis=0)
            dau = jnp.concatenate(a_parts + u_parts, axis=0)
            out_acc[...] += nn(wdT[b], hs)
            dx_acc[...] += nn(wguT[b], dau)
            acc[pl.ds(pl.multiple_of(3 * b * W, W), 2 * W)] += nn(dau, normg[c])
            acc[pl.ds(pl.multiple_of((3 * b + 2) * W, W), W)] += nn(hs, cotg[c])

            @pl.when(k == NT - 1)
            def _():
                mate_half(b)

                @pl.when(b > 0)
                def _():
                    to_chips(b - 1)

            return carry

        lax.fori_loop(0, p.NB, block, 0)
        chosen, route, gate = gates[0], gates[1], gates[2]
        rg = gates[3] * chosen
        dot = jnp.sum(jnp.where(is_expert, route * rg, 0.0), axis=0, keepdims=True)
        lgrad = jnp.where(is_expert, route * (rg - dot), rg * gate * (1.0 - gate))
        drext[...] += nn(lgrad.astype(BF), normg[c])
        lwide = jnp.concatenate([lgrad, jnp.zeros((LANES - 16, R), F32)], axis=0).astype(BF)
        dx = dx_acc[...] + nn(rextT[...], lwide)
        for b in range(R // QB):
            handed_on("n", normg, c, b, halves[b])
        handed_on("c", cotg, c, 0, slice(None))

        @pl.when(k == 0)
        def _():
            dx_own[...] = dx.T
            out_own[...] = out_acc[...].T

        @pl.when(k > 0)
        def _():
            normg[c] = dx.astype(BF).T
            cotg[c] = out_acc[...].astype(BF).T
            remote(normg.at[c], dxr.at[k - 1], "dx", k - 1, (dp, c)).start()

        return carry

    def chunks(gates, xT, gT, out_acc, dx_acc):
        lax.fori_loop(0, NT, functools.partial(unit, gates, xT, gT, out_acc, dx_acc), 0)

    pl.run_scoped(chunks, V((4, 16, R), F32), V((W, R), BF), V((W, R), BF), V((W, R), F32), V((W, R), F32))

    to_chips(p.NB - 1)

    for k in (1, 2, 3):
        remote(normg.at[zk[k]], dxr.at[k - 1], "dx", k - 1, to_z(k)).wait_recv()
    for k in (1, 2, 3):
        remote(cotg.at[zk[k]], outr.at[k - 1], "o", k - 1, to_z(k)).start()
    dn = dx_own[...] + dxr[0].astype(F32) + dxr[1].astype(F32) + dxr[2].astype(F32)
    mid_back, dgain = rms_back(mid[...], dn, gain_ffn)
    sm_own = jnp.sum(dgain, axis=0, keepdims=True)
    mg = cot_in[...].astype(F32) + mid_back
    dx_own[...] = mg
    ag = mg.astype(BF)
    agrad[...] = ag
    dO = nt(ag, wfull[3])
    for g in range(NG):
        dON[g] = dO[:, g * LANES : (g + 1) * LANES].astype(BF)
    dOt = nt(wfull[3], ag).astype(BF)
    dOT[...] = dOt
    both = dOt.astype(F32) * oT[...].astype(F32)
    for h in range(W // HD):
        delta[h : h + 1] = jnp.sum(both[h * HD : (h + 1) * HD], axis=0, keepdims=True)

    dw = [acc.at[m * W : (m + 1) * W] for m in range(4)]
    dxn = acc.at[4 * W : 4 * W + LEN]
    dw[3][...] = nn(oT[...], agrad[...])
    dxn[...] = jnp.zeros_like(dxn)

    def back_group(pT, dsT, dk_acc, dv_acc, dqT, g, carry):
        def chips(b, carry):
            from_chips(b)
            return carry

        lax.fori_loop(2 * g, jnp.minimum(2 * g + 2, p.NB), chips, 0)
        at_g = pl.ds(pl.multiple_of(g * LANES, LANES), LANES)
        for qb in range(R // QB):
            cols = slice(qb * QB, (qb + 1) * QB)
            for h in range(HPG):
                s = scores(g, h, qb)
                prob = jnp.exp2(s - lse[pl.ds(g * HPG + h, 1), cols])
                og = dOT[at_g, cols]
                d_prob = nn(vN[g], jnp.where(head_row == h, og, jnp.zeros_like(og)))
                ds = (prob * (d_prob - delta[pl.ds(g * HPG + h, 1), cols])).astype(BF)
                pT[:, h * QB : (h + 1) * QB] = prob.astype(BF)
                dsT[:, h * QB : (h + 1) * QB] = ds
                at = pl.ds(pl.multiple_of(g * LANES + h * HD, HD), HD)
                dqT[h * HD : (h + 1) * HD, cols] = nn(kvT[at], ds) * SCALE
            og, qg = dON[g, cols], qN[g, cols]
            o_heads = jnp.concatenate([jnp.where(head_lane == h, og, jnp.zeros_like(og)) for h in range(HPG)], axis=0)
            q_heads = jnp.concatenate([jnp.where(head_lane == h, qg, jnp.zeros_like(qg)) for h in range(HPG)], axis=0)
            dv = nn(pT[...], o_heads)
            dk = nn(dsT[...], q_heads) * LN2
            if qb == 0:
                dv_acc[...] = dv
                dk_acc[...] = dk
            else:
                dv_acc[...] += dv
                dk_acc[...] += dk
        dv = dv_acc[...].astype(BF)
        dk = dk_acc[...]
        dk = (dk * cosk[...] - swap_halves(dk) * sink[...]).astype(BF)
        parts = []
        for h in range(HPG):
            a = dqT[h * HD : h * HD + HD // 2]
            b = dqT[h * HD + HD // 2 : (h + 1) * HD]
            parts += [a * cos_own + b * sin_own, b * cos_own - a * sin_own]
        dq = jnp.concatenate(parts, axis=0).astype(BF)
        dw[0][at_g] = nn(dq, xn[own_pos])
        dw[1][at_g] = nn(dk.T, xn[...])
        dw[2][at_g] = nn(dv.T, xn[...])
        dxn[...] += nn(dk, wfull[1, at_g]) + nn(dv, wfull[2, at_g])
        dxn[own_pos] += nn(dq.T, wfull[0, at_g])
        return carry

    def back(pT, dsT, dk_acc, dv_acc, dqT):
        lax.fori_loop(0, NG, functools.partial(back_group, pT, dsT, dk_acc, dv_acc, dqT), 0)

    wide = V((LEN, HPG * QB), BF)
    pl.run_scoped(back, wide, wide, V((LEN, LANES), F32), V((LEN, LANES), F32), V((LANES, R), F32))

    pxs = agrad
    pxs[...] = dxn[pl.ds(pl.multiple_of((1 - half_own) * R, R), R)].astype(BF)
    px_copy = remote(pxs, pxr, "px", 0, to_z(1))
    px_copy.start()

    for t in range(NT):
        for m in range(4):
            row = m * p.HC
            A[t, row // p.hp, row % p.hp : row % p.hp + p.HC] = dw[m][t * p.HC : (t + 1) * p.HC].astype(BF)
    f1_copy = remote(A.at[:, 1 - core], f1, "f1", 0, (mate, z))
    f1_copy.start()

    dg = jnp.zeros((1, W), F32)
    for half in range(2):
        v = xs[half].astype(F32)
        dg += jnp.sum(dxn[half * R : (half + 1) * R] * (v * inv_rms(v)), axis=0, keepdims=True)
    rext32[0:1] = dg
    rext32[1:2] = sm_own
    rext32[2:16] = drext[0:14]
    smr[dp] = rext32[...].astype(BF)

    def small(j):
        there = lax.rem(dp + j, p.nd)
        return remote(smr.at[dp], smr.at[dp], "s1", j - 1, (there, z))

    for j in range(1, p.nd):
        small(j).start()

    f1_copy.wait_recv()
    for t in range(NT):
        A[t, core] = (A[t, core].astype(F32) + f1[t].astype(F32)).astype(BF)

    def f2_copy(j):
        return remote(A.at[:, core, chip_rows(j)], f2.at[j - 1], "f2", j - 1, on_chip(j))

    for j in range(1, p.nc):
        owner(chip_at(j))(lambda j=j: f2_copy(j).start())

    def f3_copy(k):
        return remote(fD.at[zk[k]], f3.at[k - 1], "f3", k - 1, to_z(k))

    @owns
    def _():
        for j in range(1, p.nc):
            f2_copy(j).wait_recv()
        for t in range(NT):
            v = A[t, core, chip_rows(0)].astype(F32)
            for j in range(1, p.nc):
                v += f2[j - 1, t].astype(F32)
            fD[t] = v.astype(BF)
        for k in (1, 2, 3):
            f3_copy(k).start()

    for j in range(1, p.nd):
        small(j).wait_recv()
    total = smr[0].astype(F32)
    for j in range(1, p.nd):
        total += smr[j].astype(F32)
    smz[z] = total

    def small_z(k):
        return remote(smz.at[z], smz.at[z], "s2", k - 1, to_z(k))

    for k in (1, 2, 3):
        small_z(k).start()
    def f4_copy(j):
        there = lax.rem(dp + j, p.nd)
        part = att.at[core, chip_rows(0)]
        return remote(part, part, "f4", j - 1, (there, z))

    @owns
    def _():
        for k in (1, 2, 3):
            f3_copy(k).wait_recv()
        v = fD[z].astype(F32)
        for k in (1, 2, 3):
            v += f3[k - 1].astype(F32)
        att[core, chip_rows(0)] = v.astype(BF)
        for j in range(1, p.nd):
            f4_copy(j).start()

    px_copy.wait_recv()
    dn = dxn[own_pos] + pxr[...].astype(F32)
    x_back, _ = rms_back(x_in[...].astype(F32), dn, gain_attn)
    din_ref[...] = dx_own[...] + x_back
    for k in (1, 2, 3):
        remote(cotg.at[zk[k]], outr.at[k - 1], "o", k - 1, to_z(k)).wait_recv()
    whole = mid[...] + (out_own[...] + outr[0].astype(F32) + outr[1].astype(F32) + outr[2].astype(F32))
    out_ref[...] = whole.astype(BF)

    for k in (1, 2, 3):
        small_z(k).wait_recv()
    sm_ref[...] = smz[0] + smz[1] + smz[2] + smz[3]

    def hand_all(b, carry):
        hand_over(b)
        return carry

    lax.fori_loop(0, p.NB, hand_all, 0)

    def mate_done(b, carry):
        for j in range(p.nc):
            owner(chip_at(j))(lambda j=j: h4_copy(b, j).wait_recv())
        return carry

    lax.fori_loop(0, p.NB, mate_done, 0)
    for j in range(1, p.nd):
        sender = lax.rem(dp + p.nd - j, p.nd)
        owner(lax.div(sender, 2))(lambda j=j: f4_copy(j).wait_recv())
    for c in range(2):
        att_ref[c * p.hp : (c + 1) * p.hp] = att[c]

    for k in (1, 2, 3):
        for i in range(4 // S):
            w_send(k, i).wait_send()
            for j in range(1, S):
                w_forward(k, i, j).wait_send()
        remote(normg.at[zk[k]], dxr.at[k - 1], "dx", k - 1, to_z(k)).wait_send()
        remote(cotg.at[zk[k]], outr.at[k - 1], "o", k - 1, to_z(k)).wait_send()
        small_z(k).wait_send()
    own_sent("c", cotg, 0, slice(None))
    for b in range(R // QB):
        own_sent("n", normg, b, halves[b])
    x_copy.wait_send()
    px_copy.wait_send()
    f1_copy.wait_send()
    for j in range(1, p.nc):
        owner(chip_at(j))(lambda j=j: f2_copy(j).wait_send())

    def sums_sent(b, carry):
        h1_copy(b).wait_send()
        for j in range(1, p.nc):
            owner(chip_at(j))(lambda j=j: h2_copy(b, j).wait_send())
            owns(lambda j=j: h3_copy(b, j).wait_send())
        owns(lambda: keep(b).wait())
        for j in range(p.nc):
            owner(chip_at(j))(lambda j=j: h4_copy(b, j).wait_send())
        return carry

    lax.fori_loop(0, p.NB, sums_sent, 0)
    for j in range(1, p.nd):
        small(j).wait_send()

    @owns
    def _():
        for k in (1, 2, 3):
            f3_copy(k).wait_send()
        for j in range(1, p.nd):
            f4_copy(j).wait_send()


def tables():
    half = HD // 2
    freqs = 10000.0 ** (-np.arange(half, dtype=np.float32) / np.float32(half))
    angles = np.arange(LEN, dtype=np.float32)[:, None] * freqs.astype(np.float32)[None, :]
    cosine, sine = np.cos(angles).astype(np.float32), np.sin(angles).astype(np.float32)
    reps = LANES // HD
    cos_wide = np.tile(np.concatenate([cosine, cosine], axis=1), (1, reps))
    sin_wide = np.tile(np.concatenate([-sine, sine], axis=1), (1, reps))
    return cos_wide, sin_wide, np.ascontiguousarray(cosine.T), np.ascontiguousarray(sine.T)


def per_device(
    nd,
    inputs,
    lengths,
    expert_ids,
    gain_attn,
    w_query,
    w_key,
    w_value,
    w_out,
    gain_ffn,
    router,
    shared_gate_vec,
    exp_gate,
    exp_up,
    exp_down,
    sh_gate,
    sh_up,
    sh_down,
    cotangent,
):
    R, W = inputs.shape
    experts, _, eff = exp_gate.shape
    ff = sh_gate.shape[1]
    p = Plan(nd, R, W, experts, eff, ff)
    number, names = sem_plan(p)
    eg = exp_gate.swapaxes(1, 2).reshape(p.EB, p.B, W)
    eu = exp_up.swapaxes(1, 2).reshape(p.EB, p.B, W)
    ed = exp_down.reshape(p.EB, p.B, W)
    cosk, sink, cost, sint = tables()
    vm = pl.BlockSpec(memory_space=pltpu.VMEM)
    hbm = pl.BlockSpec(memory_space=pl.ANY)
    V = pltpu.VMEM
    hc = W // HD
    scratch = [
        pltpu.SemaphoreType.DMA((number,)),
        pltpu.SemaphoreType.DMA((number,)),
        pltpu.SemaphoreType.DMA((8,)),
        V((4, W, W), BF),
        V((16, W), F32),
        V((16, W), BF),
        V((W, LANES), BF),
        V((2, R, W), BF),
        V((LEN, W), BF),
        V((NT, R, W), BF),
        V((NT, R, W), BF),
        V((p.NB, 2 * p.B, W), BF),
        V((p.NB, W, 2 * p.B), BF),
        V((p.NB, p.B, W), BF),
        V((p.NB, W, p.B), BF),
        V((W, R), BF),
        V((p.NG, R, LANES), BF),
        V((p.NG, LEN, LANES), BF),
        V((W, LEN), BF),
        V((p.NG, LEN, LANES), BF),
        V((W, R), BF),
        V((up16(hc), R), F32),
        V((LEN, R), F32),
        V((R, W), F32),
        V((R, W), F32),
        V((R, W), F32),
        V((3, R, W), BF),
        V((3, R, W), BF),
        V((3 * p.NB * W, W), F32),
        V((16, W), F32),
        V((p.NB, 3, 2, p.hp, W), BF),
        V((p.NB, 3, p.hp, W), BF),
        V((max(p.nc - 1, 1), p.NB, 3, p.pr, W), BF),
        V((p.NB, 3, p.pr, W), BF),
        V((R, W), BF),
        V((p.NG, R, LANES), BF),
        V((W, R), BF),
        V((up16(hc), R), F32),
        V((R, W), BF),
        V((NT, 2, p.hp, W), BF),
        V((NT, p.hp, W), BF),
        V((max(p.nc - 1, 1), NT, p.pr, W), BF),
        V((NT, p.pr, W), BF),
        V((3, p.pr, W), BF),
        V((2, p.hp, W), BF),
        V((nd, 16, W), BF),
        V((NT, 16, W), F32),
    ]
    results = pl.pallas_call(
        functools.partial(kernel, p, names),
        out_shape=[
            jax.ShapeDtypeStruct((R, W), BF),
            jax.ShapeDtypeStruct((R, W), F32),
            jax.ShapeDtypeStruct((2 * p.hp, W), BF),
            jax.ShapeDtypeStruct((16, W), F32),
            jax.ShapeDtypeStruct((p.NB, 3, 2, p.hp, W), BF),
        ],
        in_specs=[pl.BlockSpec(memory_space=pltpu.SMEM)] + [vm] * 9 + [hbm] * 8 + [vm] * 4,
        out_specs=[vm] * 4 + [hbm],
        scratch_shapes=scratch,
        compiler_params=pltpu.CompilerParams(collective_id=0, has_side_effects=True, vmem_limit_bytes=63 << 20),
        name="block",
    )(
        lengths,
        expert_ids.T,
        gain_attn,
        gain_ffn,
        router.T,
        shared_gate_vec,
        w_query.T,
        w_key.T,
        w_value.T,
        w_out,
        inputs,
        cotangent,
        eg,
        eu,
        ed,
        sh_gate,
        sh_up,
        sh_down,
        jnp.asarray(cosk),
        jnp.asarray(sink),
        jnp.asarray(cost),
        jnp.asarray(sint),
    )
    return widen(p, *results)


def widen_kernel(p, out_b, din, att, small, routed, shared, *outs):
    (out_o, din_o, ga_o, wq_o, wk_o, wv_o, wo_o, gf_o, ro_o, ve_o, eg_o, eu_o, ed_o, sg_o, su_o, sd_o) = outs
    step = pl.program_id(0)
    for c in range(2):
        rows = slice(c * p.hp, (c + 1) * p.hp)
        for kind, dst in enumerate((eg_o, eu_o, ed_o)):
            dst[0, rows] = routed[0, kind, c].astype(F32)

    @pl.when(step == 0)
    def _():
        out_o[...] = out_b[...]
        din_o[...] = din[...]
        for m, dst in enumerate((wq_o, wk_o, wv_o, wo_o)):
            dst[...] = att[m * p.HC : (m + 1) * p.HC].astype(F32)
        ga_o[...] = small[0]
        gf_o[...] = small[1]
        ro_o[...] = small[2 : 2 + p.E]
        ve_o[...] = small[2 + p.E] + small[3 + p.E]
        for c in range(2):
            rows = slice(c * p.hp, (c + 1) * p.hp)
            for kind, dst in enumerate((sg_o, su_o, sd_o)):
                dst[rows] = shared[0, kind, c].astype(F32)


def widen(p, *results):
    R, W = p.R, p.W

    def whole(shape):
        return pl.BlockSpec(shape, lambda i: (0,) * len(shape))

    def split(shape):
        return pl.BlockSpec((1,) + shape[1:], lambda i: (i,) + (0,) * (len(shape) - 1))

    block = (1, 3, 2, p.hp, W)
    routed = (p.EB, p.B, W)
    row, head, sh = (W,), (p.HC, W), (W, W)
    shapes = [(R, W), (R, W), row, head, head, head, head, row, (p.E, W), row, routed, routed, routed, sh, sh, sh]
    out = pl.pallas_call(
        functools.partial(widen_kernel, p),
        grid=(p.EB,),
        out_shape=[jax.ShapeDtypeStruct(s, BF if i == 0 else F32) for i, s in enumerate(shapes)],
        in_specs=[whole((R, W))] * 2
        + [whole((2 * p.hp, W)), whole((16, W))]
        + [pl.BlockSpec(block, lambda i: (i, 0, 0, 0, 0)), pl.BlockSpec(block, lambda i: (p.EB, 0, 0, 0, 0))],
        out_specs=[split(s) if s == routed else whole(s) for s in shapes],
        compiler_params=pltpu.CompilerParams(vmem_limit_bytes=63 << 20),
        name="widen",
    )(*results, results[-1])
    out = list(out)
    for i in (3, 4, 5, 8):
        out[i] = out[i].T
    for i in (10, 11, 12):
        out[i] = out[i].reshape(p.E, p.eff, W)
    for i in (10, 11):
        out[i] = out[i].swapaxes(1, 2)
    return tuple(out)


def solution(mesh):
    rows = P(("dp", "tensor"), None)
    cols = P(None, "tensor")
    deep = P(None, None, "tensor")
    weights = (cols, cols, cols, P("tensor", None))
    experts = (deep, deep, P(None, "tensor", None), cols, cols, P("tensor", None))
    in_specs = (rows, P("dp"), P("dp", None), P()) + weights + (P(), P(), P()) + experts + (rows,)
    out_specs = (rows, rows, P()) + weights + (P(), P(), P()) + experts
    return jax.shard_map(
        functools.partial(per_device, mesh.shape["dp"]),
        mesh=mesh,
        in_specs=in_specs,
        out_specs=out_specs,
        check_vma=False,
    )
```

```python
import functools

import jax
import jax.numpy as jnp
import numpy as np
from jax import lax
from jax.experimental import pallas as pl
from jax.experimental.pallas import tpu as pltpu
from jax.sharding import PartitionSpec as P

HD = 32
LEN = 1024
NT = 4
LANES = 128
QB = 256
TILE = 32
BF = jnp.bfloat16
F32 = jnp.float32
MESH = pl.DeviceIdType.MESH
NEG = -1e30
SCALE = HD**-0.5
LOG2E = 1.4426950408889634
LN2 = 0.6931471805599453


def nn(a, b):
    return lax.dot_general(a, b, (((1,), (0,)), ((), ())), preferred_element_type=F32)


def nt(a, b):
    return lax.dot_general(a, b, (((1,), (1,)), ((), ())), preferred_element_type=F32)


def inv_rms(v):
    return lax.rsqrt(jnp.mean(v * v, axis=-1, keepdims=True) + 1e-06)


def rms_back(v, grad, gain):
    r = inv_rms(v)
    u = v * r
    g = grad * gain
    return r * (g - u * jnp.mean(g * u, axis=-1, keepdims=True)), grad * u


def up16(n):
    return -(-n // 16) * 16


class Plan:
    def __init__(self, nd, rows, width, experts, eff, ff):
        self.nd, self.R, self.W = nd, rows, width
        self.G = NT * rows
        self.NG = width // LANES
        self.HC = width // NT
        self.B = 2 * eff
        self.EB = experts // 2
        self.NB = self.EB + 1
        assert ff == self.B == width and LEN == 2 * rows
        self.E, self.eff, self.ff = experts, eff, ff
        assert nd % 8 == 0
        self.nc = nd // 2
        self.hp = 2 * self.HC
        assert 2 * self.hp == width == self.B
        self.pr = max(16, self.hp // self.nc)
        self.owners = self.hp // self.pr
        self.att_owners = LANES // 32
        assert self.owners * self.pr == self.hp and self.pr % 16 == 0 and self.owners <= self.nc


class Sems:
    def __init__(self):
        self.n = 0

    def take(self, n):
        base = self.n
        self.n += n
        return base


def sem_plan(p):
    s, names = Sems(), {}
    names["w"] = s.take(3)
    names["f"] = s.take(9)
    names["g"] = s.take(12)
    names["x"] = s.take(1)
    for way in "rl":
        names["c" + way] = s.take(4)
        names["n" + way] = s.take(8)
    names["dx"] = s.take(4)
    names["o"] = s.take(3)
    names["h1"] = s.take(p.NB)
    names["h2"] = s.take(p.NB * max(p.nc - 1, 1))
    names["h3"] = s.take(p.NB * max(p.nc - 1, 1))
    names["h4"] = s.take(p.NB * p.nc)
    names["px"] = s.take(1)
    names["f1"] = s.take(p.NG)
    names["f2"] = s.take(p.NG * (p.nc - 1))
    names["f3"] = s.take(p.NG * NT)
    names["f4"] = s.take(p.NG * (p.nd - 1))
    names["s1"] = s.take(p.nd - 1)
    names["s2"] = s.take(3)
    return s.n, names


def kernel(
    p,
    names,
    len_ref,
    ids_ref,
    gain_attn_ref,
    gain_ffn_ref,
    router_ref,
    vec_ref,
    wq_ref,
    wk_ref,
    wv_ref,
    wo_ref,
    x_hbm,
    cot_hbm,
    eg_hbm,
    eu_hbm,
    ed_hbm,
    sg_hbm,
    su_hbm,
    sd_hbm,
    cosk,
    sink,
    cost,
    sint,
    out_ref,
    din_ref,
    att_ref,
    sm_ref,
    res,
    send,
    recv,
    lsem,
    wfull,
    rext32,
    rext,
    rextT,
    xs,
    xn,
    cotg,
    normg,
    wgu,
    wguT,
    wd,
    wdT,
    qT,
    qN,
    kN,
    kvT,
    vN,
    oT,
    lse,
    bias,
    o_acc,
    mid,
    dx_own,
    out_own,
    dxr,
    outr,
    acc,
    drext,
    stage,
    h1,
    h2,
    fin,
    agrad,
    dON,
    dOT,
    delta,
    A,
    f1,
    f2,
    fD,
    f3,
    att,
    smr,
    smz,
):
    R, W, NG = p.R, p.W, p.NG
    dp, z = lax.axis_index("dp"), lax.axis_index("tensor")
    zlo = lax.rem(z, 2)
    zk = [z, z + 1 - 2 * zlo, lax.rem(z + 2, NT), NT - 1 - z]
    core = lax.rem(dp, 2)
    chip = lax.div(dp, 2)
    mate = dp + 1 - 2 * core
    half_own = zlo

    def remote(src, dst, kind, i, dev):
        j = names[kind] + i
        return pltpu.make_async_remote_copy(
            src_ref=src, dst_ref=dst, send_sem=send.at[j], recv_sem=recv.at[j], device_id=dev, device_id_type=MESH
        )

    def to_z(k):
        return (dp, zk[k])

    def chip_at(j):
        return lax.rem(chip + j, p.nc)

    def on_chip(j):
        return (2 * chip_at(j) + core, z)

    def hop(kind, buf, way, i, part, rows, at):
        there = (dp, z + 1) if way == "r" else (dp, z - 1)
        ref = buf.at[at, rows]
        parts = 1 if kind == "c" else R // QB
        return remote(ref, ref, kind + way, i * parts + part, there)

    def send_own(kind, buf, part, rows):
        @pl.when(z < NT - 1)
        def _():
            hop(kind, buf, "r", 0, part, rows, z).start()

        @pl.when(z > 0)
        def _():
            hop(kind, buf, "l", 0, part, rows, z).start()

    def own_sent(kind, buf, part, rows):
        @pl.when(z < NT - 1)
        def _():
            hop(kind, buf, "r", 0, part, rows, z).wait_send()

        @pl.when(z > 0)
        def _():
            hop(kind, buf, "l", 0, part, rows, z).wait_send()

    def arrive(kind, buf, i, part, rows):
        @pl.when(z - 1 - i >= 0)
        def _():
            hop(kind, buf, "r", i, part, rows, z - 1 - i).wait_recv()

            @pl.when(z < NT - 1)
            def _():
                hop(kind, buf, "r", i + 1, part, rows, z - 1 - i).start()

        @pl.when(z + 1 + i < NT)
        def _():
            hop(kind, buf, "l", i, part, rows, z + 1 + i).wait_recv()

            @pl.when(z > 0)
            def _():
                hop(kind, buf, "l", i + 1, part, rows, z + 1 + i).start()

    def handed_on(kind, buf, c, part, rows):
        @pl.when((c < z) & (z < NT - 1))
        def _():
            hop(kind, buf, "r", z - c, part, rows, c).wait_send()

        @pl.when((c > z) & (z > 0))
        def _():
            hop(kind, buf, "l", c - z, part, rows, c).wait_send()

    halves = [slice(i * QB, (i + 1) * QB) for i in range(R // QB)]

    V = pltpu.VMEM
    x_in, cot_in = xs.at[0], cotg.at[z]
    loads = [
        pltpu.make_async_copy(src, dst, lsem.at[i])
        for i, (src, dst) in enumerate(
            [
                (x_hbm, x_in),
                (cot_hbm, cot_in),
                (eg_hbm, wgu.at[: p.EB, : p.B]),
                (eu_hbm, wgu.at[: p.EB, p.B :]),
                (ed_hbm, wd.at[: p.EB]),
                (sg_hbm, wguT.at[p.EB, :, : p.B]),
                (su_hbm, wguT.at[p.EB, :, p.B :]),
                (sd_hbm, wd.at[p.EB]),
            ]
        )
    ]
    for c in loads:
        c.start()
    barrier = pltpu.get_barrier_semaphore()
    for k in (1, 2, 3):
        pl.semaphore_signal(barrier, inc=1, device_id=to_z(k), device_id_type=MESH)

    def greet(j, carry):
        pl.semaphore_signal(barrier, inc=1, device_id=(lax.rem(dp + j, p.nd), z), device_id_type=MESH)
        return carry

    lax.fori_loop(1, p.nd, greet, 0)
    pl.semaphore_wait(barrier, 3 + p.nd - 1)

    member = lax.rem(dp, 8)
    quad = lax.div(member, 2)

    def w_rows(matrix, at, side):
        start = at * p.HC + side * (p.HC // 2)
        return wfull.at[matrix, pl.ds(pl.multiple_of(start, 16), p.HC // 2)]

    def w_copy(k, at):
        part = w_rows(quad, at, core)
        return remote(part, part, "w", k - 1, to_z(k))

    def f_copy(k, j, matrix):
        part = w_rows(matrix, zk[k], core)
        there = dp - member + 2 * lax.rem(quad + j, 4) + core
        return remote(part, part, "f", (k - 1) * 3 + j - 1, (there, z))

    def g_copy(k, j, side):
        part = w_rows(lax.rem(quad + 4 - j, 4), zk[k], side)
        return remote(part, part, "g", (k - 1) * 4 + j, (mate, z))

    own_cols = pl.ds(pl.multiple_of(z * p.HC, 32), p.HC)
    for m, ref in enumerate((wq_ref, wk_ref, wv_ref, wo_ref)):
        wfull[m, own_cols] = ref[...]
    for k in (1, 2, 3):
        w_copy(k, z).start()
    loads[0].wait()
    x_copy = remote(xs.at[0], xs.at[1], "x", 0, (dp, z + 1 - 2 * zlo))
    late = zlo == 1

    @pl.when(zlo == 0)
    def _():
        x_copy.start()

    gain_attn = gain_attn_ref[...].astype(F32)[None]
    gain_ffn = gain_ffn_ref[...].astype(F32)[None]
    rext32[0 : p.E] = router_ref[...].astype(F32)
    vec = vec_ref[...].astype(F32)[None]
    rext32[p.E : p.E + 1] = vec
    rext32[p.E + 1 : p.E + 2] = vec
    rext32[p.E + 2 :] = jnp.zeros((14 - p.E, W), F32)
    rext[...] = rext32[...].astype(BF)
    rextT[...] = jnp.concatenate([rext32[...], jnp.zeros((LANES - 16, W), F32)], axis=0).T.astype(BF)

    for k in (1, 2, 3):
        w_copy(k, zk[k]).wait_recv()
        for j in (1, 2, 3):
            f_copy(k, j, quad).start()
        g_copy(k, 0, core).start()

    length = len_ref[lax.div(z, 2)]
    for i in range(R // QB):
        key = lax.broadcasted_iota(jnp.int32, (QB, R), 0) + i * QB
        query = lax.broadcasted_iota(jnp.int32, (QB, R), 1)
        bias[i * QB : (i + 1) * QB] = jnp.where((key <= query) & (key + half_own * R < length), 0.0, NEG)
    v = x_in[...].astype(F32)
    xn[0] = (v * inv_rms(v) * gain_attn).astype(BF)

    for c in loads[1:]:
        c.wait()
    for i in range(2):
        at = slice(i * p.B, (i + 1) * p.B)
        wgu[p.EB, at] = wguT[p.EB, :, at].T

    def turn(b, carry):
        for i in range(2):
            at = slice(i * p.B, (i + 1) * p.B)
            wguT[b, :, at] = wgu[b, at].T
        wdT[b] = wd[b].T
        return carry

    lax.fori_loop(0, p.EB, turn, 0)
    wdT[p.EB] = wd[p.EB].T
    for k in (1, 2, 3):
        for j in (1, 2, 3):
            f_copy(k, j, lax.rem(quad + 4 - j, 4)).wait_recv()
            g_copy(k, j, core).start()
    send_own("c", cotg, 0, slice(None))
    for k in (1, 2, 3):
        for j in range(4):
            g_copy(k, j, 1 - core).wait_recv()

    own_pos = pl.ds(pl.multiple_of(half_own * R, R), R)
    lane = lax.broadcasted_iota(jnp.int32, (1, LANES), 1)
    low_half = lax.rem(lane, HD) < HD // 2

    def swap_halves(v):
        return jnp.where(low_half, pltpu.roll(v, LANES - HD // 2, 1), pltpu.roll(v, HD // 2, 1))

    q_pre = nt(wfull[0], xn[0])
    cos_own, sin_own = cost[:, own_pos], sint[:, own_pos]
    for h in range(W // HD):
        a = q_pre[h * HD : h * HD + HD // 2]
        b = q_pre[h * HD + HD // 2 : (h + 1) * HD]
        qT[h * HD : h * HD + HD // 2] = ((a * cos_own - b * sin_own) * (SCALE * LOG2E)).astype(BF)
        qT[h * HD + HD // 2 : (h + 1) * HD] = ((a * sin_own + b * cos_own) * (SCALE * LOG2E)).astype(BF)

    def keys_values(slot, start):
        def project(i, carry):
            rows = pl.ds(pl.multiple_of(i * QB, QB), QB)
            at = pl.ds(pl.multiple_of(start + i * QB, QB), QB)
            xb = xn[slot, rows]
            k_pre = nt(xb, wfull[1])
            v_pre = nt(xb, wfull[2])
            c, s = cosk[at], sink[at]
            for g in range(NG):
                kg = k_pre[:, g * LANES : (g + 1) * LANES]
                kN[slot, g, rows] = (kg * c + swap_halves(kg) * s).astype(BF)
                vN[slot, g, rows] = v_pre[:, g * LANES : (g + 1) * LANES].astype(BF)
            return carry

        lax.fori_loop(0, R // QB, project, 0)
        for g in range(NG):
            kvT[slot, g * LANES : (g + 1) * LANES] = vN[slot, g].T

    keys_values(0, half_own * R)
    for g in range(NG):
        qN[g] = qT[g * LANES : (g + 1) * LANES].T

    head_row = lax.div(lax.broadcasted_iota(jnp.int32, (LANES, 1), 0), HD)
    head_lane = lax.div(lane, HD)
    HPG = LANES // HD

    def one_head(ref, g, h, cols):
        v = ref[pl.ds(pl.multiple_of(g * LANES, LANES), LANES), cols]
        return jnp.where(head_row == h, v, jnp.zeros_like(v))

    def rows_of(g, h):
        return pl.ds(pl.multiple_of(g * LANES + h * HD, HD), HD)

    every = slice(0, R)

    def early_bias(n):
        one = jnp.where(lax.broadcasted_iota(jnp.int32, (R, LANES), 0) < length, 0.0, NEG)
        return jnp.concatenate([one] * (n // LANES), axis=1)

    def softmax_parts(slot, g, h, keys, cols, addend):
        s = nn(kN[slot, g, keys], one_head(qT, g, h, cols)) + addend
        top = jnp.max(s, axis=0, keepdims=True)
        e = jnp.exp2(s - top)
        total = jnp.sum(e, axis=0, keepdims=True)
        return top, total, nn(kvT[slot, rows_of(g, h), keys], e.astype(BF))

    def own_keys(g, carry):
        for qb in range(R // QB):
            keys, cols = slice(0, (qb + 1) * QB), halves[qb]
            for h in range(HPG):
                head = pl.ds(g * HPG + h, 1)
                lse[head, cols], delta[head, cols], o_acc[rows_of(g, h), cols] = softmax_parts(
                    0, g, h, keys, cols, bias[keys, cols]
                )
        return carry

    lax.fori_loop(0, NG, own_keys, 0)
    arrive("c", cotg, 0, 0, slice(None))

    @pl.when(late)
    def _():
        x_copy.wait_recv()
        v = xs[1].astype(F32)
        xn[1] = (v * inv_rms(v) * gain_attn).astype(BF)
        keys_values(1, 0)

    def early_keys(g, carry):
        addend = early_bias(R)
        for h in range(HPG):
            head = pl.ds(g * HPG + h, 1)
            top, total, o = softmax_parts(1, g, h, every, every, addend)
            old = lse[head]
            new = jnp.maximum(top, old)
            keep_old, keep_new = jnp.exp2(old - new), jnp.exp2(top - new)
            lse[head] = new
            delta[head] = delta[head] * keep_old + total * keep_new
            at = rows_of(g, h)
            o_acc[at] = o_acc[at] * keep_old + o * keep_new
        return carry

    @pl.when(late)
    def _():
        lax.fori_loop(0, NG, early_keys, 0)

    for qb in range(R // QB):
        rows = halves[qb]
        for h in range(W // HD):
            at = slice(h * HD, (h + 1) * HD)
            oT[at, rows] = (o_acc[at, rows] * (1.0 / delta[h : h + 1, rows])).astype(BF)
        lse[0 : W // HD, rows] = lse[0 : W // HD, rows] + jnp.log(delta[0 : W // HD, rows]) * LOG2E
        m = x_in[rows].astype(F32) + nn(oT[:, rows].T, wfull[3])
        mid[rows] = m
        normg[z, rows] = (m * inv_rms(m) * gain_ffn).astype(BF)
        send_own("n", normg, qb, rows)
    for g in range(NG):
        at = slice(g * LANES, (g + 1) * LANES)
        kvT[0, at] = kN[0, g].T

        @pl.when(late)
        def _(g=g, at=at):
            kvT[1, at] = kN[1, g].T

    def zero_acc(i, carry):
        acc[pl.ds(pl.multiple_of(i * 16, 16), 16)] = jnp.zeros((16, W), F32)
        return carry

    lax.fori_loop(0, 3 * p.NB * W // 16, zero_acc, 0)
    drext[...] = jnp.zeros_like(drext)
    zhi = lax.div(z, 2)

    def chunk_of(k):
        return 2 * lax.rem(zhi + lax.div(k, 2), 2) + lax.rem(zlo + lax.rem(k, 2), 2)

    def chip_rows(j):
        return pl.ds(pl.multiple_of(chip_at(j) * p.pr, 16), p.pr)

    def owner(c):
        return (lambda f: f()) if p.owners == p.nc else pl.when(c < p.owners)

    owns = owner(chip)

    def h1_copy(b):
        return remote(stage.at[b], h1.at[b], "h1", b, (mate, z))

    def h2_copy(b, j):
        i = b * (p.nc - 1) + j - 1
        return remote(h1.at[b, :, chip_rows(j)], h2.at[j - 1, b], "h2", i, on_chip(j))

    def h3_copy(b, j):
        i = b * (p.nc - 1) + j - 1
        return remote(fin.at[b], res.at[b, :, core, chip_rows(0)], "h3", i, on_chip(j))

    def h4_copy(b, j):
        part = res.at[b, :, core, chip_rows(j)]
        return remote(fin.at[b] if j == 0 else part, part, "h4", b * p.nc + j, (mate, z))

    def keep(b):
        return pltpu.make_async_copy(fin.at[b], res.at[b, :, core, chip_rows(0)], lsem.at[b])

    def block_half(b, kind, side, turned=False):
        first = (3 * b + kind) * W
        if not turned:
            return acc[pl.ds(pl.multiple_of(first + side * p.hp, p.hp), p.hp)]
        v = acc[pl.ds(pl.multiple_of(first, W), W)].T
        return jnp.where(side == 0, v[: p.hp], v[p.hp :])

    def each_half(b, side, step):
        step(2, block_half(b, 2, side))

        @pl.when(b < p.EB)
        def _():
            for kind in range(2):
                step(kind, block_half(b, kind, side))

        @pl.when(b == p.EB)
        def _():
            for kind in range(2):
                step(kind, block_half(b, kind, side, True))

    def mate_half(b):
        def step(kind, v):
            stage[b, kind] = v.astype(BF)

        each_half(b, 1 - core, step)
        h1_copy(b).start()

    def to_chips(b):
        h1_copy(b).wait_recv()

        def step(kind, v):
            h1[b, kind] = (v + h1[b, kind].astype(F32)).astype(BF)

        each_half(b, core, step)
        for j in range(1, p.nc):
            owner(chip_at(j))(lambda j=j: h2_copy(b, j).start())

    def from_chips(b):
        @owns
        def _():
            for j in range(1, p.nc):
                h2_copy(b, j).wait_recv()
            for kind in range(3):
                v = h1[b, kind, chip_rows(0)].astype(F32)
                for j in range(1, p.nc):
                    v += h2[j - 1, b, kind].astype(F32)
                fin[b, kind] = v.astype(BF)
            for j in range(1, p.nc):
                h3_copy(b, j).start()
            h4_copy(b, 0).start()
            keep(b).start()

    def hand_over(b):
        for j in range(1, p.nc):
            sender = lax.rem(chip + p.nc - j, p.nc)

            @owner(sender)
            def _(j=j):
                h3_copy(b, j).wait_recv()
                h4_copy(b, p.nc - j).start()

    def unit(gates, xT, gT, out_acc, dx_acc, last, part, k, carry):
        c = chunk_of(k)
        n = part.stop - part.start

        xT[...] = normg[c, part].T
        gT[...] = cotg[c, part].T
        logits = nn(rext[...], xT[...])
        down = lax.broadcasted_iota(jnp.int32, (16, n), 0)
        is_expert = down < p.E
        lg = jnp.where(is_expert, logits, NEG)
        ex = jnp.exp(lg - jnp.max(lg, axis=0, keepdims=True))
        route = ex / jnp.sum(ex, axis=0, keepdims=True)
        at = pl.ds(pl.multiple_of(c * R + part.start, n), n)
        named = (down == ids_ref[0:1, at]) | (down == ids_ref[1:2, at]) | ((down >= p.E) & (down < p.E + 2))
        chosen = jnp.where(named, 1.0, 0.0)
        gate = jnp.where(is_expert, route, lax.logistic(logits)) * chosen
        gates[0] = chosen
        gates[1] = route
        gates[2] = gate
        gates[3] = jnp.zeros_like(gate)
        out_acc[...] = jnp.zeros_like(out_acc)
        dx_acc[...] = jnp.zeros_like(dx_acc)

        def block(b, carry):
            if not last:

                @pl.when((b == 1) & (k > 0))
                def _():
                    arrive("c", cotg, k, 0, slice(None))

                @pl.when(b == 2)
                def _():
                    arrive("n", normg, k, 0, halves[0])

                @pl.when(b == 4)
                def _():
                    arrive("n", normg, k, 1, halves[1])

            au = nn(wgu[b], xT[...])
            hg = nn(wd[b], gT[...])
            h_parts, a_parts, u_parts = [], [], []
            for e in range(2):
                expert = pl.ds(2 * b + e, 1)
                gc = gates[2, expert]
                sums = 0.0
                for first in range(e * p.eff, (e + 1) * p.eff, TILE):
                    rows = slice(first, first + TILE)
                    a, u, back = au[rows], au[p.B + first : p.B + first + TILE], hg[rows]
                    sig = 0.5 * jnp.tanh(0.5 * a) + 0.5
                    act = a * sig
                    slope = sig + act * (1.0 - sig)
                    h = act * u
                    sums += jnp.sum((h * back).reshape(TILE // 8, 8, n), axis=0)
                    scaled = back * gc
                    h_parts.append((h * gc).astype(BF))
                    a_parts.append((scaled * u * slope).astype(BF))
                    u_parts.append((scaled * act).astype(BF))
                gates[3, expert] = jnp.sum(sums, axis=0, keepdims=True)
            hs = jnp.concatenate(h_parts, axis=0)
            dau = jnp.concatenate(a_parts + u_parts, axis=0)
            out_acc[...] += nn(wdT[b], hs)
            dx_acc[...] += nn(wguT[b], dau)
            acc[pl.ds(pl.multiple_of(3 * b * W, W), 2 * W)] += nn(dau, normg[c, part])
            acc[pl.ds(pl.multiple_of((3 * b + 2) * W, W), W)] += nn(hs, cotg[c, part])

            if last == 1:
                mate_half(b)
                pl.when(b > 0)(lambda: to_chips(b - 1))

            return carry

        lax.fori_loop(0, p.NB, block, 0)
        chosen, route, gate = gates[0], gates[1], gates[2]
        rg = gates[3] * chosen
        dot = jnp.sum(jnp.where(is_expert, route * rg, 0.0), axis=0, keepdims=True)
        lgrad = jnp.where(is_expert, route * (rg - dot), rg * gate * (1.0 - gate))
        drext[...] += nn(lgrad.astype(BF), normg[c, part])
        lwide = jnp.concatenate([lgrad, jnp.zeros((LANES - 16, n), F32)], axis=0).astype(BF)
        dx = dx_acc[...] + nn(rextT[...], lwide)
        if last != 1:
            for b in range(R // QB):
                handed_on("n", normg, c, b, halves[b])
            handed_on("c", cotg, c, 0, slice(None))

        if not last:

            @pl.when(k == 0)
            def _():
                dx_own[...] = dx.T
                out_own[...] = out_acc[...].astype(BF).T

        @pl.when(k > 0)
        def _():
            normg[c, part] = dx.astype(BF).T
            cotg[c, part] = out_acc[...].astype(BF).T
            remote(normg.at[c, part], dxr.at[k - 1, part], "dx", NT - last if last else k - 1, (dp, c)).start()

        return carry

    def chunks(n, body):
        pl.run_scoped(body, V((4, 16, n), F32), V((W, n), BF), V((W, n), BF), V((W, n), F32), V((W, n), F32))

    chunks(R, lambda *refs: lax.fori_loop(0, NT - 1, functools.partial(unit, *refs, 0, every), 0) and None)
    for i, part in enumerate(halves):
        chunks(QB, lambda *refs, i=i, part=part: unit(*refs, len(halves) - i, part, NT - 1, 0) and None)
    to_chips(p.NB - 1)

    def dx_copies():
        copies = [remote(normg.at[zk[k]], dxr.at[k - 1], "dx", k - 1, to_z(k)) for k in range(1, NT - 1)]
        for i, part in enumerate(halves):
            at = normg.at[zk[NT - 1], part]
            copies.append(remote(at, dxr.at[NT - 2, part], "dx", NT - len(halves) + i, to_z(NT - 1)))
        return copies

    for copy in dx_copies():
        copy.wait_recv()
    def o_next(i):
        return remote(cotg.at[zk[1 + 2 * i]], outr.at[i], "o", i, to_z(1))

    def o_far():
        return remote(cotg.at[zk[2]], outr.at[2], "o", 2, to_z(2))

    for i in (1, 0):
        o_next(i).start()

    dn = dx_own[...] + dxr[0].astype(F32) + dxr[1].astype(F32) + dxr[2].astype(F32)
    mid_back, dgain = rms_back(mid[...], dn, gain_ffn)
    sm_own = jnp.sum(dgain, axis=0, keepdims=True)
    mg = cot_in[...].astype(F32) + mid_back
    dx_own[...] = mg
    ag = mg.astype(BF)
    agrad[...] = ag
    dO = nt(ag, wfull[3])
    for g in range(NG):
        dON[g] = dO[:, g * LANES : (g + 1) * LANES].astype(BF)
    dOt = nt(wfull[3], ag).astype(BF)
    dOT[...] = dOt
    both = dOt.astype(F32) * oT[...].astype(F32)
    for h in range(W // HD):
        delta[h : h + 1] = jnp.sum(both[h * HD : (h + 1) * HD], axis=0, keepdims=True)

    dw = [acc.at[m * W : (m + 1) * W] for m in range(4)]
    dxn, dxn_early = acc.at[4 * W : 4 * W + R], acc.at[4 * W + R : 4 * W + 2 * R]
    dw[3][...] = nn(oT[...], agrad[...])
    dw[1][...] = jnp.zeros((W, W), F32)
    dw[2][...] = jnp.zeros((W, W), F32)
    dxn[...] = jnp.zeros((R, W), F32)
    dxn_early[...] = jnp.zeros((R, W), F32)
    o_acc[...] = jnp.zeros_like(o_acc)
    pxs = agrad
    px_copy = remote(pxs, xs.at[1], "px", 0, (dp, z + 1 - 2 * zlo))

    def score_grads(pT, dsT, slot, g, h, keys, cols, addend, place):
        head = pl.ds(g * HPG + h, 1)
        s = nn(kN[slot, g, keys], one_head(qT, g, h, cols)) + addend
        prob = jnp.exp2(s - lse[head, cols])
        d_prob = nn(vN[slot, g, keys], one_head(dOT, g, h, cols))
        ds = (prob * (d_prob - delta[head, cols])).astype(BF)
        pT[keys, place] = prob.astype(BF)
        dsT[keys, place] = ds
        o_acc[rows_of(g, h), cols] += nn(kvT[slot, rows_of(g, h), keys], ds) * SCALE

    def all_heads(ref, g, rows):
        v = ref[g, rows]
        return jnp.concatenate([jnp.where(head_lane == h, v, jnp.zeros_like(v)) for h in range(HPG)], axis=0)

    def unturn(dk, at):
        return (dk * cosk[at] - swap_halves(dk) * sink[at]).astype(BF)

    def keys_back(slot, g, at_g, dk, dv, sums):
        dv = dv.astype(BF)
        dw[1][at_g] += nn(dk.T, xn[slot])
        dw[2][at_g] += nn(dv.T, xn[slot])
        sums[...] += nn(dk, wfull[1, at_g]) + nn(dv, wfull[2, at_g])

    def f1_copy(g):
        return remote(A.at[g], f1.at[g], "f1", g, (mate, z))

    def f2_rows(j):
        return pl.ds(pl.multiple_of(chip_at(j) * 16, 16), 16)

    def f2_copy(g, j):
        i = g * (p.nc - 1) + j - 1
        return remote(f1.at[g, :, f2_rows(j)], f2.at[j - 1, g], "f2", i, on_chip(j))

    def sums_heads(c):
        return (lambda f: f()) if p.att_owners == p.nc else pl.when(c < p.att_owners)

    def home(g, side, c):
        head = HPG * g + (HPG // 2) * side + lax.div(c, 2)
        to = lax.div(head, p.HC // HD)
        return to, g * LANES + side * (LANES // 2) + c * 16 - to * p.HC

    def f3_copy(g, at):
        to, _ = home(g, core, chip)
        return remote(fD.at[g], f3.at[g, at], "f3", g * NT + at, (dp, to))

    def f4_copy(g, j, row):
        part = att.at[:, pl.ds(pl.multiple_of(row, 16), 16)]
        return remote(part, part, "f4", g * (p.nd - 1) + j - 1, (lax.rem(dp + j, p.nd), z))

    def head_half(g, m, side):
        at = g * LANES + side * (LANES // 2)
        return dw[m][pl.ds(pl.multiple_of(at, LANES // 2), LANES // 2)]

    def stage_heads(g):
        for m in range(4):
            A[g, m] = head_half(g, m, 1 - core).astype(BF)
        f1_copy(g).start()

    def heads_to_chips(g):
        f1_copy(g).wait_recv()
        for m in range(4):
            f1[g, m] = (head_half(g, m, core) + f1[g, m].astype(F32)).astype(BF)
        for j in range(1, p.nc):
            sums_heads(chip_at(j))(lambda j=j: f2_copy(g, j).start())

    def heads_along_z(g):
        @sums_heads(chip)
        def _():
            for j in range(1, p.nc):
                f2_copy(g, j).wait_recv()
            for m in range(4):
                v = f1[g, m, f2_rows(0)].astype(F32)
                for j in range(1, p.nc):
                    v += f2[j - 1, g, m].astype(F32)
                fD[g, m] = v.astype(BF)
            to, _ = home(g, core, chip)

            @pl.when(to != z)
            def _():
                f3_copy(g, z).start()

    def heads_home(g):
        @sums_heads(chip)
        def _():
            to, row = home(g, core, chip)

            @pl.when(to == z)
            def _():
                for at in range(NT):

                    @pl.when(at != z)
                    def _(at=at):
                        f3_copy(g, at).wait_recv()

                f3[g, z] = fD[g]
                for m in range(4):
                    v = f3[g, 0, m].astype(F32)
                    for at in range(1, NT):
                        v += f3[g, at, m].astype(F32)
                    att[m, pl.ds(pl.multiple_of(row, 16), 16)] = v.astype(BF)
                for j in range(1, p.nd):
                    f4_copy(g, j, row).start()

    def chips(b, carry):
        from_chips(b)
        return carry

    lax.fori_loop(0, p.NB, chips, 0)

    def back(pT, dsT):
        @pl.when(late)
        def _():
            def early(g, carry):
                at_g = pl.ds(pl.multiple_of(g * LANES, LANES), LANES)
                for h in range(HPG):
                    place = slice(h * R, (h + 1) * R)
                    score_grads(pT, dsT, 1, g, h, every, every, early_bias(R), place)
                dv = nn(pT[...], all_heads(dON, g, every))
                dk = nn(dsT[...], all_heads(qN, g, every)) * LN2
                keys_back(1, g, at_g, unturn(dk, every), dv, dxn_early)
                return carry

            lax.fori_loop(0, NG, early, 0)
            pxs[...] = dxn_early[...].astype(BF)
            px_copy.start()

        def own(g, carry):
            @pl.when(g > 0)
            def _():
                heads_to_chips(g - 1)

            at_g = pl.ds(pl.multiple_of(g * LANES, LANES), LANES)
            for qb in range(R // QB):
                keys, cols = slice(0, (qb + 1) * QB), halves[qb]
                for h in range(HPG):
                    first = (qb * HPG + h) * QB
                    score_grads(pT, dsT, 0, g, h, keys, cols, bias[keys, cols], slice(first, first + QB))
            dk, dv = [], []
            for qb in range(R // QB):
                keys, place = slice(0, (qb + 1) * QB), slice(qb * HPG * QB, (qb + 1) * HPG * QB)
                dv.append(nn(pT[keys, place], all_heads(dON, g, halves[qb])))
                dk.append(nn(dsT[keys, place], all_heads(qN, g, halves[qb])))
            dv = jnp.concatenate([dv[0] + dv[1][:QB], dv[1][QB:]], axis=0)
            dk = jnp.concatenate([dk[0] + dk[1][:QB], dk[1][QB:]], axis=0) * LN2
            keys_back(0, g, at_g, unturn(dk, own_pos), dv, dxn)
            parts = []
            for h in range(HPG):
                a = o_acc[pl.ds(pl.multiple_of(g * LANES + h * HD, 16), HD // 2)]
                b = o_acc[pl.ds(pl.multiple_of(g * LANES + h * HD + HD // 2, 16), HD // 2)]
                parts += [a * cos_own + b * sin_own, b * cos_own - a * sin_own]
            dq = jnp.concatenate(parts, axis=0).astype(BF)
            dw[0][at_g] = nn(dq, xn[0])
            dxn[...] += nn(dq.T, wfull[0, at_g])
            stage_heads(g)
            return carry

        o_next(1).wait_recv()
        cotg[zk[2]] = (cotg[zk[2]].astype(F32) + outr[1].astype(F32)).astype(BF)
        o_far().start()
        lax.fori_loop(0, NG, own, 0)

    wide = V((R, HPG * R), BF)
    pl.run_scoped(back, wide, wide)

    def gain_part(slot, sums):
        v = xs[slot].astype(F32)
        return jnp.sum(sums[...] * (v * inv_rms(v)), axis=0, keepdims=True)

    rext32[0:1] = gain_part(0, dxn)

    @pl.when(late)
    def _():
        rext32[0:1] += gain_part(1, dxn_early)

    rext32[1:2] = sm_own
    rext32[2:16] = drext[0:14]
    smr[dp] = rext32[...].astype(BF)

    def small(j):
        there = lax.rem(dp + j, p.nd)
        return remote(smr.at[dp], smr.at[dp], "s1", j - 1, (there, z))

    for j in range(1, p.nd):
        small(j).start()

    heads_to_chips(NG - 1)
    for g in range(NG):
        heads_along_z(g)
    for g in range(NG - 1):
        heads_home(g)

    for j in range(1, p.nd):
        small(j).wait_recv()
    total = smr[0].astype(F32)
    for j in range(1, p.nd):
        total += smr[j].astype(F32)
    smz[z] = total

    def small_z(k):
        return remote(smz.at[z], smz.at[z], "s2", k - 1, to_z(k))

    for k in (1, 2, 3):
        small_z(k).start()
    heads_home(NG - 1)

    @pl.when(zlo == 0)
    def _():
        px_copy.wait_recv()
        dxn[...] += xs[1].astype(F32)

    dn = dxn[...]
    x_back, _ = rms_back(x_in[...].astype(F32), dn, gain_attn)
    din_ref[...] = dx_own[...] + x_back
    o_next(0).wait_recv()
    o_far().wait_recv()
    whole = mid[...] + (out_own[...].astype(F32) + outr[0].astype(F32) + outr[2].astype(F32))
    out_ref[...] = whole.astype(BF)

    for k in (1, 2, 3):
        small_z(k).wait_recv()
    sm_ref[...] = smz[0] + smz[1] + smz[2] + smz[3]

    def hand_all(b, carry):
        hand_over(b)
        return carry

    lax.fori_loop(0, p.NB, hand_all, 0)

    def mate_done(b, carry):
        for j in range(p.nc):
            owner(chip_at(j))(lambda j=j: h4_copy(b, j).wait_recv())
        return carry

    lax.fori_loop(0, p.NB, mate_done, 0)
    for g in range(NG):
        for j in range(1, p.nd):
            sender = lax.rem(dp + p.nd - j, p.nd)
            c, side = lax.div(sender, 2), lax.rem(sender, 2)

            @sums_heads(c)
            def _(g=g, j=j, c=c, side=side):
                to, row = home(g, side, c)
                pl.when(to == z)(lambda: f4_copy(g, j, row).wait_recv())

    for m in range(4):
        att_ref[m * p.HC : (m + 1) * p.HC] = att[m]

    for k in (1, 2, 3):
        w_copy(k, z).wait_send()
        for j in (1, 2, 3):
            f_copy(k, j, quad).wait_send()
        for j in range(4):
            g_copy(k, j, core).wait_send()
        small_z(k).wait_send()
    for copy in dx_copies() + [o_next(0), o_next(1), o_far()]:
        copy.wait_send()
    own_sent("c", cotg, 0, slice(None))
    for b in range(R // QB):
        own_sent("n", normg, b, halves[b])
    pl.when(zlo == 0)(lambda: x_copy.wait_send())
    pl.when(late)(lambda: px_copy.wait_send())
    for g in range(NG):
        f1_copy(g).wait_send()
        for j in range(1, p.nc):
            sums_heads(chip_at(j))(lambda g=g, j=j: f2_copy(g, j).wait_send())

        @sums_heads(chip)
        def _(g=g):
            to, row = home(g, core, chip)
            pl.when(to != z)(lambda: f3_copy(g, z).wait_send())

            @pl.when(to == z)
            def _():
                for j in range(1, p.nd):
                    f4_copy(g, j, row).wait_send()

    def sums_sent(b, carry):
        h1_copy(b).wait_send()
        for j in range(1, p.nc):
            owner(chip_at(j))(lambda j=j: h2_copy(b, j).wait_send())
            owns(lambda j=j: h3_copy(b, j).wait_send())
        owns(lambda: keep(b).wait())
        for j in range(p.nc):
            owner(chip_at(j))(lambda j=j: h4_copy(b, j).wait_send())
        return carry

    lax.fori_loop(0, p.NB, sums_sent, 0)
    for j in range(1, p.nd):
        small(j).wait_send()


def tables():
    half = HD // 2
    freqs = 10000.0 ** (-np.arange(half, dtype=np.float32) / np.float32(half))
    angles = np.arange(LEN, dtype=np.float32)[:, None] * freqs.astype(np.float32)[None, :]
    cosine, sine = np.cos(angles).astype(np.float32), np.sin(angles).astype(np.float32)
    reps = LANES // HD
    cos_wide = np.tile(np.concatenate([cosine, cosine], axis=1), (1, reps))
    sin_wide = np.tile(np.concatenate([-sine, sine], axis=1), (1, reps))
    return cos_wide, sin_wide, np.ascontiguousarray(cosine.T), np.ascontiguousarray(sine.T)


def per_device(
    nd,
    inputs,
    lengths,
    expert_ids,
    gain_attn,
    w_query,
    w_key,
    w_value,
    w_out,
    gain_ffn,
    router,
    shared_gate_vec,
    exp_gate,
    exp_up,
    exp_down,
    sh_gate,
    sh_up,
    sh_down,
    cotangent,
):
    R, W = inputs.shape
    experts, _, eff = exp_gate.shape
    ff = sh_gate.shape[1]
    p = Plan(nd, R, W, experts, eff, ff)
    number, names = sem_plan(p)
    eg = exp_gate.swapaxes(1, 2).reshape(p.EB, p.B, W)
    eu = exp_up.swapaxes(1, 2).reshape(p.EB, p.B, W)
    ed = exp_down.reshape(p.EB, p.B, W)
    cosk, sink, cost, sint = tables()
    vm = pl.BlockSpec(memory_space=pltpu.VMEM)
    hbm = pl.BlockSpec(memory_space=pl.ANY)
    V = pltpu.VMEM
    hc = W // HD
    scratch = [
        pltpu.SemaphoreType.DMA((number,)),
        pltpu.SemaphoreType.DMA((number,)),
        pltpu.SemaphoreType.DMA((8,)),
        V((4, W, W), BF),
        V((16, W), F32),
        V((16, W), BF),
        V((W, LANES), BF),
        V((2, R, W), BF),
        V((2, R, W), BF),
        V((NT, R, W), BF),
        V((NT, R, W), BF),
        V((p.NB, 2 * p.B, W), BF),
        V((p.NB, W, 2 * p.B), BF),
        V((p.NB, p.B, W), BF),
        V((p.NB, W, p.B), BF),
        V((W, R), BF),
        V((p.NG, R, LANES), BF),
        V((2, p.NG, R, LANES), BF),
        V((2, W, R), BF),
        V((2, p.NG, R, LANES), BF),
        V((W, R), BF),
        V((up16(hc), R), F32),
        V((R, R), F32),
        V((W, R), F32),
        V((R, W), F32),
        V((R, W), F32),
        V((R, W), BF),
        V((3, R, W), BF),
        V((3, R, W), BF),
        V((3 * p.NB * W, W), F32),
        V((16, W), F32),
        V((p.NB, 3, p.hp, W), BF),
        V((p.NB, 3, p.hp, W), BF),
        V((max(p.nc - 1, 1), p.NB, 3, p.pr, W), BF),
        V((p.NB, 3, p.pr, W), BF),
        V((R, W), BF),
        V((p.NG, R, LANES), BF),
        V((W, R), BF),
        V((up16(hc), R), F32),
        V((p.NG, 4, LANES // 2, W), BF),
        V((p.NG, 4, LANES // 2, W), BF),
        V((p.nc - 1, p.NG, 4, 16, W), BF),
        V((p.NG, 4, 16, W), BF),
        V((p.NG, NT, 4, 16, W), BF),
        V((4, p.HC, W), BF),
        V((nd, 16, W), BF),
        V((NT, 16, W), F32),
    ]
    results = pl.pallas_call(
        functools.partial(kernel, p, names),
        out_shape=[
            jax.ShapeDtypeStruct((R, W), BF),
            jax.ShapeDtypeStruct((R, W), F32),
            jax.ShapeDtypeStruct((2 * p.hp, W), BF),
            jax.ShapeDtypeStruct((16, W), F32),
            jax.ShapeDtypeStruct((p.NB, 3, 2, p.hp, W), BF),
        ],
        in_specs=[pl.BlockSpec(memory_space=pltpu.SMEM)] + [vm] * 9 + [hbm] * 8 + [vm] * 4,
        out_specs=[vm] * 4 + [hbm],
        scratch_shapes=scratch,
        compiler_params=pltpu.CompilerParams(collective_id=0, has_side_effects=True, vmem_limit_bytes=63 << 20),
        name="block",
    )(
        lengths,
        expert_ids.T,
        gain_attn,
        gain_ffn,
        router.T,
        shared_gate_vec,
        w_query.T,
        w_key.T,
        w_value.T,
        w_out,
        inputs,
        cotangent,
        eg,
        eu,
        ed,
        sh_gate,
        sh_up,
        sh_down,
        jnp.asarray(cosk),
        jnp.asarray(sink),
        jnp.asarray(cost),
        jnp.asarray(sint),
    )
    return widen(p, *results)


def widen_kernel(p, out_b, din, att, small, routed, shared, *outs):
    (out_o, din_o, ga_o, wq_o, wk_o, wv_o, wo_o, gf_o, ro_o, ve_o, eg_o, eu_o, ed_o, sg_o, su_o, sd_o) = outs
    step = pl.program_id(0)
    for c in range(2):
        rows = slice(c * p.hp, (c + 1) * p.hp)
        for kind, dst in enumerate((eg_o, eu_o, ed_o)):
            dst[0, rows] = routed[0, kind, c].astype(F32)

    @pl.when(step == 0)
    def _():
        out_o[...] = out_b[...]
        din_o[...] = din[...]
        for m, dst in enumerate((wq_o, wk_o, wv_o, wo_o)):
            dst[...] = att[m * p.HC : (m + 1) * p.HC].astype(F32)
        ga_o[...] = small[0]
        gf_o[...] = small[1]
        ro_o[...] = small[2 : 2 + p.E]
        ve_o[...] = small[2 + p.E] + small[3 + p.E]
        for c in range(2):
            rows = slice(c * p.hp, (c + 1) * p.hp)
            for kind, dst in enumerate((sg_o, su_o, sd_o)):
                dst[rows] = shared[0, kind, c].astype(F32)


def widen(p, *results):
    R, W = p.R, p.W

    def whole(shape):
        return pl.BlockSpec(shape, lambda i: (0,) * len(shape))

    def split(shape):
        return pl.BlockSpec((1,) + shape[1:], lambda i: (i,) + (0,) * (len(shape) - 1))

    block = (1, 3, 2, p.hp, W)
    routed = (p.EB, p.B, W)
    row, head, sh = (W,), (p.HC, W), (W, W)
    shapes = [(R, W), (R, W), row, head, head, head, head, row, (p.E, W), row, routed, routed, routed, sh, sh, sh]
    out = pl.pallas_call(
        functools.partial(widen_kernel, p),
        grid=(p.EB,),
        out_shape=[jax.ShapeDtypeStruct(s, BF if i == 0 else F32) for i, s in enumerate(shapes)],
        in_specs=[whole((R, W))] * 2
        + [whole((2 * p.hp, W)), whole((16, W))]
        + [pl.BlockSpec(block, lambda i: (i, 0, 0, 0, 0)), pl.BlockSpec(block, lambda i: (p.EB, 0, 0, 0, 0))],
        out_specs=[split(s) if s == routed else whole(s) for s in shapes],
        compiler_params=pltpu.CompilerParams(vmem_limit_bytes=63 << 20),
        name="widen",
    )(*results, results[-1])
    out = list(out)
    for i in (3, 4, 5, 8):
        out[i] = out[i].T
    for i in (10, 11, 12):
        out[i] = out[i].reshape(p.E, p.eff, W)
    for i in (10, 11):
        out[i] = out[i].swapaxes(1, 2)
    return tuple(out)


def solution(mesh):
    rows = P(("dp", "tensor"), None)
    cols = P(None, "tensor")
    deep = P(None, None, "tensor")
    weights = (cols, cols, cols, P("tensor", None))
    experts = (deep, deep, P(None, "tensor", None), cols, cols, P("tensor", None))
    in_specs = (rows, P("dp"), P("dp", None), P()) + weights + (P(), P(), P()) + experts + (rows,)
    out_specs = (rows, rows, P()) + weights + (P(), P(), P()) + experts
    return jax.shard_map(
        functools.partial(per_device, mesh.shape["dp"]),
        mesh=mesh,
        in_specs=in_specs,
        out_specs=out_specs,
        check_vma=False,
    )
```

```python
import functools

import jax
import jax.numpy as jnp
import numpy as np
from jax import lax
from jax.experimental import pallas as pl
from jax.experimental.pallas import tpu as pltpu
from jax.sharding import PartitionSpec as P

HD = 32
LEN = 1024
NT = 4
LANES = 128
QB = 256
TILE = 32
BF = jnp.bfloat16
F32 = jnp.float32
MESH = pl.DeviceIdType.MESH
NEG = -1e30
SCALE = HD**-0.5
LOG2E = 1.4426950408889634
LN2 = 0.6931471805599453


def nn(a, b):
    return lax.dot_general(a, b, (((1,), (0,)), ((), ())), preferred_element_type=F32)


def nt(a, b):
    return lax.dot_general(a, b, (((1,), (1,)), ((), ())), preferred_element_type=F32)


def inv_rms(v):
    return lax.rsqrt(jnp.mean(v * v, axis=-1, keepdims=True) + 1e-06)


def rms_back(v, grad, gain):
    r = inv_rms(v)
    u = v * r
    g = grad * gain
    return r * (g - u * jnp.mean(g * u, axis=-1, keepdims=True)), grad * u


def up16(n):
    return -(-n // 16) * 16


class Plan:
    def __init__(self, nd, rows, width, experts, eff, ff):
        self.nd, self.R, self.W = nd, rows, width
        self.G = NT * rows
        self.NG = width // LANES
        self.HC = width // NT
        self.B = 2 * eff
        self.EB = experts // 2
        self.NB = self.EB + 1
        assert ff == self.B == width and LEN == 2 * rows
        self.E, self.eff, self.ff = experts, eff, ff
        assert nd % 8 == 0
        self.nc = nd // 2
        self.hp = 2 * self.HC
        assert 2 * self.hp == width == self.B
        self.pr = max(16, self.hp // self.nc)
        self.owners = self.hp // self.pr
        self.att_owners = LANES // 32
        assert self.owners * self.pr == self.hp and self.pr % 16 == 0 and self.owners <= self.nc


class Sems:
    def __init__(self):
        self.n = 0

    def take(self, n):
        base = self.n
        self.n += n
        return base


def sem_plan(p):
    s, names = Sems(), {}
    names["w"] = s.take(3)
    names["f"] = s.take(9)
    names["g"] = s.take(12)
    names["x"] = s.take(1)
    for way in "rl":
        names["c" + way] = s.take(4)
        names["n" + way] = s.take(8)
    names["dx"] = s.take(4)
    names["o"] = s.take(3)
    names["h1"] = s.take(p.NB)
    names["h2"] = s.take(p.NB * max(p.nc - 1, 1))
    names["h3"] = s.take(p.NB * max(p.nc - 1, 1))
    names["h4"] = s.take(p.NB * p.nc)
    names["px"] = s.take(1)
    names["f1"] = s.take(p.NG)
    names["f2"] = s.take(p.NG * (p.nc - 1))
    names["f3"] = s.take(p.NG * NT)
    names["f4"] = s.take(p.NG * (p.nd - 1))
    names["s1"] = s.take(p.nd - 1)
    names["s2"] = s.take(3)
    return s.n, names


def kernel(
    p,
    names,
    len_ref,
    ids_ref,
    gain_attn_ref,
    gain_ffn_ref,
    router_ref,
    vec_ref,
    wq_ref,
    wk_ref,
    wv_ref,
    wo_ref,
    x_hbm,
    cot_hbm,
    eg_hbm,
    eu_hbm,
    ed_hbm,
    sg_hbm,
    su_hbm,
    sd_hbm,
    cosk,
    sink,
    cost,
    sint,
    out_ref,
    din_ref,
    att_ref,
    sm_ref,
    res,
    send,
    recv,
    lsem,
    wfull,
    rext32,
    rext,
    rextT,
    xs,
    xn,
    cotg,
    normg,
    wgu,
    wguT,
    wd,
    wdT,
    qT,
    qN,
    kN,
    kvT,
    vN,
    oT,
    lse,
    bias,
    o_acc,
    mid,
    dx_own,
    out_own,
    dxr,
    outr,
    acc,
    drext,
    stage,
    h1,
    h2,
    fin,
    agrad,
    dON,
    dOT,
    delta,
    A,
    f1,
    f2,
    fD,
    f3,
    att,
    smr,
    smz,
):
    R, W, NG = p.R, p.W, p.NG
    dp, z = lax.axis_index("dp"), lax.axis_index("tensor")
    zlo = lax.rem(z, 2)
    zk = [z, z + 1 - 2 * zlo, lax.rem(z + 2, NT), NT - 1 - z]
    core = lax.rem(dp, 2)
    chip = lax.div(dp, 2)
    mate = dp + 1 - 2 * core
    half_own = zlo

    def remote(src, dst, kind, i, dev):
        j = names[kind] + i
        return pltpu.make_async_remote_copy(
            src_ref=src, dst_ref=dst, send_sem=send.at[j], recv_sem=recv.at[j], device_id=dev, device_id_type=MESH
        )

    def to_z(k):
        return (dp, zk[k])

    def chip_at(j):
        return lax.rem(chip + j, p.nc)

    def on_chip(j):
        return (2 * chip_at(j) + core, z)

    def hop(kind, buf, way, i, part, rows, at):
        there = (dp, z + 1) if way == "r" else (dp, z - 1)
        ref = buf.at[at, rows]
        parts = 1 if kind == "c" else R // QB
        return remote(ref, ref, kind + way, i * parts + part, there)

    def send_own(kind, buf, part, rows):
        @pl.when(z < NT - 1)
        def _():
            hop(kind, buf, "r", 0, part, rows, z).start()

        @pl.when(z > 0)
        def _():
            hop(kind, buf, "l", 0, part, rows, z).start()

    def own_sent(kind, buf, part, rows):
        @pl.when(z < NT - 1)
        def _():
            hop(kind, buf, "r", 0, part, rows, z).wait_send()

        @pl.when(z > 0)
        def _():
            hop(kind, buf, "l", 0, part, rows, z).wait_send()

    def arrive(kind, buf, i, part, rows):
        @pl.when(z - 1 - i >= 0)
        def _():
            hop(kind, buf, "r", i, part, rows, z - 1 - i).wait_recv()

            @pl.when(z < NT - 1)
            def _():
                hop(kind, buf, "r", i + 1, part, rows, z - 1 - i).start()

        @pl.when(z + 1 + i < NT)
        def _():
            hop(kind, buf, "l", i, part, rows, z + 1 + i).wait_recv()

            @pl.when(z > 0)
            def _():
                hop(kind, buf, "l", i + 1, part, rows, z + 1 + i).start()

    def handed_on(kind, buf, c, part, rows):
        @pl.when((c < z) & (z < NT - 1))
        def _():
            hop(kind, buf, "r", z - c, part, rows, c).wait_send()

        @pl.when((c > z) & (z > 0))
        def _():
            hop(kind, buf, "l", c - z, part, rows, c).wait_send()

    halves = [slice(i * QB, (i + 1) * QB) for i in range(R // QB)]

    V = pltpu.VMEM
    x_in, cot_in = xs.at[0], cotg.at[z]
    loads = [
        pltpu.make_async_copy(src, dst, lsem.at[i])
        for i, (src, dst) in enumerate(
            [
                (x_hbm, x_in),
                (cot_hbm, cot_in),
                (eg_hbm, wgu.at[: p.EB, : p.B]),
                (eu_hbm, wgu.at[: p.EB, p.B :]),
                (ed_hbm, wd.at[: p.EB]),
                (sg_hbm, wguT.at[p.EB, :, : p.B]),
                (su_hbm, wguT.at[p.EB, :, p.B :]),
                (sd_hbm, wd.at[p.EB]),
            ]
        )
    ]
    for c in loads:
        c.start()
    barrier = pltpu.get_barrier_semaphore()
    for k in (1, 2, 3):
        pl.semaphore_signal(barrier, inc=1, device_id=to_z(k), device_id_type=MESH)

    def greet(j, carry):
        pl.semaphore_signal(barrier, inc=1, device_id=(lax.rem(dp + j, p.nd), z), device_id_type=MESH)
        return carry

    lax.fori_loop(1, p.nd, greet, 0)
    pl.semaphore_wait(barrier, 3 + p.nd - 1)

    member = lax.rem(dp, 8)
    quad = lax.div(member, 2)

    def w_rows(matrix, at, side):
        start = at * p.HC + side * (p.HC // 2)
        return wfull.at[matrix, pl.ds(pl.multiple_of(start, 16), p.HC // 2)]

    def w_copy(k, at):
        part = w_rows(quad, at, core)
        return remote(part, part, "w", k - 1, to_z(k))

    def f_copy(k, j, matrix):
        part = w_rows(matrix, zk[k], core)
        there = dp - member + 2 * lax.rem(quad + j, 4) + core
        return remote(part, part, "f", (k - 1) * 3 + j - 1, (there, z))

    def g_copy(k, j, side):
        part = w_rows(lax.rem(quad + 4 - j, 4), zk[k], side)
        return remote(part, part, "g", (k - 1) * 4 + j, (mate, z))

    own_cols = pl.ds(pl.multiple_of(z * p.HC, 32), p.HC)
    for m, ref in enumerate((wq_ref, wk_ref, wv_ref, wo_ref)):
        wfull[m, own_cols] = ref[...]
    for k in (1, 2, 3):
        w_copy(k, z).start()
    loads[0].wait()
    x_copy = remote(xs.at[0], xs.at[1], "x", 0, (dp, z + 1 - 2 * zlo))
    late = zlo == 1

    @pl.when(zlo == 0)
    def _():
        x_copy.start()

    gain_attn = gain_attn_ref[...].astype(F32)[None]
    gain_ffn = gain_ffn_ref[...].astype(F32)[None]
    rext32[0 : p.E] = router_ref[...].astype(F32)
    vec = vec_ref[...].astype(F32)[None]
    rext32[p.E : p.E + 1] = vec
    rext32[p.E + 1 : p.E + 2] = vec
    rext32[p.E + 2 :] = jnp.zeros((14 - p.E, W), F32)
    rext[...] = rext32[...].astype(BF)
    rextT[...] = jnp.concatenate([rext32[...], jnp.zeros((LANES - 16, W), F32)], axis=0).T.astype(BF)

    for k in (1, 2, 3):
        w_copy(k, zk[k]).wait_recv()
        for j in (1, 2, 3):
            f_copy(k, j, quad).start()
        g_copy(k, 0, core).start()

    length = len_ref[lax.div(z, 2)]
    for i in range(R // QB):
        key = lax.broadcasted_iota(jnp.int32, (QB, R), 0) + i * QB
        query = lax.broadcasted_iota(jnp.int32, (QB, R), 1)
        bias[i * QB : (i + 1) * QB] = jnp.where((key <= query) & (key + half_own * R < length), 0.0, NEG)
    v = x_in[...].astype(F32)
    xn[0] = (v * inv_rms(v) * gain_attn).astype(BF)

    for c in loads[1:]:
        c.wait()
    for i in range(2):
        at = slice(i * p.B, (i + 1) * p.B)
        wgu[p.EB, at] = wguT[p.EB, :, at].T

    def turn(b, carry):
        for i in range(2):
            at = slice(i * p.B, (i + 1) * p.B)
            wguT[b, :, at] = wgu[b, at].T
        wdT[b] = wd[b].T
        return carry

    lax.fori_loop(0, p.EB, turn, 0)
    wdT[p.EB] = wd[p.EB].T
    for k in (1, 2, 3):
        for j in (1, 2, 3):
            f_copy(k, j, lax.rem(quad + 4 - j, 4)).wait_recv()
            g_copy(k, j, core).start()
    send_own("c", cotg, 0, slice(None))
    for k in (1, 2, 3):
        for j in range(4):
            g_copy(k, j, 1 - core).wait_recv()

    own_pos = pl.ds(pl.multiple_of(half_own * R, R), R)
    lane = lax.broadcasted_iota(jnp.int32, (1, LANES), 1)
    low_half = lax.rem(lane, HD) < HD // 2

    def swap_halves(v):
        return jnp.where(low_half, pltpu.roll(v, LANES - HD // 2, 1), pltpu.roll(v, HD // 2, 1))

    q_pre = nt(wfull[0], xn[0])
    cos_own, sin_own = cost[:, own_pos], sint[:, own_pos]
    for h in range(W // HD):
        a = q_pre[h * HD : h * HD + HD // 2]
        b = q_pre[h * HD + HD // 2 : (h + 1) * HD]
        qT[h * HD : h * HD + HD // 2] = ((a * cos_own - b * sin_own) * (SCALE * LOG2E)).astype(BF)
        qT[h * HD + HD // 2 : (h + 1) * HD] = ((a * sin_own + b * cos_own) * (SCALE * LOG2E)).astype(BF)

    def keys_values(slot, start):
        def project(i, carry):
            rows = pl.ds(pl.multiple_of(i * QB, QB), QB)
            at = pl.ds(pl.multiple_of(start + i * QB, QB), QB)
            xb = xn[slot, rows]
            k_pre = nt(xb, wfull[1])
            v_pre = nt(xb, wfull[2])
            c, s = cosk[at], sink[at]
            for g in range(NG):
                kg = k_pre[:, g * LANES : (g + 1) * LANES]
                kN[slot, g, rows] = (kg * c + swap_halves(kg) * s).astype(BF)
                vN[slot, g, rows] = v_pre[:, g * LANES : (g + 1) * LANES].astype(BF)
            return carry

        lax.fori_loop(0, R // QB, project, 0)
        for g in range(NG):
            kvT[slot, g * LANES : (g + 1) * LANES] = vN[slot, g].T

    keys_values(0, half_own * R)
    for g in range(NG):
        qN[g] = qT[g * LANES : (g + 1) * LANES].T

    head_row = lax.div(lax.broadcasted_iota(jnp.int32, (LANES, 1), 0), HD)
    head_lane = lax.div(lane, HD)
    HPG = LANES // HD

    def one_head(ref, g, h, cols):
        v = ref[pl.ds(pl.multiple_of(g * LANES, LANES), LANES), cols]
        return jnp.where(head_row == h, v, jnp.zeros_like(v))

    def rows_of(g, h):
        return pl.ds(pl.multiple_of(g * LANES + h * HD, HD), HD)

    every = slice(0, R)

    def early_bias(n):
        one = jnp.where(lax.broadcasted_iota(jnp.int32, (R, LANES), 0) < length, 0.0, NEG)
        return jnp.concatenate([one] * (n // LANES), axis=1)

    def softmax_heads(slot, g, keys, cols, addend):
        scores, parts, found = {}, {}, []
        for step in range(HPG + 2):
            if step < HPG:
                scores[step] = nn(kN[slot, g, keys], one_head(qT, g, step, cols)) + addend
            if 1 <= step <= HPG:
                s = scores.pop(step - 1)
                top = jnp.max(s, axis=0, keepdims=True)
                e = jnp.exp2(s - top)
                parts[step - 1] = top, jnp.sum(e, axis=0, keepdims=True), e.astype(BF)
            if step >= 2:
                top, total, e = parts.pop(step - 2)
                found.append((top, total, nn(kvT[slot, rows_of(g, step - 2), keys], e)))
        return found

    def own_keys(g, carry):
        for qb in range(R // QB):
            keys, cols = slice(0, (qb + 1) * QB), halves[qb]
            for h, found in enumerate(softmax_heads(0, g, keys, cols, bias[keys, cols])):
                head = pl.ds(g * HPG + h, 1)
                lse[head, cols], delta[head, cols], o_acc[rows_of(g, h), cols] = found
        return carry

    lax.fori_loop(0, NG, own_keys, 0)
    arrive("c", cotg, 0, 0, slice(None))

    @pl.when(late)
    def _():
        x_copy.wait_recv()
        v = xs[1].astype(F32)
        xn[1] = (v * inv_rms(v) * gain_attn).astype(BF)
        keys_values(1, 0)

    def early_keys(g, carry):
        for h, (top, total, o) in enumerate(softmax_heads(1, g, every, every, early_bias(R))):
            head = pl.ds(g * HPG + h, 1)
            old = lse[head]
            new = jnp.maximum(top, old)
            keep_old, keep_new = jnp.exp2(old - new), jnp.exp2(top - new)
            lse[head] = new
            delta[head] = delta[head] * keep_old + total * keep_new
            at = rows_of(g, h)
            o_acc[at] = o_acc[at] * keep_old + o * keep_new
        return carry

    @pl.when(late)
    def _():
        lax.fori_loop(0, NG, early_keys, 0)

    for qb in range(R // QB):
        rows = halves[qb]
        for h in range(W // HD):
            at = slice(h * HD, (h + 1) * HD)
            oT[at, rows] = (o_acc[at, rows] * (1.0 / delta[h : h + 1, rows])).astype(BF)
        lse[0 : W // HD, rows] = lse[0 : W // HD, rows] + jnp.log(delta[0 : W // HD, rows]) * LOG2E
        m = x_in[rows].astype(F32) + nn(oT[:, rows].T, wfull[3])
        mid[rows] = m
        normg[z, rows] = (m * inv_rms(m) * gain_ffn).astype(BF)
        send_own("n", normg, qb, rows)
    for g in range(NG):
        at = slice(g * LANES, (g + 1) * LANES)
        kvT[0, at] = kN[0, g].T

        @pl.when(late)
        def _(g=g, at=at):
            kvT[1, at] = kN[1, g].T

    def zero_acc(i, carry):
        acc[pl.ds(pl.multiple_of(i * 16, 16), 16)] = jnp.zeros((16, W), F32)
        return carry

    lax.fori_loop(0, 3 * p.NB * W // 16, zero_acc, 0)
    drext[...] = jnp.zeros_like(drext)
    zhi = lax.div(z, 2)

    def chunk_of(k):
        return 2 * lax.rem(zhi + lax.div(k, 2), 2) + lax.rem(zlo + lax.rem(k, 2), 2)

    def chip_rows(j):
        return pl.ds(pl.multiple_of(chip_at(j) * p.pr, 16), p.pr)

    def owner(c):
        return (lambda f: f()) if p.owners == p.nc else pl.when(c < p.owners)

    owns = owner(chip)

    def h1_copy(b):
        return remote(stage.at[b], h1.at[b], "h1", b, (mate, z))

    def h2_copy(b, j):
        i = b * (p.nc - 1) + j - 1
        return remote(h1.at[b, :, chip_rows(j)], h2.at[j - 1, b], "h2", i, on_chip(j))

    def h3_copy(b, j):
        i = b * (p.nc - 1) + j - 1
        return remote(fin.at[b], res.at[b, :, core, chip_rows(0)], "h3", i, on_chip(j))

    def h4_copy(b, j):
        part = res.at[b, :, core, chip_rows(j)]
        return remote(fin.at[b] if j == 0 else part, part, "h4", b * p.nc + j, (mate, z))

    def keep(b):
        return pltpu.make_async_copy(fin.at[b], res.at[b, :, core, chip_rows(0)], lsem.at[b])

    def block_half(b, kind, side, turned=False):
        first = (3 * b + kind) * W
        if not turned:
            return acc[pl.ds(pl.multiple_of(first + side * p.hp, p.hp), p.hp)]
        v = acc[pl.ds(pl.multiple_of(first, W), W)].T
        return jnp.where(side == 0, v[: p.hp], v[p.hp :])

    def each_half(b, side, step):
        step(2, block_half(b, 2, side))

        @pl.when(b < p.EB)
        def _():
            for kind in range(2):
                step(kind, block_half(b, kind, side))

        @pl.when(b == p.EB)
        def _():
            for kind in range(2):
                step(kind, block_half(b, kind, side, True))

    def mate_half(b):
        def step(kind, v):
            stage[b, kind] = v.astype(BF)

        each_half(b, 1 - core, step)
        h1_copy(b).start()

    def to_chips(b):
        h1_copy(b).wait_recv()

        def step(kind, v):
            h1[b, kind] = (v + h1[b, kind].astype(F32)).astype(BF)

        each_half(b, core, step)
        for j in range(1, p.nc):
            owner(chip_at(j))(lambda j=j: h2_copy(b, j).start())

    def from_chips(b):
        @owns
        def _():
            for j in range(1, p.nc):
                h2_copy(b, j).wait_recv()
            for kind in range(3):
                v = h1[b, kind, chip_rows(0)].astype(F32)
                for j in range(1, p.nc):
                    v += h2[j - 1, b, kind].astype(F32)
                fin[b, kind] = v.astype(BF)
            for j in range(1, p.nc):
                h3_copy(b, j).start()
            h4_copy(b, 0).start()
            keep(b).start()

    def hand_over(b):
        for j in range(1, p.nc):
            sender = lax.rem(chip + p.nc - j, p.nc)

            @owner(sender)
            def _(j=j):
                h3_copy(b, j).wait_recv()
                h4_copy(b, p.nc - j).start()

    def unit(gates, xT, gT, out_acc, dx_acc, last, part, k, carry):
        c = chunk_of(k)
        n = part.stop - part.start

        xT[...] = normg[c, part].T
        gT[...] = cotg[c, part].T
        logits = nn(rext[...], xT[...])
        down = lax.broadcasted_iota(jnp.int32, (16, n), 0)
        is_expert = down < p.E
        lg = jnp.where(is_expert, logits, NEG)
        ex = jnp.exp(lg - jnp.max(lg, axis=0, keepdims=True))
        route = ex / jnp.sum(ex, axis=0, keepdims=True)
        at = pl.ds(pl.multiple_of(c * R + part.start, n), n)
        named = (down == ids_ref[0:1, at]) | (down == ids_ref[1:2, at]) | ((down >= p.E) & (down < p.E + 2))
        chosen = jnp.where(named, 1.0, 0.0)
        gate = jnp.where(is_expert, route, lax.logistic(logits)) * chosen
        gates[0] = chosen
        gates[1] = route
        gates[2] = gate
        gates[3] = jnp.zeros_like(gate)
        out_acc[...] = jnp.zeros_like(out_acc)
        dx_acc[...] = jnp.zeros_like(dx_acc)

        def block(b, carry):
            if not last:

                @pl.when((b == 1) & (k > 0))
                def _():
                    arrive("c", cotg, k, 0, slice(None))

                @pl.when(b == 2)
                def _():
                    arrive("n", normg, k, 0, halves[0])

                @pl.when(b == 4)
                def _():
                    arrive("n", normg, k, 1, halves[1])

            au = nn(wgu[b], xT[...])
            hg = nn(wd[b], gT[...])
            h_parts, a_parts, u_parts = [], [], []
            for e in range(2):
                expert = pl.ds(2 * b + e, 1)
                gc = gates[2, expert]
                sums = 0.0
                for first in range(e * p.eff, (e + 1) * p.eff, TILE):
                    rows = slice(first, first + TILE)
                    a, u, back = au[rows], au[p.B + first : p.B + first + TILE], hg[rows]
                    sig = 0.5 * jnp.tanh(0.5 * a) + 0.5
                    act = a * sig
                    slope = sig + act * (1.0 - sig)
                    h = act * u
                    sums += jnp.sum((h * back).reshape(TILE // 8, 8, n), axis=0)
                    scaled = back * gc
                    h_parts.append((h * gc).astype(BF))
                    a_parts.append((scaled * u * slope).astype(BF))
                    u_parts.append((scaled * act).astype(BF))
                gates[3, expert] = jnp.sum(sums, axis=0, keepdims=True)
            hs = jnp.concatenate(h_parts, axis=0)
            dau = jnp.concatenate(a_parts + u_parts, axis=0)
            out_acc[...] += nn(wdT[b], hs)
            dx_acc[...] += nn(wguT[b], dau)
            acc[pl.ds(pl.multiple_of(3 * b * W, W), 2 * W)] += nn(dau, normg[c, part])
            acc[pl.ds(pl.multiple_of((3 * b + 2) * W, W), W)] += nn(hs, cotg[c, part])

            if last == 1:
                mate_half(b)
                pl.when(b > 0)(lambda: to_chips(b - 1))

            return carry

        lax.fori_loop(0, p.NB, block, 0)
        chosen, route, gate = gates[0], gates[1], gates[2]
        rg = gates[3] * chosen
        dot = jnp.sum(jnp.where(is_expert, route * rg, 0.0), axis=0, keepdims=True)
        lgrad = jnp.where(is_expert, route * (rg - dot), rg * gate * (1.0 - gate))
        drext[...] += nn(lgrad.astype(BF), normg[c, part])
        lwide = jnp.concatenate([lgrad, jnp.zeros((LANES - 16, n), F32)], axis=0).astype(BF)
        dx = dx_acc[...] + nn(rextT[...], lwide)
        if last != 1:
            for b in range(R // QB):
                handed_on("n", normg, c, b, halves[b])
            handed_on("c", cotg, c, 0, slice(None))

        if not last:

            @pl.when(k == 0)
            def _():
                dx_own[...] = dx.T
                out_own[...] = out_acc[...].astype(BF).T

        @pl.when(k > 0)
        def _():
            normg[c, part] = dx.astype(BF).T
            cotg[c, part] = out_acc[...].astype(BF).T
            remote(normg.at[c, part], dxr.at[k - 1, part], "dx", NT - last if last else k - 1, (dp, c)).start()

        return carry

    def chunks(n, body):
        pl.run_scoped(body, V((4, 16, n), F32), V((W, n), BF), V((W, n), BF), V((W, n), F32), V((W, n), F32))

    chunks(R, lambda *refs: lax.fori_loop(0, NT - 1, functools.partial(unit, *refs, 0, every), 0) and None)
    for i, part in enumerate(halves):
        chunks(QB, lambda *refs, i=i, part=part: unit(*refs, len(halves) - i, part, NT - 1, 0) and None)
    to_chips(p.NB - 1)

    def dx_copies():
        copies = [remote(normg.at[zk[k]], dxr.at[k - 1], "dx", k - 1, to_z(k)) for k in range(1, NT - 1)]
        for i, part in enumerate(halves):
            at = normg.at[zk[NT - 1], part]
            copies.append(remote(at, dxr.at[NT - 2, part], "dx", NT - len(halves) + i, to_z(NT - 1)))
        return copies

    def chips(b, carry):
        from_chips(b)
        return carry

    lax.fori_loop(0, p.NB - 2, chips, 0)
    for copy in dx_copies():
        copy.wait_recv()
    def o_next(i):
        return remote(cotg.at[zk[1 + 2 * i]], outr.at[i], "o", i, to_z(1))

    def o_far():
        return remote(cotg.at[zk[2]], outr.at[2], "o", 2, to_z(2))

    for i in (1, 0):
        o_next(i).start()

    dn = dx_own[...] + dxr[0].astype(F32) + dxr[1].astype(F32) + dxr[2].astype(F32)
    mid_back, dgain = rms_back(mid[...], dn, gain_ffn)
    sm_own = jnp.sum(dgain, axis=0, keepdims=True)
    mg = cot_in[...].astype(F32) + mid_back
    dx_own[...] = mg
    ag = mg.astype(BF)
    agrad[...] = ag
    dO = nt(ag, wfull[3])
    for g in range(NG):
        dON[g] = dO[:, g * LANES : (g + 1) * LANES].astype(BF)
    dOt = nt(wfull[3], ag).astype(BF)
    dOT[...] = dOt
    both = dOt.astype(F32) * oT[...].astype(F32)
    for h in range(W // HD):
        delta[h : h + 1] = jnp.sum(both[h * HD : (h + 1) * HD], axis=0, keepdims=True)

    dw = [acc.at[m * W : (m + 1) * W] for m in range(4)]
    dxn, dxn_early = acc.at[4 * W : 4 * W + R], acc.at[4 * W + R : 4 * W + 2 * R]
    dw[3][...] = nn(oT[...], agrad[...])
    dw[1][...] = jnp.zeros((W, W), F32)
    dw[2][...] = jnp.zeros((W, W), F32)
    dxn[...] = jnp.zeros((R, W), F32)
    dxn_early[...] = jnp.zeros((R, W), F32)
    o_acc[...] = jnp.zeros_like(o_acc)
    pxs = agrad
    px_copy = remote(pxs, xs.at[1], "px", 0, (dp, z + 1 - 2 * zlo))

    def score_grads(pT, dsT, slot, g, keys, cols, addend, first):
        n = cols.stop - cols.start
        made, turned = {}, {}
        for step in range(HPG + 2):
            if step < HPG:
                s = nn(kN[slot, g, keys], one_head(qT, g, step, cols)) + addend
                made[step] = s, nn(vN[slot, g, keys], one_head(dOT, g, step, cols))
            if 1 <= step <= HPG:
                s, d_prob = made.pop(step - 1)
                head = pl.ds(g * HPG + step - 1, 1)
                prob = jnp.exp2(s - lse[head, cols])
                ds = (prob * (d_prob - delta[head, cols])).astype(BF)
                place = slice(first + (step - 1) * n, first + step * n)
                pT[keys, place] = prob.astype(BF)
                dsT[keys, place] = ds
                turned[step - 1] = ds
            if step >= 2:
                at = rows_of(g, step - 2)
                o_acc[at, cols] += nn(kvT[slot, at, keys], turned.pop(step - 2)) * SCALE

    def all_heads(ref, g, rows):
        v = ref[g, rows]
        return jnp.concatenate([jnp.where(head_lane == h, v, jnp.zeros_like(v)) for h in range(HPG)], axis=0)

    def unturn(dk, at):
        return (dk * cosk[at] - swap_halves(dk) * sink[at]).astype(BF)

    def keys_back(slot, g, at_g, dk, dv, sums):
        dv = dv.astype(BF)
        dw[1][at_g] += nn(dk.T, xn[slot])
        dw[2][at_g] += nn(dv.T, xn[slot])
        sums[...] += nn(dk, wfull[1, at_g]) + nn(dv, wfull[2, at_g])

    def f1_copy(g):
        return remote(A.at[g], f1.at[g], "f1", g, (mate, z))

    def f2_rows(j):
        return pl.ds(pl.multiple_of(chip_at(j) * 16, 16), 16)

    def f2_copy(g, j):
        i = g * (p.nc - 1) + j - 1
        return remote(f1.at[g, :, f2_rows(j)], f2.at[j - 1, g], "f2", i, on_chip(j))

    def sums_heads(c):
        return (lambda f: f()) if p.att_owners == p.nc else pl.when(c < p.att_owners)

    def home(g, side, c):
        head = HPG * g + (HPG // 2) * side + lax.div(c, 2)
        to = lax.div(head, p.HC // HD)
        return to, g * LANES + side * (LANES // 2) + c * 16 - to * p.HC

    def f3_copy(g, at):
        to, _ = home(g, core, chip)
        return remote(fD.at[g], f3.at[g, at], "f3", g * NT + at, (dp, to))

    def f4_copy(g, j, row):
        part = att.at[:, pl.ds(pl.multiple_of(row, 16), 16)]
        return remote(part, part, "f4", g * (p.nd - 1) + j - 1, (lax.rem(dp + j, p.nd), z))

    def head_half(g, m, side):
        at = g * LANES + side * (LANES // 2)
        return dw[m][pl.ds(pl.multiple_of(at, LANES // 2), LANES // 2)]

    def stage_heads(g):
        for m in range(4):
            A[g, m] = head_half(g, m, 1 - core).astype(BF)
        f1_copy(g).start()

    def heads_to_chips(g):
        f1_copy(g).wait_recv()
        for m in range(4):
            f1[g, m] = (head_half(g, m, core) + f1[g, m].astype(F32)).astype(BF)
        for j in range(1, p.nc):
            sums_heads(chip_at(j))(lambda j=j: f2_copy(g, j).start())

    def heads_along_z(g):
        @sums_heads(chip)
        def _():
            for j in range(1, p.nc):
                f2_copy(g, j).wait_recv()
            for m in range(4):
                v = f1[g, m, f2_rows(0)].astype(F32)
                for j in range(1, p.nc):
                    v += f2[j - 1, g, m].astype(F32)
                fD[g, m] = v.astype(BF)
            to, _ = home(g, core, chip)

            @pl.when(to != z)
            def _():
                f3_copy(g, z).start()

    def heads_home(g):
        @sums_heads(chip)
        def _():
            to, row = home(g, core, chip)

            @pl.when(to == z)
            def _():
                for at in range(NT):

                    @pl.when(at != z)
                    def _(at=at):
                        f3_copy(g, at).wait_recv()

                f3[g, z] = fD[g]
                for m in range(4):
                    v = f3[g, 0, m].astype(F32)
                    for at in range(1, NT):
                        v += f3[g, at, m].astype(F32)
                    att[m, pl.ds(pl.multiple_of(row, 16), 16)] = v.astype(BF)
                for j in range(1, p.nd):
                    f4_copy(g, j, row).start()

    lax.fori_loop(p.NB - 2, p.NB, chips, 0)

    def back(pT, dsT):
        @pl.when(late)
        def _():
            def early(g, carry):
                at_g = pl.ds(pl.multiple_of(g * LANES, LANES), LANES)
                score_grads(pT, dsT, 1, g, every, every, early_bias(R), 0)
                dv = nn(pT[...], all_heads(dON, g, every))
                dk = nn(dsT[...], all_heads(qN, g, every)) * LN2
                keys_back(1, g, at_g, unturn(dk, every), dv, dxn_early)
                return carry

            lax.fori_loop(0, NG, early, 0)
            pxs[...] = dxn_early[...].astype(BF)
            px_copy.start()

        def own(g, carry):
            @pl.when(g > 0)
            def _():
                heads_to_chips(g - 1)

            at_g = pl.ds(pl.multiple_of(g * LANES, LANES), LANES)
            for qb in range(R // QB):
                keys, cols = slice(0, (qb + 1) * QB), halves[qb]
                score_grads(pT, dsT, 0, g, keys, cols, bias[keys, cols], qb * HPG * QB)
            dk, dv = [], []
            for qb in range(R // QB):
                keys, place = slice(0, (qb + 1) * QB), slice(qb * HPG * QB, (qb + 1) * HPG * QB)
                dv.append(nn(pT[keys, place], all_heads(dON, g, halves[qb])))
                dk.append(nn(dsT[keys, place], all_heads(qN, g, halves[qb])))
            dv = jnp.concatenate([dv[0] + dv[1][:QB], dv[1][QB:]], axis=0)
            dk = jnp.concatenate([dk[0] + dk[1][:QB], dk[1][QB:]], axis=0) * LN2
            keys_back(0, g, at_g, unturn(dk, own_pos), dv, dxn)
            parts = []
            for h in range(HPG):
                a = o_acc[pl.ds(pl.multiple_of(g * LANES + h * HD, 16), HD // 2)]
                b = o_acc[pl.ds(pl.multiple_of(g * LANES + h * HD + HD // 2, 16), HD // 2)]
                parts += [a * cos_own + b * sin_own, b * cos_own - a * sin_own]
            dq = jnp.concatenate(parts, axis=0).astype(BF)
            dw[0][at_g] = nn(dq, xn[0])
            dxn[...] += nn(dq.T, wfull[0, at_g])
            stage_heads(g)
            return carry

        o_next(1).wait_recv()
        cotg[zk[2]] = (cotg[zk[2]].astype(F32) + outr[1].astype(F32)).astype(BF)
        o_far().start()
        lax.fori_loop(0, NG, own, 0)

    wide = V((R, HPG * R), BF)
    pl.run_scoped(back, wide, wide)

    def gain_part(slot, sums):
        v = xs[slot].astype(F32)
        return jnp.sum(sums[...] * (v * inv_rms(v)), axis=0, keepdims=True)

    rext32[0:1] = gain_part(0, dxn)

    @pl.when(late)
    def _():
        rext32[0:1] += gain_part(1, dxn_early)

    rext32[1:2] = sm_own
    rext32[2:16] = drext[0:14]
    smr[dp] = rext32[...].astype(BF)

    def small(j):
        there = lax.rem(dp + j, p.nd)
        return remote(smr.at[dp], smr.at[dp], "s1", j - 1, (there, z))

    for j in range(1, p.nd):
        small(j).start()

    heads_to_chips(NG - 1)
    for g in range(NG):
        heads_along_z(g)
    for g in range(NG - 1):
        heads_home(g)

    for j in range(1, p.nd):
        small(j).wait_recv()
    total = smr[0].astype(F32)
    for j in range(1, p.nd):
        total += smr[j].astype(F32)
    smz[z] = total

    def small_z(k):
        return remote(smz.at[z], smz.at[z], "s2", k - 1, to_z(k))

    for k in (1, 2, 3):
        small_z(k).start()
    heads_home(NG - 1)

    @pl.when(zlo == 0)
    def _():
        px_copy.wait_recv()
        dxn[...] += xs[1].astype(F32)

    dn = dxn[...]
    x_back, _ = rms_back(x_in[...].astype(F32), dn, gain_attn)
    din_ref[...] = dx_own[...] + x_back
    o_next(0).wait_recv()
    o_far().wait_recv()
    whole = mid[...] + (out_own[...].astype(F32) + outr[0].astype(F32) + outr[2].astype(F32))
    out_ref[...] = whole.astype(BF)

    for k in (1, 2, 3):
        small_z(k).wait_recv()
    sm_ref[...] = smz[0] + smz[1] + smz[2] + smz[3]

    def hand_all(b, carry):
        hand_over(b)
        return carry

    lax.fori_loop(0, p.NB, hand_all, 0)

    def mate_done(b, carry):
        for j in range(p.nc):
            owner(chip_at(j))(lambda j=j: h4_copy(b, j).wait_recv())
        return carry

    lax.fori_loop(0, p.NB, mate_done, 0)
    for g in range(NG):
        for j in range(1, p.nd):
            sender = lax.rem(dp + p.nd - j, p.nd)
            c, side = lax.div(sender, 2), lax.rem(sender, 2)

            @sums_heads(c)
            def _(g=g, j=j, c=c, side=side):
                to, row = home(g, side, c)
                pl.when(to == z)(lambda: f4_copy(g, j, row).wait_recv())

    for m in range(4):
        att_ref[m * p.HC : (m + 1) * p.HC] = att[m]

    for k in (1, 2, 3):
        w_copy(k, z).wait_send()
        for j in (1, 2, 3):
            f_copy(k, j, quad).wait_send()
        for j in range(4):
            g_copy(k, j, core).wait_send()
        small_z(k).wait_send()
    for copy in dx_copies() + [o_next(0), o_next(1), o_far()]:
        copy.wait_send()
    own_sent("c", cotg, 0, slice(None))
    for b in range(R // QB):
        own_sent("n", normg, b, halves[b])
    pl.when(zlo == 0)(lambda: x_copy.wait_send())
    pl.when(late)(lambda: px_copy.wait_send())
    for g in range(NG):
        f1_copy(g).wait_send()
        for j in range(1, p.nc):
            sums_heads(chip_at(j))(lambda g=g, j=j: f2_copy(g, j).wait_send())

        @sums_heads(chip)
        def _(g=g):
            to, row = home(g, core, chip)
            pl.when(to != z)(lambda: f3_copy(g, z).wait_send())

            @pl.when(to == z)
            def _():
                for j in range(1, p.nd):
                    f4_copy(g, j, row).wait_send()

    def sums_sent(b, carry):
        h1_copy(b).wait_send()
        for j in range(1, p.nc):
            owner(chip_at(j))(lambda j=j: h2_copy(b, j).wait_send())
            owns(lambda j=j: h3_copy(b, j).wait_send())
        owns(lambda: keep(b).wait())
        for j in range(p.nc):
            owner(chip_at(j))(lambda j=j: h4_copy(b, j).wait_send())
        return carry

    lax.fori_loop(0, p.NB, sums_sent, 0)
    for j in range(1, p.nd):
        small(j).wait_send()


def tables():
    half = HD // 2
    freqs = 10000.0 ** (-np.arange(half, dtype=np.float32) / np.float32(half))
    angles = np.arange(LEN, dtype=np.float32)[:, None] * freqs.astype(np.float32)[None, :]
    cosine, sine = np.cos(angles).astype(np.float32), np.sin(angles).astype(np.float32)
    reps = LANES // HD
    cos_wide = np.tile(np.concatenate([cosine, cosine], axis=1), (1, reps))
    sin_wide = np.tile(np.concatenate([-sine, sine], axis=1), (1, reps))
    return cos_wide, sin_wide, np.ascontiguousarray(cosine.T), np.ascontiguousarray(sine.T)


def per_device(
    nd,
    inputs,
    lengths,
    expert_ids,
    gain_attn,
    w_query,
    w_key,
    w_value,
    w_out,
    gain_ffn,
    router,
    shared_gate_vec,
    exp_gate,
    exp_up,
    exp_down,
    sh_gate,
    sh_up,
    sh_down,
    cotangent,
):
    R, W = inputs.shape
    experts, _, eff = exp_gate.shape
    ff = sh_gate.shape[1]
    p = Plan(nd, R, W, experts, eff, ff)
    number, names = sem_plan(p)
    eg = exp_gate.swapaxes(1, 2).reshape(p.EB, p.B, W)
    eu = exp_up.swapaxes(1, 2).reshape(p.EB, p.B, W)
    ed = exp_down.reshape(p.EB, p.B, W)
    cosk, sink, cost, sint = tables()
    vm = pl.BlockSpec(memory_space=pltpu.VMEM)
    hbm = pl.BlockSpec(memory_space=pl.ANY)
    V = pltpu.VMEM
    hc = W // HD
    scratch = [
        pltpu.SemaphoreType.DMA((number,)),
        pltpu.SemaphoreType.DMA((number,)),
        pltpu.SemaphoreType.DMA((8,)),
        V((4, W, W), BF),
        V((16, W), F32),
        V((16, W), BF),
        V((W, LANES), BF),
        V((2, R, W), BF),
        V((2, R, W), BF),
        V((NT, R, W), BF),
        V((NT, R, W), BF),
        V((p.NB, 2 * p.B, W), BF),
        V((p.NB, W, 2 * p.B), BF),
        V((p.NB, p.B, W), BF),
        V((p.NB, W, p.B), BF),
        V((W, R), BF),
        V((p.NG, R, LANES), BF),
        V((2, p.NG, R, LANES), BF),
        V((2, W, R), BF),
        V((2, p.NG, R, LANES), BF),
        V((W, R), BF),
        V((up16(hc), R), F32),
        V((R, R), F32),
        V((W, R), F32),
        V((R, W), F32),
        V((R, W), F32),
        V((R, W), BF),
        V((3, R, W), BF),
        V((3, R, W), BF),
        V((3 * p.NB * W, W), F32),
        V((16, W), F32),
        V((p.NB, 3, p.hp, W), BF),
        V((p.NB, 3, p.hp, W), BF),
        V((max(p.nc - 1, 1), p.NB, 3, p.pr, W), BF),
        V((p.NB, 3, p.pr, W), BF),
        V((R, W), BF),
        V((p.NG, R, LANES), BF),
        V((W, R), BF),
        V((up16(hc), R), F32),
        V((p.NG, 4, LANES // 2, W), BF),
        V((p.NG, 4, LANES // 2, W), BF),
        V((p.nc - 1, p.NG, 4, 16, W), BF),
        V((p.NG, 4, 16, W), BF),
        V((p.NG, NT, 4, 16, W), BF),
        V((4, p.HC, W), BF),
        V((nd, 16, W), BF),
        V((NT, 16, W), F32),
    ]
    results = pl.pallas_call(
        functools.partial(kernel, p, names),
        out_shape=[
            jax.ShapeDtypeStruct((R, W), BF),
            jax.ShapeDtypeStruct((R, W), F32),
            jax.ShapeDtypeStruct((2 * p.hp, W), BF),
            jax.ShapeDtypeStruct((16, W), F32),
            jax.ShapeDtypeStruct((p.NB, 3, 2, p.hp, W), BF),
        ],
        in_specs=[pl.BlockSpec(memory_space=pltpu.SMEM)] + [vm] * 9 + [hbm] * 8 + [vm] * 4,
        out_specs=[vm] * 4 + [hbm],
        scratch_shapes=scratch,
        compiler_params=pltpu.CompilerParams(collective_id=0, has_side_effects=True, vmem_limit_bytes=63 << 20),
        name="block",
    )(
        lengths,
        expert_ids.T,
        gain_attn,
        gain_ffn,
        router.T,
        shared_gate_vec,
        w_query.T,
        w_key.T,
        w_value.T,
        w_out,
        inputs,
        cotangent,
        eg,
        eu,
        ed,
        sh_gate,
        sh_up,
        sh_down,
        jnp.asarray(cosk),
        jnp.asarray(sink),
        jnp.asarray(cost),
        jnp.asarray(sint),
    )
    return widen(p, *results)


def widen_kernel(p, out_b, din, att, small, routed, shared, *outs):
    (out_o, din_o, ga_o, wq_o, wk_o, wv_o, wo_o, gf_o, ro_o, ve_o, eg_o, eu_o, ed_o, sg_o, su_o, sd_o) = outs
    step = pl.program_id(0)
    for c in range(2):
        rows = slice(c * p.hp, (c + 1) * p.hp)
        for kind, dst in enumerate((eg_o, eu_o, ed_o)):
            dst[0, rows] = routed[0, kind, c].astype(F32)

    @pl.when(step == 0)
    def _():
        out_o[...] = out_b[...]
        din_o[...] = din[...]
        for m, dst in enumerate((wq_o, wk_o, wv_o, wo_o)):
            dst[...] = att[m * p.HC : (m + 1) * p.HC].astype(F32)
        ga_o[...] = small[0]
        gf_o[...] = small[1]
        ro_o[...] = small[2 : 2 + p.E]
        ve_o[...] = small[2 + p.E] + small[3 + p.E]
        for c in range(2):
            rows = slice(c * p.hp, (c + 1) * p.hp)
            for kind, dst in enumerate((sg_o, su_o, sd_o)):
                dst[rows] = shared[0, kind, c].astype(F32)


def widen(p, *results):
    R, W = p.R, p.W

    def whole(shape):
        return pl.BlockSpec(shape, lambda i: (0,) * len(shape))

    def split(shape):
        return pl.BlockSpec((1,) + shape[1:], lambda i: (i,) + (0,) * (len(shape) - 1))

    block = (1, 3, 2, p.hp, W)
    routed = (p.EB, p.B, W)
    row, head, sh = (W,), (p.HC, W), (W, W)
    shapes = [(R, W), (R, W), row, head, head, head, head, row, (p.E, W), row, routed, routed, routed, sh, sh, sh]
    out = pl.pallas_call(
        functools.partial(widen_kernel, p),
        grid=(p.EB,),
        out_shape=[jax.ShapeDtypeStruct(s, BF if i == 0 else F32) for i, s in enumerate(shapes)],
        in_specs=[whole((R, W))] * 2
        + [whole((2 * p.hp, W)), whole((16, W))]
        + [pl.BlockSpec(block, lambda i: (i, 0, 0, 0, 0)), pl.BlockSpec(block, lambda i: (p.EB, 0, 0, 0, 0))],
        out_specs=[split(s) if s == routed else whole(s) for s in shapes],
        compiler_params=pltpu.CompilerParams(vmem_limit_bytes=63 << 20),
        name="widen",
    )(*results, results[-1])
    out = list(out)
    for i in (3, 4, 5, 8):
        out[i] = out[i].T
    for i in (10, 11, 12):
        out[i] = out[i].reshape(p.E, p.eff, W)
    for i in (10, 11):
        out[i] = out[i].swapaxes(1, 2)
    return tuple(out)


def solution(mesh):
    rows = P(("dp", "tensor"), None)
    cols = P(None, "tensor")
    deep = P(None, None, "tensor")
    weights = (cols, cols, cols, P("tensor", None))
    experts = (deep, deep, P(None, "tensor", None), cols, cols, P("tensor", None))
    in_specs = (rows, P("dp"), P("dp", None), P()) + weights + (P(), P(), P()) + experts + (rows,)
    out_specs = (rows, rows, P()) + weights + (P(), P(), P()) + experts
    return jax.shard_map(
        functools.partial(per_device, mesh.shape["dp"]),
        mesh=mesh,
        in_specs=in_specs,
        out_specs=out_specs,
        check_vma=False,
    )
```

```python
import functools

import jax
import jax.numpy as jnp
import numpy as np
from jax import lax
from jax.experimental import pallas as pl
from jax.experimental.pallas import tpu as pltpu
from jax.sharding import PartitionSpec as P

HD = 32
LEN = 1024
NT = 4
LANES = 128
QB = 256
TILE = 32
BF = jnp.bfloat16
F32 = jnp.float32
MESH = pl.DeviceIdType.MESH
NEG = -1e30
SCALE = HD**-0.5
LOG2E = 1.4426950408889634
LN2 = 0.6931471805599453


def nn(a, b):
    return lax.dot_general(a, b, (((1,), (0,)), ((), ())), preferred_element_type=F32)


def nt(a, b):
    return lax.dot_general(a, b, (((1,), (1,)), ((), ())), preferred_element_type=F32)


def inv_rms(v):
    return lax.rsqrt(jnp.mean(v * v, axis=-1, keepdims=True) + 1e-06)


def rms_back(v, grad, gain):
    r = inv_rms(v)
    u = v * r
    g = grad * gain
    return r * (g - u * jnp.mean(g * u, axis=-1, keepdims=True)), grad * u


def up16(n):
    return -(-n // 16) * 16


class Plan:
    def __init__(self, nd, rows, width, experts, eff, ff):
        self.nd, self.R, self.W = nd, rows, width
        self.G = NT * rows
        self.NG = width // LANES
        self.HC = width // NT
        self.B = 2 * eff
        self.EB = experts // 2
        self.NB = self.EB + 1
        assert ff == self.B == width and LEN == 2 * rows
        self.E, self.eff, self.ff = experts, eff, ff
        assert nd % 8 == 0
        self.nc = nd // 2
        self.hp = 2 * self.HC
        assert 2 * self.hp == width == self.B
        self.pr = max(16, self.hp // self.nc)
        self.owners = self.hp // self.pr
        self.att_owners = LANES // 32
        assert self.owners * self.pr == self.hp and self.pr % 16 == 0 and self.owners <= self.nc


class Sems:
    def __init__(self):
        self.n = 0

    def take(self, n):
        base = self.n
        self.n += n
        return base


def sem_plan(p):
    s, names = Sems(), {}
    names["w"] = s.take(3)
    names["f"] = s.take(9)
    names["g"] = s.take(12)
    names["x"] = s.take(1)
    for way in "rl":
        names["c" + way] = s.take(4)
        names["n" + way] = s.take(8)
    names["dx"] = s.take(4)
    names["o"] = s.take(3)
    names["h1"] = s.take(p.NB)
    names["h2"] = s.take(p.NB * max(p.nc - 1, 1))
    names["h3"] = s.take(p.NB * max(p.nc - 1, 1))
    names["h4"] = s.take(p.NB * p.nc)
    names["px"] = s.take(1)
    names["f1"] = s.take(p.NG)
    names["f2"] = s.take(p.NG * (p.nc - 1))
    names["f3"] = s.take(p.NG * NT)
    names["f4"] = s.take(p.NG * (p.nd - 1))
    names["s1"] = s.take(p.nd - 1)
    names["s2"] = s.take(3)
    return s.n, names


def kernel(
    p,
    names,
    len_ref,
    ids_ref,
    gain_attn_ref,
    gain_ffn_ref,
    router_ref,
    vec_ref,
    wq_ref,
    wk_ref,
    wv_ref,
    wo_ref,
    x_hbm,
    cot_hbm,
    eg_hbm,
    eu_hbm,
    ed_hbm,
    sg_hbm,
    su_hbm,
    sd_hbm,
    cosk,
    sink,
    cost,
    sint,
    out_ref,
    din_ref,
    att_ref,
    sm_ref,
    res,
    send,
    recv,
    lsem,
    wfull,
    rext32,
    rext,
    rextT,
    xs,
    xn,
    cotg,
    normg,
    wgu,
    wguT,
    wd,
    wdT,
    qT,
    qN,
    kN,
    kvT,
    vN,
    oT,
    lse,
    bias,
    o_acc,
    mid,
    dx_own,
    out_own,
    dxr,
    outr,
    acc,
    drext,
    stage,
    h1,
    h2,
    fin,
    agrad,
    dON,
    dOT,
    delta,
    A,
    f1,
    f2,
    fD,
    f3,
    att,
    smr,
    smz,
):
    R, W, NG = p.R, p.W, p.NG
    dp, z = lax.axis_index("dp"), lax.axis_index("tensor")
    zlo = lax.rem(z, 2)
    zk = [z, z + 1 - 2 * zlo, lax.rem(z + 2, NT), NT - 1 - z]
    core = lax.rem(dp, 2)
    chip = lax.div(dp, 2)
    mate = dp + 1 - 2 * core
    half_own = zlo

    def remote(src, dst, kind, i, dev):
        j = names[kind] + i
        return pltpu.make_async_remote_copy(
            src_ref=src, dst_ref=dst, send_sem=send.at[j], recv_sem=recv.at[j], device_id=dev, device_id_type=MESH
        )

    def to_z(k):
        return (dp, zk[k])

    def chip_at(j):
        return lax.rem(chip + j, p.nc)

    def on_chip(j):
        return (2 * chip_at(j) + core, z)

    def hop(kind, buf, way, i, part, rows, at):
        there = (dp, z + 1) if way == "r" else (dp, z - 1)
        ref = buf.at[at, rows]
        parts = 1 if kind == "c" else R // QB
        return remote(ref, ref, kind + way, i * parts + part, there)

    def send_own(kind, buf, part, rows):
        @pl.when(z < NT - 1)
        def _():
            hop(kind, buf, "r", 0, part, rows, z).start()

        @pl.when(z > 0)
        def _():
            hop(kind, buf, "l", 0, part, rows, z).start()

    def own_sent(kind, buf, part, rows):
        @pl.when(z < NT - 1)
        def _():
            hop(kind, buf, "r", 0, part, rows, z).wait_send()

        @pl.when(z > 0)
        def _():
            hop(kind, buf, "l", 0, part, rows, z).wait_send()

    def arrive(kind, buf, i, part, rows):
        @pl.when(z - 1 - i >= 0)
        def _():
            hop(kind, buf, "r", i, part, rows, z - 1 - i).wait_recv()

            @pl.when(z < NT - 1)
            def _():
                hop(kind, buf, "r", i + 1, part, rows, z - 1 - i).start()

        @pl.when(z + 1 + i < NT)
        def _():
            hop(kind, buf, "l", i, part, rows, z + 1 + i).wait_recv()

            @pl.when(z > 0)
            def _():
                hop(kind, buf, "l", i + 1, part, rows, z + 1 + i).start()

    def handed_on(kind, buf, c, part, rows):
        @pl.when((c < z) & (z < NT - 1))
        def _():
            hop(kind, buf, "r", z - c, part, rows, c).wait_send()

        @pl.when((c > z) & (z > 0))
        def _():
            hop(kind, buf, "l", c - z, part, rows, c).wait_send()

    halves = [slice(i * QB, (i + 1) * QB) for i in range(R // QB)]

    V = pltpu.VMEM
    x_in, cot_in = xs.at[0], cotg.at[z]
    loads = [
        pltpu.make_async_copy(src, dst, lsem.at[i])
        for i, (src, dst) in enumerate(
            [
                (x_hbm, x_in),
                (cot_hbm, cot_in),
                (eg_hbm, wgu.at[: p.EB, : p.B]),
                (eu_hbm, wgu.at[: p.EB, p.B :]),
                (ed_hbm, wd.at[: p.EB]),
                (sg_hbm, wguT.at[p.EB, :, : p.B]),
                (su_hbm, wguT.at[p.EB, :, p.B :]),
                (sd_hbm, wd.at[p.EB]),
            ]
        )
    ]
    for c in loads:
        c.start()
    barrier = pltpu.get_barrier_semaphore()
    for k in (1, 2, 3):
        pl.semaphore_signal(barrier, inc=1, device_id=to_z(k), device_id_type=MESH)

    def greet(j, carry):
        pl.semaphore_signal(barrier, inc=1, device_id=(lax.rem(dp + j, p.nd), z), device_id_type=MESH)
        return carry

    lax.fori_loop(1, p.nd, greet, 0)
    pl.semaphore_wait(barrier, 3 + p.nd - 1)

    member = lax.rem(dp, 8)
    quad = lax.div(member, 2)

    def w_rows(matrix, at, side):
        start = at * p.HC + side * (p.HC // 2)
        return wfull.at[matrix, pl.ds(pl.multiple_of(start, 16), p.HC // 2)]

    def w_copy(k, at):
        part = w_rows(quad, at, core)
        return remote(part, part, "w", k - 1, to_z(k))

    def f_copy(k, j, matrix):
        part = w_rows(matrix, zk[k], core)
        there = dp - member + 2 * lax.rem(quad + j, 4) + core
        return remote(part, part, "f", (k - 1) * 3 + j - 1, (there, z))

    def g_copy(k, j, side):
        part = w_rows(lax.rem(quad + 4 - j, 4), zk[k], side)
        return remote(part, part, "g", (k - 1) * 4 + j, (mate, z))

    own_cols = pl.ds(pl.multiple_of(z * p.HC, 32), p.HC)
    for m, ref in enumerate((wq_ref, wk_ref, wv_ref, wo_ref)):
        wfull[m, own_cols] = ref[...]
    for k in (1, 2, 3):
        w_copy(k, z).start()
    loads[0].wait()
    x_copy = remote(xs.at[0], xs.at[1], "x", 0, (dp, z + 1 - 2 * zlo))
    late = zlo == 1

    @pl.when(zlo == 0)
    def _():
        x_copy.start()

    gain_attn = gain_attn_ref[...].astype(F32)[None]
    gain_ffn = gain_ffn_ref[...].astype(F32)[None]
    rext32[0 : p.E] = router_ref[...].astype(F32)
    vec = vec_ref[...].astype(F32)[None]
    rext32[p.E : p.E + 1] = vec
    rext32[p.E + 1 : p.E + 2] = vec
    rext32[p.E + 2 :] = jnp.zeros((14 - p.E, W), F32)
    rext[...] = rext32[...].astype(BF)
    rextT[...] = jnp.concatenate([rext32[...], jnp.zeros((LANES - 16, W), F32)], axis=0).T.astype(BF)

    for k in (1, 2, 3):
        w_copy(k, zk[k]).wait_recv()
        for j in (1, 2, 3):
            f_copy(k, j, quad).start()
        g_copy(k, 0, core).start()

    length = len_ref[lax.div(z, 2)]
    for i in range(R // QB):
        key = lax.broadcasted_iota(jnp.int32, (QB, R), 0) + i * QB
        query = lax.broadcasted_iota(jnp.int32, (QB, R), 1)
        bias[i * QB : (i + 1) * QB] = jnp.where((key <= query) & (key + half_own * R < length), 0.0, NEG)
    v = x_in[...].astype(F32)
    xn[0] = (v * inv_rms(v) * gain_attn).astype(BF)

    for c in loads[1:]:
        c.wait()
    for i in range(2):
        at = slice(i * p.B, (i + 1) * p.B)
        wgu[p.EB, at] = wguT[p.EB, :, at].T

    def turn(b, carry):
        for i in range(2):
            at = slice(i * p.B, (i + 1) * p.B)
            wguT[b, :, at] = wgu[b, at].T
        wdT[b] = wd[b].T
        return carry

    lax.fori_loop(0, p.EB, turn, 0)
    wdT[p.EB] = wd[p.EB].T
    for k in (1, 2, 3):
        for j in (1, 2, 3):
            f_copy(k, j, lax.rem(quad + 4 - j, 4)).wait_recv()
            g_copy(k, j, core).start()
    send_own("c", cotg, 0, slice(None))
    for k in (1, 2, 3):
        for j in range(4):
            g_copy(k, j, 1 - core).wait_recv()

    own_pos = pl.ds(pl.multiple_of(half_own * R, R), R)
    lane = lax.broadcasted_iota(jnp.int32, (1, LANES), 1)
    low_half = lax.rem(lane, HD) < HD // 2

    def swap_halves(v):
        return jnp.where(low_half, pltpu.roll(v, LANES - HD // 2, 1), pltpu.roll(v, HD // 2, 1))

    q_pre = nt(wfull[0], xn[0])
    cos_own, sin_own = cost[:, own_pos], sint[:, own_pos]
    for h in range(W // HD):
        a = q_pre[h * HD : h * HD + HD // 2]
        b = q_pre[h * HD + HD // 2 : (h + 1) * HD]
        qT[h * HD : h * HD + HD // 2] = ((a * cos_own - b * sin_own) * (SCALE * LOG2E)).astype(BF)
        qT[h * HD + HD // 2 : (h + 1) * HD] = ((a * sin_own + b * cos_own) * (SCALE * LOG2E)).astype(BF)

    def keys_values(slot, start):
        def project(i, carry):
            rows = pl.ds(pl.multiple_of(i * QB, QB), QB)
            at = pl.ds(pl.multiple_of(start + i * QB, QB), QB)
            xb = xn[slot, rows]
            k_pre = nt(xb, wfull[1])
            v_pre = nt(xb, wfull[2])
            c, s = cosk[at], sink[at]
            for g in range(NG):
                kg = k_pre[:, g * LANES : (g + 1) * LANES]
                kN[slot, g, rows] = (kg * c + swap_halves(kg) * s).astype(BF)
                vN[slot, g, rows] = v_pre[:, g * LANES : (g + 1) * LANES].astype(BF)
            return carry

        lax.fori_loop(0, R // QB, project, 0)
        for g in range(NG):
            kvT[slot, g * LANES : (g + 1) * LANES] = vN[slot, g].T

    keys_values(0, half_own * R)
    for g in range(NG):
        qN[g] = qT[g * LANES : (g + 1) * LANES].T

    head_row = lax.div(lax.broadcasted_iota(jnp.int32, (LANES, 1), 0), HD)
    head_lane = lax.div(lane, HD)
    HPG = LANES // HD

    def one_head(ref, g, h, cols):
        v = ref[pl.ds(pl.multiple_of(g * LANES, LANES), LANES), cols]
        return jnp.where(head_row == h, v, jnp.zeros_like(v))

    def rows_of(g, h):
        return pl.ds(pl.multiple_of(g * LANES + h * HD, HD), HD)

    every = slice(0, R)

    def early_bias(n):
        one = jnp.where(lax.broadcasted_iota(jnp.int32, (R, LANES), 0) < length, 0.0, NEG)
        return jnp.concatenate([one] * (n // LANES), axis=1)

    def softmax_heads(slot, g, keys, cols, addend):
        scores, parts, found = {}, {}, []
        for step in range(HPG + 2):
            if step < HPG:
                scores[step] = nn(kN[slot, g, keys], one_head(qT, g, step, cols)) + addend
            if 1 <= step <= HPG:
                s = scores.pop(step - 1)
                top = jnp.max(s, axis=0, keepdims=True)
                e = jnp.exp2(s - top)
                parts[step - 1] = top, jnp.sum(e, axis=0, keepdims=True), e.astype(BF)
            if step >= 2:
                top, total, e = parts.pop(step - 2)
                found.append((top, total, nn(kvT[slot, rows_of(g, step - 2), keys], e)))
        return found

    def own_keys(g, carry):
        for qb in range(R // QB):
            keys, cols = slice(0, (qb + 1) * QB), halves[qb]
            for h, found in enumerate(softmax_heads(0, g, keys, cols, bias[keys, cols])):
                head = pl.ds(g * HPG + h, 1)
                lse[head, cols], delta[head, cols], o_acc[rows_of(g, h), cols] = found
        return carry

    lax.fori_loop(0, NG, own_keys, 0)
    arrive("c", cotg, 0, 0, slice(None))

    @pl.when(late)
    def _():
        x_copy.wait_recv()
        v = xs[1].astype(F32)
        xn[1] = (v * inv_rms(v) * gain_attn).astype(BF)
        keys_values(1, 0)

    def early_keys(g, carry):
        for h, (top, total, o) in enumerate(softmax_heads(1, g, every, every, early_bias(R))):
            head = pl.ds(g * HPG + h, 1)
            old = lse[head]
            new = jnp.maximum(top, old)
            keep_old, keep_new = jnp.exp2(old - new), jnp.exp2(top - new)
            lse[head] = new
            delta[head] = delta[head] * keep_old + total * keep_new
            at = rows_of(g, h)
            o_acc[at] = o_acc[at] * keep_old + o * keep_new
        return carry

    @pl.when(late)
    def _():
        lax.fori_loop(0, NG, early_keys, 0)

    for qb in range(R // QB):
        rows = halves[qb]
        for h in range(W // HD):
            at = slice(h * HD, (h + 1) * HD)
            oT[at, rows] = (o_acc[at, rows] * (1.0 / delta[h : h + 1, rows])).astype(BF)
        lse[0 : W // HD, rows] = lse[0 : W // HD, rows] + jnp.log(delta[0 : W // HD, rows]) * LOG2E
        m = x_in[rows].astype(F32) + nn(oT[:, rows].T, wfull[3])
        mid[rows] = m
        normg[z, rows] = (m * inv_rms(m) * gain_ffn).astype(BF)
        send_own("n", normg, qb, rows)
    for g in range(NG):
        at = slice(g * LANES, (g + 1) * LANES)
        kvT[0, at] = kN[0, g].T

        @pl.when(late)
        def _(g=g, at=at):
            kvT[1, at] = kN[1, g].T

    def zero_acc(i, carry):
        acc[pl.ds(pl.multiple_of(i * 16, 16), 16)] = jnp.zeros((16, W), F32)
        return carry

    lax.fori_loop(0, 3 * p.NB * W // 16, zero_acc, 0)
    drext[...] = jnp.zeros_like(drext)
    zhi = lax.div(z, 2)

    def chunk_of(k):
        return 2 * lax.rem(zhi + lax.div(k, 2), 2) + lax.rem(zlo + lax.rem(k, 2), 2)

    def chip_rows(j):
        return pl.ds(pl.multiple_of(chip_at(j) * p.pr, 16), p.pr)

    def owner(c):
        return (lambda f: f()) if p.owners == p.nc else pl.when(c < p.owners)

    owns = owner(chip)

    def h1_copy(b):
        return remote(stage.at[b], h1.at[b], "h1", b, (mate, z))

    def h2_copy(b, j):
        i = b * (p.nc - 1) + j - 1
        return remote(h1.at[b, :, chip_rows(j)], h2.at[j - 1, b], "h2", i, on_chip(j))

    def h3_copy(b, j):
        i = b * (p.nc - 1) + j - 1
        return remote(fin.at[b], res.at[b, :, core, chip_rows(0)], "h3", i, on_chip(j))

    def h4_copy(b, j):
        part = res.at[b, :, core, chip_rows(j)]
        return remote(fin.at[b] if j == 0 else part, part, "h4", b * p.nc + j, (mate, z))

    def keep(b):
        return pltpu.make_async_copy(fin.at[b], res.at[b, :, core, chip_rows(0)], lsem.at[b])

    def block_half(b, kind, side, turned=False):
        first = (3 * b + kind) * W
        if not turned:
            return acc[pl.ds(pl.multiple_of(first + side * p.hp, p.hp), p.hp)]
        v = acc[pl.ds(pl.multiple_of(first, W), W)].T
        return jnp.where(side == 0, v[: p.hp], v[p.hp :])

    def each_half(b, side, step):
        step(2, block_half(b, 2, side))

        @pl.when(b < p.EB)
        def _():
            for kind in range(2):
                step(kind, block_half(b, kind, side))

        @pl.when(b == p.EB)
        def _():
            for kind in range(2):
                step(kind, block_half(b, kind, side, True))

    def mate_half(b):
        def step(kind, v):
            stage[b, kind] = v.astype(BF)

        each_half(b, 1 - core, step)
        h1_copy(b).start()

    def to_chips(b):
        h1_copy(b).wait_recv()

        def step(kind, v):
            h1[b, kind] = (v + h1[b, kind].astype(F32)).astype(BF)

        each_half(b, core, step)
        for j in range(1, p.nc):
            owner(chip_at(j))(lambda j=j: h2_copy(b, j).start())

    def from_chips(b):
        @owns
        def _():
            for j in range(1, p.nc):
                h2_copy(b, j).wait_recv()
            for kind in range(3):
                v = h1[b, kind, chip_rows(0)].astype(F32)
                for j in range(1, p.nc):
                    v += h2[j - 1, b, kind].astype(F32)
                fin[b, kind] = v.astype(BF)
            for j in range(1, p.nc):
                h3_copy(b, j).start()
            h4_copy(b, 0).start()
            keep(b).start()

    def hand_over(b):
        for j in range(1, p.nc):
            sender = lax.rem(chip + p.nc - j, p.nc)

            @owner(sender)
            def _(j=j):
                h3_copy(b, j).wait_recv()
                h4_copy(b, p.nc - j).start()

    def unit(gates, xT, gT, out_acc, dx_acc, last, part, k, carry):
        c = chunk_of(k)
        n = part.stop - part.start

        xT[...] = normg[c, part].T
        gT[...] = cotg[c, part].T
        logits = nn(rext[...], xT[...])
        down = lax.broadcasted_iota(jnp.int32, (16, n), 0)
        is_expert = down < p.E
        lg = jnp.where(is_expert, logits, NEG)
        ex = jnp.exp(lg - jnp.max(lg, axis=0, keepdims=True))
        route = ex / jnp.sum(ex, axis=0, keepdims=True)
        at = pl.ds(pl.multiple_of(c * R + part.start, n), n)
        named = (down == ids_ref[0:1, at]) | (down == ids_ref[1:2, at]) | ((down >= p.E) & (down < p.E + 2))
        chosen = jnp.where(named, 1.0, 0.0)
        gate = jnp.where(is_expert, route, lax.logistic(logits)) * chosen
        gates[0] = chosen
        gates[1] = route
        gates[2] = gate
        gates[3] = jnp.zeros_like(gate)
        out_acc[...] = jnp.zeros_like(out_acc)
        dx_acc[...] = jnp.zeros_like(dx_acc)

        def block(b, carry):
            if not last:

                @pl.when((b == 1) & (k > 0))
                def _():
                    arrive("c", cotg, k, 0, slice(None))

                @pl.when(b == 2)
                def _():
                    arrive("n", normg, k, 0, halves[0])

                @pl.when(b == 4)
                def _():
                    arrive("n", normg, k, 1, halves[1])

            def made(e):
                rows = slice(e * p.eff, (e + 1) * p.eff)
                up = slice(p.B + e * p.eff, p.B + (e + 1) * p.eff)
                return nn(wgu[b, rows], xT[...]), nn(wgu[b, up], xT[...]), nn(wd[b, rows], gT[...])

            def worked(e, a_all, u_all, back_all):
                expert = pl.ds(2 * b + e, 1)
                gc = gates[2, expert]
                sums, h_parts, a_parts, u_parts = 0.0, [], [], []
                for first in range(0, p.eff, TILE):
                    rows = slice(first, first + TILE)
                    a, u, back = a_all[rows], u_all[rows], back_all[rows]
                    sig = 0.5 * jnp.tanh(0.5 * a) + 0.5
                    act = a * sig
                    slope = sig + act * (1.0 - sig)
                    h = act * u
                    sums += jnp.sum((h * back).reshape(TILE // 8, 8, n), axis=0)
                    scaled = back * gc
                    h_parts.append((h * gc).astype(BF))
                    a_parts.append((scaled * u * slope).astype(BF))
                    u_parts.append((scaled * act).astype(BF))
                gates[3, expert] = jnp.sum(sums, axis=0, keepdims=True)
                return [jnp.concatenate(v, axis=0) for v in (a_parts, u_parts, h_parts)]

            def weights_back(e, da, du, hs):
                for kind, v, rows in ((0, da, normg), (1, du, normg), (2, hs, cotg)):
                    at = pl.ds(pl.multiple_of((3 * b + kind) * W + e * p.eff, p.eff), p.eff)
                    acc[at] += nn(v, rows[c, part])

            products = [made(0), made(1)]
            first = worked(0, *products[0])
            weights_back(0, *first)
            second = worked(1, *products[1])
            da, du, hs = (jnp.concatenate(v, axis=0) for v in zip(first, second))
            out_acc[...] += nn(wdT[b], hs)
            dx_acc[...] += nn(wguT[b], jnp.concatenate([da, du], axis=0))
            weights_back(1, *second)

            if last == 1:
                mate_half(b)
                pl.when(b > 0)(lambda: to_chips(b - 1))

            return carry

        lax.fori_loop(0, p.NB, block, 0)
        chosen, route, gate = gates[0], gates[1], gates[2]
        rg = gates[3] * chosen
        dot = jnp.sum(jnp.where(is_expert, route * rg, 0.0), axis=0, keepdims=True)
        lgrad = jnp.where(is_expert, route * (rg - dot), rg * gate * (1.0 - gate))
        drext[...] += nn(lgrad.astype(BF), normg[c, part])
        lwide = jnp.concatenate([lgrad, jnp.zeros((LANES - 16, n), F32)], axis=0).astype(BF)
        dx = dx_acc[...] + nn(rextT[...], lwide)
        if last != 1:
            for b in range(R // QB):
                handed_on("n", normg, c, b, halves[b])
            handed_on("c", cotg, c, 0, slice(None))

        if not last:

            @pl.when(k == 0)
            def _():
                dx_own[...] = dx.T
                out_own[...] = out_acc[...].astype(BF).T

        @pl.when(k > 0)
        def _():
            normg[c, part] = dx.astype(BF).T
            cotg[c, part] = out_acc[...].astype(BF).T
            remote(normg.at[c, part], dxr.at[k - 1, part], "dx", NT - last if last else k - 1, (dp, c)).start()

        return carry

    def chunks(n, body):
        pl.run_scoped(body, V((4, 16, n), F32), V((W, n), BF), V((W, n), BF), V((W, n), F32), V((W, n), F32))

    chunks(R, lambda *refs: lax.fori_loop(0, NT - 1, functools.partial(unit, *refs, 0, every), 0) and None)
    for i, part in enumerate(halves):
        chunks(QB, lambda *refs, i=i, part=part: unit(*refs, len(halves) - i, part, NT - 1, 0) and None)
    to_chips(p.NB - 1)

    def dx_copies():
        copies = [remote(normg.at[zk[k]], dxr.at[k - 1], "dx", k - 1, to_z(k)) for k in range(1, NT - 1)]
        for i, part in enumerate(halves):
            at = normg.at[zk[NT - 1], part]
            copies.append(remote(at, dxr.at[NT - 2, part], "dx", NT - len(halves) + i, to_z(NT - 1)))
        return copies

    def chips(b, carry):
        from_chips(b)
        return carry

    lax.fori_loop(0, p.NB - 2, chips, 0)
    for copy in dx_copies():
        copy.wait_recv()
    def o_next(i):
        return remote(cotg.at[zk[1 + 2 * i]], outr.at[i], "o", i, to_z(1))

    def o_far():
        return remote(cotg.at[zk[2]], outr.at[2], "o", 2, to_z(2))

    for i in (1, 0):
        o_next(i).start()

    dn = dx_own[...] + dxr[0].astype(F32) + dxr[1].astype(F32) + dxr[2].astype(F32)
    mid_back, dgain = rms_back(mid[...], dn, gain_ffn)
    sm_own = jnp.sum(dgain, axis=0, keepdims=True)
    mg = cot_in[...].astype(F32) + mid_back
    dx_own[...] = mg
    ag = mg.astype(BF)
    agrad[...] = ag
    dO = nt(ag, wfull[3])
    for g in range(NG):
        dON[g] = dO[:, g * LANES : (g + 1) * LANES].astype(BF)
    dOt = nt(wfull[3], ag).astype(BF)
    dOT[...] = dOt
    both = dOt.astype(F32) * oT[...].astype(F32)
    for h in range(W // HD):
        delta[h : h + 1] = jnp.sum(both[h * HD : (h + 1) * HD], axis=0, keepdims=True)

    dw = [acc.at[m * W : (m + 1) * W] for m in range(4)]
    dxn, dxn_early = acc.at[4 * W : 4 * W + R], acc.at[4 * W + R : 4 * W + 2 * R]
    dw[3][...] = nn(oT[...], agrad[...])
    dw[1][...] = jnp.zeros((W, W), F32)
    dw[2][...] = jnp.zeros((W, W), F32)
    dxn[...] = jnp.zeros((R, W), F32)
    dxn_early[...] = jnp.zeros((R, W), F32)
    o_acc[...] = jnp.zeros_like(o_acc)
    pxs = agrad
    px_copy = remote(pxs, xs.at[1], "px", 0, (dp, z + 1 - 2 * zlo))

    def score_grads(pT, dsT, slot, g, keys, cols, addend, first):
        n = cols.stop - cols.start
        made, turned = {}, {}
        for step in range(HPG + 2):
            if step < HPG:
                s = nn(kN[slot, g, keys], one_head(qT, g, step, cols)) + addend
                made[step] = s, nn(vN[slot, g, keys], one_head(dOT, g, step, cols))
            if 1 <= step <= HPG:
                s, d_prob = made.pop(step - 1)
                head = pl.ds(g * HPG + step - 1, 1)
                prob = jnp.exp2(s - lse[head, cols])
                ds = (prob * (d_prob - delta[head, cols])).astype(BF)
                place = slice(first + (step - 1) * n, first + step * n)
                pT[keys, place] = prob.astype(BF)
                dsT[keys, place] = ds
                turned[step - 1] = ds
            if step >= 2:
                at = rows_of(g, step - 2)
                o_acc[at, cols] += nn(kvT[slot, at, keys], turned.pop(step - 2)) * SCALE

    def all_heads(ref, g, rows):
        v = ref[g, rows]
        return jnp.concatenate([jnp.where(head_lane == h, v, jnp.zeros_like(v)) for h in range(HPG)], axis=0)

    def unturn(dk, at):
        return (dk * cosk[at] - swap_halves(dk) * sink[at]).astype(BF)

    def keys_back(slot, g, at_g, dk, dv, sums):
        dv = dv.astype(BF)
        dw[1][at_g] += nn(dk.T, xn[slot])
        dw[2][at_g] += nn(dv.T, xn[slot])
        sums[...] += nn(dk, wfull[1, at_g]) + nn(dv, wfull[2, at_g])

    def f1_copy(g):
        return remote(A.at[g], f1.at[g], "f1", g, (mate, z))

    def f2_rows(j):
        return pl.ds(pl.multiple_of(chip_at(j) * 16, 16), 16)

    def f2_copy(g, j):
        i = g * (p.nc - 1) + j - 1
        return remote(f1.at[g, :, f2_rows(j)], f2.at[j - 1, g], "f2", i, on_chip(j))

    def sums_heads(c):
        return (lambda f: f()) if p.att_owners == p.nc else pl.when(c < p.att_owners)

    def home(g, side, c):
        head = HPG * g + (HPG // 2) * side + lax.div(c, 2)
        to = lax.div(head, p.HC // HD)
        return to, g * LANES + side * (LANES // 2) + c * 16 - to * p.HC

    def f3_copy(g, at):
        to, _ = home(g, core, chip)
        return remote(fD.at[g], f3.at[g, at], "f3", g * NT + at, (dp, to))

    def f4_copy(g, j, row):
        part = att.at[:, pl.ds(pl.multiple_of(row, 16), 16)]
        return remote(part, part, "f4", g * (p.nd - 1) + j - 1, (lax.rem(dp + j, p.nd), z))

    def head_half(g, m, side):
        at = g * LANES + side * (LANES // 2)
        return dw[m][pl.ds(pl.multiple_of(at, LANES // 2), LANES // 2)]

    def stage_heads(g):
        for m in range(4):
            A[g, m] = head_half(g, m, 1 - core).astype(BF)
        f1_copy(g).start()

    def heads_to_chips(g):
        f1_copy(g).wait_recv()
        for m in range(4):
            f1[g, m] = (head_half(g, m, core) + f1[g, m].astype(F32)).astype(BF)
        for j in range(1, p.nc):
            sums_heads(chip_at(j))(lambda j=j: f2_copy(g, j).start())

    def heads_along_z(g):
        @sums_heads(chip)
        def _():
            for j in range(1, p.nc):
                f2_copy(g, j).wait_recv()
            for m in range(4):
                v = f1[g, m, f2_rows(0)].astype(F32)
                for j in range(1, p.nc):
                    v += f2[j - 1, g, m].astype(F32)
                fD[g, m] = v.astype(BF)
            to, _ = home(g, core, chip)

            @pl.when(to != z)
            def _():
                f3_copy(g, z).start()

    def heads_home(g):
        @sums_heads(chip)
        def _():
            to, row = home(g, core, chip)

            @pl.when(to == z)
            def _():
                for at in range(NT):

                    @pl.when(at != z)
                    def _(at=at):
                        f3_copy(g, at).wait_recv()

                f3[g, z] = fD[g]
                for m in range(4):
                    v = f3[g, 0, m].astype(F32)
                    for at in range(1, NT):
                        v += f3[g, at, m].astype(F32)
                    att[m, pl.ds(pl.multiple_of(row, 16), 16)] = v.astype(BF)
                for j in range(1, p.nd):
                    f4_copy(g, j, row).start()

    lax.fori_loop(p.NB - 2, p.NB, chips, 0)

    def back(pT, dsT):
        @pl.when(late)
        def _():
            def early(g, carry):
                at_g = pl.ds(pl.multiple_of(g * LANES, LANES), LANES)
                score_grads(pT, dsT, 1, g, every, every, early_bias(R), 0)
                dv = nn(pT[...], all_heads(dON, g, every))
                dk = nn(dsT[...], all_heads(qN, g, every)) * LN2
                keys_back(1, g, at_g, unturn(dk, every), dv, dxn_early)
                return carry

            lax.fori_loop(0, NG, early, 0)
            pxs[...] = dxn_early[...].astype(BF)
            px_copy.start()

        def own(g, carry):
            @pl.when(g > 0)
            def _():
                heads_to_chips(g - 1)

            at_g = pl.ds(pl.multiple_of(g * LANES, LANES), LANES)
            for qb in range(R // QB):
                keys, cols = slice(0, (qb + 1) * QB), halves[qb]
                score_grads(pT, dsT, 0, g, keys, cols, bias[keys, cols], qb * HPG * QB)
            dk, dv = [], []
            for qb in range(R // QB):
                keys, place = slice(0, (qb + 1) * QB), slice(qb * HPG * QB, (qb + 1) * HPG * QB)
                dv.append(nn(pT[keys, place], all_heads(dON, g, halves[qb])))
                dk.append(nn(dsT[keys, place], all_heads(qN, g, halves[qb])))
            dv = jnp.concatenate([dv[0] + dv[1][:QB], dv[1][QB:]], axis=0)
            dk = jnp.concatenate([dk[0] + dk[1][:QB], dk[1][QB:]], axis=0) * LN2
            keys_back(0, g, at_g, unturn(dk, own_pos), dv, dxn)
            parts = []
            for h in range(HPG):
                a = o_acc[pl.ds(pl.multiple_of(g * LANES + h * HD, 16), HD // 2)]
                b = o_acc[pl.ds(pl.multiple_of(g * LANES + h * HD + HD // 2, 16), HD // 2)]
                parts += [a * cos_own + b * sin_own, b * cos_own - a * sin_own]
            dq = jnp.concatenate(parts, axis=0).astype(BF)
            dw[0][at_g] = nn(dq, xn[0])
            dxn[...] += nn(dq.T, wfull[0, at_g])
            stage_heads(g)
            return carry

        o_next(1).wait_recv()
        cotg[zk[2]] = (cotg[zk[2]].astype(F32) + outr[1].astype(F32)).astype(BF)
        o_far().start()
        lax.fori_loop(0, NG, own, 0)

    wide = V((R, HPG * R), BF)
    pl.run_scoped(back, wide, wide)

    def gain_part(slot, sums):
        v = xs[slot].astype(F32)
        return jnp.sum(sums[...] * (v * inv_rms(v)), axis=0, keepdims=True)

    rext32[0:1] = gain_part(0, dxn)

    @pl.when(late)
    def _():
        rext32[0:1] += gain_part(1, dxn_early)

    rext32[1:2] = sm_own
    rext32[2:16] = drext[0:14]
    smr[dp] = rext32[...].astype(BF)

    def small(j):
        there = lax.rem(dp + j, p.nd)
        return remote(smr.at[dp], smr.at[dp], "s1", j - 1, (there, z))

    for j in range(1, p.nd):
        small(j).start()

    heads_to_chips(NG - 1)
    for g in range(NG):
        heads_along_z(g)
    for g in range(NG - 1):
        heads_home(g)

    for j in range(1, p.nd):
        small(j).wait_recv()
    total = smr[0].astype(F32)
    for j in range(1, p.nd):
        total += smr[j].astype(F32)
    smz[z] = total

    def small_z(k):
        return remote(smz.at[z], smz.at[z], "s2", k - 1, to_z(k))

    for k in (1, 2, 3):
        small_z(k).start()
    heads_home(NG - 1)

    @pl.when(zlo == 0)
    def _():
        px_copy.wait_recv()
        dxn[...] += xs[1].astype(F32)

    dn = dxn[...]
    x_back, _ = rms_back(x_in[...].astype(F32), dn, gain_attn)
    din_ref[...] = dx_own[...] + x_back
    o_next(0).wait_recv()
    o_far().wait_recv()
    whole = mid[...] + (out_own[...].astype(F32) + outr[0].astype(F32) + outr[2].astype(F32))
    out_ref[...] = whole.astype(BF)

    for k in (1, 2, 3):
        small_z(k).wait_recv()
    sm_ref[...] = smz[0] + smz[1] + smz[2] + smz[3]

    def hand_all(b, carry):
        hand_over(b)
        return carry

    lax.fori_loop(0, p.NB, hand_all, 0)

    def mate_done(b, carry):
        for j in range(p.nc):
            owner(chip_at(j))(lambda j=j: h4_copy(b, j).wait_recv())
        return carry

    lax.fori_loop(0, p.NB, mate_done, 0)
    for g in range(NG):
        for j in range(1, p.nd):
            sender = lax.rem(dp + p.nd - j, p.nd)
            c, side = lax.div(sender, 2), lax.rem(sender, 2)

            @sums_heads(c)
            def _(g=g, j=j, c=c, side=side):
                to, row = home(g, side, c)
                pl.when(to == z)(lambda: f4_copy(g, j, row).wait_recv())

    for m in range(4):
        att_ref[m * p.HC : (m + 1) * p.HC] = att[m]

    for k in (1, 2, 3):
        w_copy(k, z).wait_send()
        for j in (1, 2, 3):
            f_copy(k, j, quad).wait_send()
        for j in range(4):
            g_copy(k, j, core).wait_send()
        small_z(k).wait_send()
    for copy in dx_copies() + [o_next(0), o_next(1), o_far()]:
        copy.wait_send()
    own_sent("c", cotg, 0, slice(None))
    for b in range(R // QB):
        own_sent("n", normg, b, halves[b])
    pl.when(zlo == 0)(lambda: x_copy.wait_send())
    pl.when(late)(lambda: px_copy.wait_send())
    for g in range(NG):
        f1_copy(g).wait_send()
        for j in range(1, p.nc):
            sums_heads(chip_at(j))(lambda g=g, j=j: f2_copy(g, j).wait_send())

        @sums_heads(chip)
        def _(g=g):
            to, row = home(g, core, chip)
            pl.when(to != z)(lambda: f3_copy(g, z).wait_send())

            @pl.when(to == z)
            def _():
                for j in range(1, p.nd):
                    f4_copy(g, j, row).wait_send()

    def sums_sent(b, carry):
        h1_copy(b).wait_send()
        for j in range(1, p.nc):
            owner(chip_at(j))(lambda j=j: h2_copy(b, j).wait_send())
            owns(lambda j=j: h3_copy(b, j).wait_send())
        owns(lambda: keep(b).wait())
        for j in range(p.nc):
            owner(chip_at(j))(lambda j=j: h4_copy(b, j).wait_send())
        return carry

    lax.fori_loop(0, p.NB, sums_sent, 0)
    for j in range(1, p.nd):
        small(j).wait_send()


def tables():
    half = HD // 2
    freqs = 10000.0 ** (-np.arange(half, dtype=np.float32) / np.float32(half))
    angles = np.arange(LEN, dtype=np.float32)[:, None] * freqs.astype(np.float32)[None, :]
    cosine, sine = np.cos(angles).astype(np.float32), np.sin(angles).astype(np.float32)
    reps = LANES // HD
    cos_wide = np.tile(np.concatenate([cosine, cosine], axis=1), (1, reps))
    sin_wide = np.tile(np.concatenate([-sine, sine], axis=1), (1, reps))
    return cos_wide, sin_wide, np.ascontiguousarray(cosine.T), np.ascontiguousarray(sine.T)


def per_device(
    nd,
    inputs,
    lengths,
    expert_ids,
    gain_attn,
    w_query,
    w_key,
    w_value,
    w_out,
    gain_ffn,
    router,
    shared_gate_vec,
    exp_gate,
    exp_up,
    exp_down,
    sh_gate,
    sh_up,
    sh_down,
    cotangent,
):
    R, W = inputs.shape
    experts, _, eff = exp_gate.shape
    ff = sh_gate.shape[1]
    p = Plan(nd, R, W, experts, eff, ff)
    number, names = sem_plan(p)
    eg = exp_gate.swapaxes(1, 2).reshape(p.EB, p.B, W)
    eu = exp_up.swapaxes(1, 2).reshape(p.EB, p.B, W)
    ed = exp_down.reshape(p.EB, p.B, W)
    cosk, sink, cost, sint = tables()
    vm = pl.BlockSpec(memory_space=pltpu.VMEM)
    hbm = pl.BlockSpec(memory_space=pl.ANY)
    V = pltpu.VMEM
    hc = W // HD
    scratch = [
        pltpu.SemaphoreType.DMA((number,)),
        pltpu.SemaphoreType.DMA((number,)),
        pltpu.SemaphoreType.DMA((8,)),
        V((4, W, W), BF),
        V((16, W), F32),
        V((16, W), BF),
        V((W, LANES), BF),
        V((2, R, W), BF),
        V((2, R, W), BF),
        V((NT, R, W), BF),
        V((NT, R, W), BF),
        V((p.NB, 2 * p.B, W), BF),
        V((p.NB, W, 2 * p.B), BF),
        V((p.NB, p.B, W), BF),
        V((p.NB, W, p.B), BF),
        V((W, R), BF),
        V((p.NG, R, LANES), BF),
        V((2, p.NG, R, LANES), BF),
        V((2, W, R), BF),
        V((2, p.NG, R, LANES), BF),
        V((W, R), BF),
        V((up16(hc), R), F32),
        V((R, R), F32),
        V((W, R), F32),
        V((R, W), F32),
        V((R, W), F32),
        V((R, W), BF),
        V((3, R, W), BF),
        V((3, R, W), BF),
        V((3 * p.NB * W, W), F32),
        V((16, W), F32),
        V((p.NB, 3, p.hp, W), BF),
        V((p.NB, 3, p.hp, W), BF),
        V((max(p.nc - 1, 1), p.NB, 3, p.pr, W), BF),
        V((p.NB, 3, p.pr, W), BF),
        V((R, W), BF),
        V((p.NG, R, LANES), BF),
        V((W, R), BF),
        V((up16(hc), R), F32),
        V((p.NG, 4, LANES // 2, W), BF),
        V((p.NG, 4, LANES // 2, W), BF),
        V((p.nc - 1, p.NG, 4, 16, W), BF),
        V((p.NG, 4, 16, W), BF),
        V((p.NG, NT, 4, 16, W), BF),
        V((4, p.HC, W), BF),
        V((nd, 16, W), BF),
        V((NT, 16, W), F32),
    ]
    results = pl.pallas_call(
        functools.partial(kernel, p, names),
        out_shape=[
            jax.ShapeDtypeStruct((R, W), BF),
            jax.ShapeDtypeStruct((R, W), F32),
            jax.ShapeDtypeStruct((2 * p.hp, W), BF),
            jax.ShapeDtypeStruct((16, W), F32),
            jax.ShapeDtypeStruct((p.NB, 3, 2, p.hp, W), BF),
        ],
        in_specs=[pl.BlockSpec(memory_space=pltpu.SMEM)] + [vm] * 9 + [hbm] * 8 + [vm] * 4,
        out_specs=[vm] * 4 + [hbm],
        scratch_shapes=scratch,
        compiler_params=pltpu.CompilerParams(collective_id=0, has_side_effects=True, vmem_limit_bytes=63 << 20),
        name="block",
    )(
        lengths,
        expert_ids.T,
        gain_attn,
        gain_ffn,
        router.T,
        shared_gate_vec,
        w_query.T,
        w_key.T,
        w_value.T,
        w_out,
        inputs,
        cotangent,
        eg,
        eu,
        ed,
        sh_gate,
        sh_up,
        sh_down,
        jnp.asarray(cosk),
        jnp.asarray(sink),
        jnp.asarray(cost),
        jnp.asarray(sint),
    )
    return widen(p, *results)


def widen_kernel(p, out_b, din, att, small, routed, shared, *outs):
    (out_o, din_o, ga_o, wq_o, wk_o, wv_o, wo_o, gf_o, ro_o, ve_o, eg_o, eu_o, ed_o, sg_o, su_o, sd_o) = outs
    step = pl.program_id(0)
    for c in range(2):
        rows = slice(c * p.hp, (c + 1) * p.hp)
        for kind, dst in enumerate((eg_o, eu_o, ed_o)):
            dst[0, rows] = routed[0, kind, c].astype(F32)

    @pl.when(step == 0)
    def _():
        out_o[...] = out_b[...]
        din_o[...] = din[...]
        for m, dst in enumerate((wq_o, wk_o, wv_o, wo_o)):
            dst[...] = att[m * p.HC : (m + 1) * p.HC].astype(F32)
        ga_o[...] = small[0]
        gf_o[...] = small[1]
        ro_o[...] = small[2 : 2 + p.E]
        ve_o[...] = small[2 + p.E] + small[3 + p.E]
        for c in range(2):
            rows = slice(c * p.hp, (c + 1) * p.hp)
            for kind, dst in enumerate((sg_o, su_o, sd_o)):
                dst[rows] = shared[0, kind, c].astype(F32)


def widen(p, *results):
    R, W = p.R, p.W

    def whole(shape):
        return pl.BlockSpec(shape, lambda i: (0,) * len(shape))

    def split(shape):
        return pl.BlockSpec((1,) + shape[1:], lambda i: (i,) + (0,) * (len(shape) - 1))

    block = (1, 3, 2, p.hp, W)
    routed = (p.EB, p.B, W)
    row, head, sh = (W,), (p.HC, W), (W, W)
    shapes = [(R, W), (R, W), row, head, head, head, head, row, (p.E, W), row, routed, routed, routed, sh, sh, sh]
    out = pl.pallas_call(
        functools.partial(widen_kernel, p),
        grid=(p.EB,),
        out_shape=[jax.ShapeDtypeStruct(s, BF if i == 0 else F32) for i, s in enumerate(shapes)],
        in_specs=[whole((R, W))] * 2
        + [whole((2 * p.hp, W)), whole((16, W))]
        + [pl.BlockSpec(block, lambda i: (i, 0, 0, 0, 0)), pl.BlockSpec(block, lambda i: (p.EB, 0, 0, 0, 0))],
        out_specs=[split(s) if s == routed else whole(s) for s in shapes],
        compiler_params=pltpu.CompilerParams(vmem_limit_bytes=63 << 20),
        name="widen",
    )(*results, results[-1])
    out = list(out)
    for i in (3, 4, 5, 8):
        out[i] = out[i].T
    for i in (10, 11, 12):
        out[i] = out[i].reshape(p.E, p.eff, W)
    for i in (10, 11):
        out[i] = out[i].swapaxes(1, 2)
    return tuple(out)


def solution(mesh):
    rows = P(("dp", "tensor"), None)
    cols = P(None, "tensor")
    deep = P(None, None, "tensor")
    weights = (cols, cols, cols, P("tensor", None))
    experts = (deep, deep, P(None, "tensor", None), cols, cols, P("tensor", None))
    in_specs = (rows, P("dp"), P("dp", None), P()) + weights + (P(), P(), P()) + experts + (rows,)
    out_specs = (rows, rows, P()) + weights + (P(), P(), P()) + experts
    return jax.shard_map(
        functools.partial(per_device, mesh.shape["dp"]),
        mesh=mesh,
        in_specs=in_specs,
        out_specs=out_specs,
        check_vma=False,
    )
```
